32 devices in a mesh: dp: 16 (over z, y, x), tensor: 2 (over core).
Axes of the slice: x: 2, y: 2, z: 4, core: 2. Of those that a mesh axis runs over, the one named last changes fastest.
Arguments:
- hidden_in: bfloat16 [8192, 1536], P('dp'), may hold values from -6 to 6
- attn_gain: float32 [1536], replicated, may hold values from 0.5 to 1.5
- w_query: bfloat16 [1536, 1536], P(None, 'tensor'), may hold values from -0.4375 to 0.4375
- key_weight: bfloat16 [1536, 512], P(None, 'tensor'), may hold values from -0.4375 to 0.4375
- value_weight: bfloat16 [1536, 512], P(None, 'tensor'), may hold values from -0.15625 to 0.15625
- w_output: bfloat16 [1536, 1536], P('tensor'), may hold values from -4 to 4
- moe_gain: float32 [1536], replicated, may hold values from 0.5 to 1.5
- w_router: bfloat16 [1536, 16], replicated, may hold values from -0.0625 to 0.0625
- w_gate: bfloat16 [16, 1536, 512], P('dp'), may hold values from -0.15625 to 0.15625
- w_up: bfloat16 [16, 1536, 512], P('dp'), may hold values from -0.15625 to 0.15625
- w_down: bfloat16 [16, 512, 1536], P('dp'), may hold values from -4 to 4
- expert_ids: int32 [8192, 8], P('dp'), may hold values from 0 to 15, all different within a row; in each aligned block of 512 rows (0 to 511, 512 to 1023, ...) at most 320 rows name the same one
- segment_ids: int32 [16, 512], P('dp'), may hold values from 0 to 7, never falling along the last dimension, each value on 1 to 256 neighbouring positions
- out_grad: bfloat16 [8192, 1536], P('dp'), may hold values from -6 to 6
Outputs:
- block_out: bfloat16 [8192, 1536], P('dp')
- input_grad: float32 [8192, 1536], P('dp')
- attn_gain_grad: float32 [1536], replicated
- query_grad: float32 [1536, 1536], P(None, 'tensor')
- key_grad: float32 [1536, 512], P(None, 'tensor')
- value_grad: float32 [1536, 512], P(None, 'tensor')
- w_output_grad: float32 [1536, 1536], P('tensor')
- moe_gain_grad: float32 [1536], replicated
- router_grad: float32 [1536, 16], replicated
- gate_grad: float32 [16, 1536, 512], P('dp')
- up_grad: float32 [16, 1536, 512], P('dp')
- down_grad: float32 [16, 512, 1536], P('dp')
The draws below stay inside these ranges and needn't reach their ends.
Inputs may be any that keep to these rules, and one draw needn't show every extreme that they name: `expert_ids`: each row names 8 different experts. Among the rows of one index of dp no expert is named by more than 320 rows, and in every draw some expert is named by exactly 320 rows of some index. `segment_ids`: within each sequence the ids never fall; a document spans 1 to 256 positions, and some document exactly 256.
All inputs are finite; a program needn't handle non-finite values.
Results may differ from the reference program's by a relative error of at most 0.015.
Values may be sent and summed in bfloat16 or wider, within the bound.
A program may use at most 384 MiB of HBM per device.

```python
import math
import jax
import jax.numpy as jnp
import numpy as np
from jax import lax

MODEL_DIM = 1536
QUERY_HEADS = 24
KEY_VALUE_HEADS = 8
HEAD_DIM = 64
FFE = 512
TOP = 8
DOCS = 8
TOK_DEV = 512
SEQ = 512
SEQS = 16
TOKENS = 8192
EXPERTS = 16
CAP = 320


def shard_levels(rng, dims, pieces, least, high):
    def one(axis_at, shards_of):
        heights = jax.random.uniform(jax.random.fold_in(jax.random.fold_in(rng, 6), axis_at), (shards_of,), jnp.float32, least / len(pieces), high / len(pieces))
        return jnp.repeat(jnp.exp(heights), dims[axis_at] // shards_of).reshape((-1,) + (1,) * (len(dims) - axis_at - 1))

    level = one(*pieces[0])
    for cut in pieces[1:]:
        level = level * one(*cut)
    return level


def split_up(number_of, total, most, skew):
    loads = [(1 << 20) // math.isqrt(rank ** skew) + 1 for rank in range(2, number_of + 1)]
    rest, holding = total - most - (number_of - 1), [1] * (number_of - 1)
    while rest > 0:
        candidates = [i for i in range(number_of - 1) if holding[i] < most]
        mass, remaining = sum([loads[i] for i in candidates]), rest
        for i in candidates:
            extra = min(most - holding[i], max(1, remaining * loads[i] // mass), rest)
            holding[i] = holding[i] + extra
            rest = rest - extra
    return np.array([most] + holding)


def ragged_sizes(stream_key, number_of, total, reach, slope):
    if number_of == 2:
        one = jax.random.randint(stream_key, (), max(1, total - reach), min(reach, total - 1) + 1)
        return jnp.stack([one, total - one])
    tallies = jnp.asarray(split_up(number_of, total, reach, slope), jnp.int32)
    twos = (number_of - 1) // 2
    giver, taker = tallies[1:1 + 2 * twos:2], tallies[2:2 + 2 * twos:2]
    slack = jnp.minimum(giver - 1, reach - taker)
    passed = jax.random.randint(jax.random.fold_in(stream_key, 1), (twos,), 0, 1 << 20) % (slack + 1)
    tallies = tallies.at[1:1 + 2 * twos:2].set(giver - passed).at[2:2 + 2 * twos:2].set(taker + passed)
    return tallies[jax.random.permutation(jax.random.fold_in(stream_key, 2), number_of)]


def shared_out(stream_key, own, number, rows, amount, top, bound, skew):
    ranking = jax.random.permutation(stream_key, amount)
    packed, ordinary = portions_of(amount, rows * top, bound, skew, True), portions_of(amount, rows * top, bound, skew, False)
    places = jnp.arange(amount)

    def named(tallies, offset_by):
        used = int((tallies > 0).sum())
        fixed = max(1, used // 4)
        moved = fixed + (places - fixed + offset_by * (used - fixed)) % max(1, amount - fixed)
        return jnp.zeros((amount,), jnp.int32).at[ranking[jnp.where(places < fixed, places, moved)]].set(jnp.asarray(tallies, jnp.int32))

    tallies = jnp.where(number % 4 == 0, named(packed, number // 4), named(ordinary, number - number // 4 - 1))
    mixed = jax.random.permutation(jax.random.fold_in(own, 3), amount)
    source_of, receiver = mixed[0:amount // 2 * 2:2], mixed[1:amount // 2 * 2:2]
    slack = jnp.minimum(tallies[source_of] - 1, bound - tallies[receiver]) // 2
    slack = jnp.where((source_of == ranking[0]) | (receiver == ranking[0]) | (tallies[receiver] == 0), 0, jnp.maximum(slack, 0))
    moved = jax.random.randint(jax.random.fold_in(own, 4), (amount // 2,), 0, 1 << 20) % (slack + 1)
    tallies = tallies.at[source_of].add(-moved).at[receiver].add(moved)
    items = jnp.searchsorted(jnp.cumsum(tallies), jnp.arange(rows * top), side="right").astype(jnp.int32)
    grid = items.reshape(top, rows).T
    grid = grid[jax.random.permutation(jax.random.fold_in(own, 1), rows)]
    offset_by = jax.random.randint(jax.random.fold_in(own, 2), (rows, 1), 0, top)
    return jnp.take_along_axis(grid, (jnp.arange(top)[None, :] + offset_by) % top, axis=1)


def portions_of(count, total, most, slope, full):
    loads = [(1 << 20) // math.isqrt(rank ** slope) + 1 for rank in range(1, count + 1)]
    largest = most if full else min(most, max(-(-total // count), total * loads[0] // sum(loads)))
    least = 1 if total - largest >= count - 1 else 0
    holding, rest = [largest] + [least] * (count - 1), total - largest - least * (count - 1)
    while rest > 0:
        movable = [i for i in range(1, count) if holding[i] < largest] or [i for i in range(1, count) if holding[i] < most]
        pool, remaining = sum([loads[i] for i in movable]), rest
        for i in movable:
            more = min(most - holding[i], max(1, remaining * loads[i] // pool), rest)
            holding[i] = holding[i] + more
            rest = rest - more
    return np.array(holding)


def centred(key, shape, scale, reach, pieces=(), kind=jnp.bfloat16):
    values = jax.random.normal(key, shape, jnp.float32) * scale
    if len(pieces) > 0:
        values = shard_levels(key, shape, pieces, -0.22, 0.18) * values
    return jnp.clip(values, min=-reach, max=reach).astype(kind)


def setup_inputs(seed: int = 0) -> dict:
    streams_of = jax.random.split(jax.random.key(seed), 15)
    hidden_in = centred(streams_of[0], (TOKENS, MODEL_DIM), 1.0, 6.0, ((0, 16),))
    attn_gain = jnp.clip(1.0 + 0.1 * jax.random.normal(streams_of[1], (MODEL_DIM,), jnp.float32), 0.5, 1.5)
    w_query = centred(streams_of[2], (MODEL_DIM, QUERY_HEADS * HEAD_DIM), (MODEL_DIM // 8) ** -0.5, 0.4375, ((1, 2),))
    key_weight = centred(streams_of[3], (MODEL_DIM, KEY_VALUE_HEADS * HEAD_DIM), (MODEL_DIM // 8) ** -0.5, 0.4375, ((1, 2),))
    value_weight = centred(streams_of[4], (MODEL_DIM, KEY_VALUE_HEADS * HEAD_DIM), MODEL_DIM ** -0.5, 0.15625, ((1, 2),))
    w_output = centred(streams_of[5], (QUERY_HEADS * HEAD_DIM, MODEL_DIM), 2 ** -0.5, 4.0, ((0, 2),))
    moe_gain = jnp.clip(1.0 + 0.1 * jax.random.normal(streams_of[6], (MODEL_DIM,), jnp.float32), 0.5, 1.5)
    w_router = centred(streams_of[7], (MODEL_DIM, EXPERTS), (6 * MODEL_DIM) ** -0.5, 0.0625)
    w_gate = centred(streams_of[8], (EXPERTS, MODEL_DIM, FFE), MODEL_DIM ** -0.5, 0.15625, ((0, 16),))
    w_up = centred(streams_of[9], (EXPERTS, MODEL_DIM, FFE), MODEL_DIM ** -0.5, 0.15625, ((0, 16),))
    w_down = centred(streams_of[10], (EXPERTS, FFE, MODEL_DIM), (max(1, FFE // 256)) ** -0.5, 4.0, ((0, 16),))
    expert_ids_keys = jax.random.split(jax.random.fold_in(streams_of[11], 1), TOKENS // TOK_DEV)
    expert_ids_turns = jax.random.permutation(jax.random.fold_in(streams_of[11], 3), TOKENS // TOK_DEV)
    expert_ids = jax.vmap(lambda own, number: shared_out(jax.random.fold_in(streams_of[11], 2), own, number, TOK_DEV, EXPERTS, TOP, CAP, 1))(expert_ids_keys, expert_ids_turns).reshape((TOKENS, TOP))
    segment_ids = jax.vmap(lambda own: jnp.searchsorted(jnp.cumsum(ragged_sizes(own, DOCS, SEQ, SEQ // 2, 2)), jnp.arange(SEQ), side="right"))(jax.random.split(streams_of[12], SEQS)).reshape((SEQS, SEQ)).astype(jnp.int32)
    out_grad = centred(streams_of[13], (TOKENS, MODEL_DIM), 1.0, 6.0, ((0, 16),))
    return {"hidden_in": hidden_in, "attn_gain": attn_gain, "w_query": w_query, "key_weight": key_weight, "value_weight": value_weight, "w_output": w_output, "moe_gain": moe_gain, "w_router": w_router, "w_gate": w_gate, "w_up": w_up, "w_down": w_down, "expert_ids": expert_ids, "segment_ids": segment_ids, "out_grad": out_grad}


@jax.custom_vjp
def reduced_precision(v):
    return lax.optimization_barrier(v.astype(jnp.bfloat16)).astype(jnp.float32)

@jax.custom_vjp
def reduced_backward(v):
    return v

def low_keep(v):
    return (reduced_precision(v), None)

def low_pass(kept, grad):
    return (grad,)

def back_keep(v):
    return (v, None)

def back_low(kept, grad):
    return (reduced_precision(grad),)
reduced_precision.defvjp(low_keep, low_pass)
reduced_backward.defvjp(back_keep, back_low)
epsilon = 1e-06
residual_scale = 0.22
attn_scale = 0.015625
rope_base = 10000.0
masked_score = -1e+30
highest_precision = lax.Precision.HIGHEST

def rms_norm(values, gain):
    return values * lax.rsqrt(lax.optimization_barrier(jnp.mean(values * values, axis=-1, keepdims=True)) + epsilon) * gain

def positions_of(segment):
    position_index = jnp.arange(segment.shape[0], dtype=jnp.int32)
    earlier = jnp.concatenate([segment[:1] - 1, segment[:-1]])
    starts = lax.cummax(jnp.where(segment != earlier, position_index, 0), axis=0)
    return position_index - starts

def rope_tables(segment):
    position = positions_of(segment).astype(jnp.float32)
    frequency = rope_base ** (-jnp.arange(HEAD_DIM // 2, dtype=jnp.float32) * 2.0 / HEAD_DIM)
    angle = position[:, None] * frequency[None, :]
    return (jnp.cos(angle)[:, None, :], jnp.sin(angle)[:, None, :])

def apply_rotation(heads_in, cosine_table, sine_values):
    middle_index = heads_in.shape[-1] // 2
    first_half = heads_in[..., :middle_index]
    second_half = heads_in[..., middle_index:]
    return jnp.concatenate([first_half * cosine_table - second_half * sine_values, second_half * cosine_table + first_half * sine_values], axis=-1)

def attend(normalized_input, segment, w_query, key_weight, value_weight):
    sequence_length = normalized_input.shape[0]
    cosine_table, sine_values = rope_tables(segment)
    query_rows = reduced_backward(jnp.dot(normalized_input, w_query, precision=highest_precision)).reshape(sequence_length, QUERY_HEADS, HEAD_DIM)
    key_rows = reduced_backward(jnp.dot(normalized_input, key_weight, precision=highest_precision)).reshape(sequence_length, KEY_VALUE_HEADS, HEAD_DIM)
    query_heads = reduced_precision(apply_rotation(query_rows, cosine_table, sine_values)).reshape(sequence_length, KEY_VALUE_HEADS, QUERY_HEADS // KEY_VALUE_HEADS, HEAD_DIM)
    key_heads = reduced_precision(apply_rotation(key_rows, cosine_table, sine_values))
    value_head_rows = reduced_precision(reduced_backward(jnp.dot(normalized_input, value_weight, precision=highest_precision))).reshape(sequence_length, KEY_VALUE_HEADS, HEAD_DIM)
    raw_scores = jnp.einsum('qhgd,khd->hgqk', query_heads, key_heads, precision=highest_precision) * attn_scale
    position_index = jnp.arange(sequence_length, dtype=jnp.int32)
    allowed = (position_index[:, None] >= position_index[None, :]) & (segment[:, None] == segment[None, :])
    scores = reduced_backward(jnp.where(allowed, raw_scores, masked_score))
    probability = reduced_precision(jax.nn.softmax(scores, axis=-1))
    head_out = jnp.einsum('hgqk,khd->qhgd', probability, value_head_rows, precision=highest_precision).reshape(sequence_length, QUERY_HEADS * HEAD_DIM)
    return reduced_precision(reduced_backward(head_out))

def forward(hidden_in, attn_gain, w_query, key_weight, value_weight, w_output, moe_gain, w_router, w_gate, w_up, w_down, expert_ids, segment_ids):
    normalized_input = reduced_precision(rms_norm(hidden_in, attn_gain))

    def one_sequence(running, seq_item):
        return (running, attend(seq_item[0], seq_item[1], w_query, key_weight, value_weight))
    scanned = lax.scan(jax.checkpoint(one_sequence), jnp.zeros((), jnp.float32), (normalized_input.reshape(SEQS, SEQ, MODEL_DIM), segment_ids))
    head_out = scanned[1].reshape(TOKENS, QUERY_HEADS * HEAD_DIM)
    branch = reduced_backward(jnp.dot(head_out, w_output, precision=highest_precision))
    middle = hidden_in + residual_scale * branch
    routed = reduced_precision(rms_norm(middle, moe_gain))
    logits = reduced_backward(jnp.dot(routed, w_router, precision=highest_precision))
    expert_range = jnp.arange(EXPERTS, dtype=jnp.int32)
    pick_mask = expert_ids[:, :, None] == expert_range[None, None, :]
    chosen = lax.optimization_barrier(jnp.sum(jnp.where(pick_mask, logits[:, None, :], 0.0), axis=-1))
    gate_weights = jax.nn.softmax(chosen, axis=-1)
    columns = lax.optimization_barrier(jnp.sum(jnp.where(pick_mask, gate_weights[:, :, None], 0.0), axis=1))

    def one_expert(totals, expert_item):
        gate_matrix, up_matrix, down_matrix, column = expert_item
        gate_act = reduced_backward(jnp.dot(routed, gate_matrix, precision=highest_precision))
        up_act = reduced_backward(jnp.dot(routed, up_matrix, precision=highest_precision))
        hidden = reduced_precision(jax.nn.silu(gate_act) * up_act)
        expert_out = reduced_backward(jnp.dot(hidden, down_matrix, precision=highest_precision))
        return (totals + column[:, None] * expert_out, None)
    mixed = lax.scan(jax.checkpoint(one_expert), jnp.zeros((TOKENS, MODEL_DIM), jnp.float32), (w_gate, w_up, w_down, columns.T))
    return middle + residual_scale * mixed[0]

def reference(hidden_in, attn_gain, w_query, key_weight, value_weight, w_output, moe_gain, w_router, w_gate, w_up, w_down, expert_ids, segment_ids, out_grad):
    floats = tuple((array.astype(jnp.float32) for array in (hidden_in, attn_gain, w_query, key_weight, value_weight, w_output, moe_gain, w_router, w_gate, w_up, w_down)))

    def closed(*arrays):
        return forward(*arrays, expert_ids, segment_ids)
    block_out, pullback = jax.vjp(closed, *floats)
    gradients = pullback(out_grad.astype(jnp.float32))
    return (block_out.astype(jnp.bfloat16), gradients[0], gradients[1], gradients[2], gradients[3], gradients[4], gradients[5], gradients[6], gradients[7], gradients[8], gradients[9], gradients[10])
```

```python
import jax
import jax.numpy as jnp
from jax import lax
from jax.sharding import PartitionSpec as P

HEAD_DIM = 64

bf16 = jnp.bfloat16
f32 = jnp.float32
epsilon = 1e-06
residual_scale = 0.22
attn_scale = 0.015625
rope_base = 10000.0
masked_score = -1e30


def positions_of(segment):
    position_index = jnp.arange(segment.shape[0], dtype=jnp.int32)
    earlier = jnp.concatenate([segment[:1] - 1, segment[:-1]])
    starts = lax.cummax(jnp.where(segment != earlier, position_index, 0), axis=0)
    return position_index - starts


def rope_tables(segment, head_size):
    position = positions_of(segment).astype(f32)
    frequency = rope_base ** (-jnp.arange(head_size // 2, dtype=f32) * 2.0 / head_size)
    angle = position[:, None] * frequency[None, :]
    return (jnp.cos(angle)[:, None, :], jnp.sin(angle)[:, None, :])


def apply_rotation(heads_in, cosine_table, sine_values):
    middle_index = heads_in.shape[-1] // 2
    first_half = heads_in[..., :middle_index]
    second_half = heads_in[..., middle_index:]
    return jnp.concatenate(
        [
            first_half * cosine_table - second_half * sine_values,
            second_half * cosine_table + first_half * sine_values,
        ],
        axis=-1,
    )


def block_scores(query_heads, key_heads, segment):
    kv_count = key_heads.shape[1]
    length = query_heads.shape[0]
    grouped = query_heads.reshape(length, kv_count, -1, query_heads.shape[2])
    raw_scores = (
        jnp.einsum("qhgd,khd->hgqk", grouped, key_heads, preferred_element_type=f32) * attn_scale
    )
    index = jnp.arange(length, dtype=jnp.int32)
    allowed = (index[:, None] >= index[None, :]) & (segment[:, None] == segment[None, :])
    return (jnp.where(allowed, raw_scores, masked_score), grouped)


def attend_forward(normed, segment, tables, w_query, key_weight, value_weight, head_size):
    length = normed.shape[0]

    def heads(weight):
        return jnp.dot(normed, weight, preferred_element_type=f32).reshape(length, -1, head_size)

    query_heads = apply_rotation(heads(w_query), *tables).astype(bf16)
    key_heads = apply_rotation(heads(key_weight), *tables).astype(bf16)
    value_heads = heads(value_weight).astype(bf16)
    scores, _ = block_scores(query_heads, key_heads, segment)
    largest = jnp.max(scores, axis=-1, keepdims=True)
    weights_raw = jnp.exp(scores - largest)
    totals = jnp.sum(weights_raw, axis=-1, keepdims=True)
    probs_low = (weights_raw / totals).astype(bf16)
    head_out = jnp.einsum("hgqk,khd->qhgd", probs_low, value_heads, preferred_element_type=f32)
    return (
        head_out.reshape(length, -1).astype(bf16),
        query_heads,
        key_heads,
        value_heads,
        (largest + jnp.log(totals))[..., 0],
    )


def attend_backward(query_heads, key_heads, value_heads, log_sums, heads_grad, segment, tables):
    length = query_heads.shape[0]
    cosine_table, sine_values = tables
    scores, grouped = block_scores(query_heads, key_heads, segment)
    probability = jnp.exp(scores - log_sums[..., None])
    probs_low = probability.astype(bf16)
    grad_grouped = heads_grad.reshape(grouped.shape)
    prob_grad = jnp.einsum(
        "qhgd,khd->hgqk", grad_grouped, value_heads, preferred_element_type=f32
    )
    weighted = jnp.sum(probability * prob_grad, axis=-1, keepdims=True)
    score_low = (probability * (prob_grad - weighted)).astype(bf16)
    query_part = (
        jnp.einsum("hgqk,khd->qhgd", score_low, key_heads, preferred_element_type=f32) * attn_scale
    ).reshape(query_heads.shape)
    key_sum = (
        jnp.einsum("hgqk,qhgd->khd", score_low, grouped, preferred_element_type=f32) * attn_scale
    )
    value_sum = jnp.einsum(
        "hgqk,qhgd->khd", probs_low, grad_grouped, preferred_element_type=f32
    )
    query_low = apply_rotation(query_part, cosine_table, -sine_values).astype(bf16)
    key_low = apply_rotation(key_sum, cosine_table, -sine_values).astype(bf16)
    return (
        query_low.reshape(length, -1),
        key_low.reshape(length, -1),
        value_sum.astype(bf16).reshape(length, -1),
    )


def bit_masks(size):
    masks = []
    while size > 1:
        size //= 2
        masks.append(size)
    return masks[::-1]


def swap(x, axis, mask):
    return lax.ppermute(x, axis, [(i, i ^ mask) for i in range(lax.axis_size(axis))])


def bit_of(axis, mask):
    return (lax.axis_index(axis) // mask) % 2


def halves_by_bit(x, axis, mask, dim=0):
    half = x.shape[dim] // 2
    bit = bit_of(axis, mask)
    mine = lax.dynamic_slice_in_dim(x, bit * half, half, dim)
    other = lax.dynamic_slice_in_dim(x, (1 - bit) * half, half, dim)
    return mine, other


def join_by_bit(mine, other, axis, mask, dim=0):
    return jnp.where(
        bit_of(axis, mask) == 0,
        jnp.concatenate([mine, other], dim),
        jnp.concatenate([other, mine], dim),
    )


def scatter_sum(x, axis, masks, kind, dim=0):
    x = x.astype(f32)
    for mask in masks:
        mine, other = halves_by_bit(x, axis, mask, dim)
        x = mine + swap(other.astype(kind), axis, mask).astype(f32)
    return x


def gather_blocks(x, axis, masks, dim=0):
    for mask in reversed(masks):
        x = join_by_bit(x, swap(x, axis, mask), axis, mask, dim)
    return x


def sum_all(x, axis):
    for mask in bit_masks(lax.axis_size(axis)):
        x = x + swap(x, axis, mask)
    return x


def rotated(masks, j):
    j = j % len(masks)
    return masks[j:] + masks[:j]


def row_parts(rows, count):
    units = rows // 16
    sizes = [16 * (units // count + (1 if i < units % count else 0)) for i in range(count)]
    starts = [sum(sizes[:i]) for i in range(count)]
    return list(zip(starts, sizes))


def cube_orders(masks, count):
    orders = []
    for j in range(count):
        order = [0]
        for mask in rotated(masks, j):
            order = order + [o ^ mask for o in order]
        orders.append(order)
    return orders


def cube_gather(x, masks):
    bufs = [x[s : s + n] for s, n in row_parts(x.shape[0], len(masks))]
    for phase in range(len(masks)):
        got = [swap(b, "dp", rotated(masks, j)[phase]) for j, b in enumerate(bufs)]
        bufs = [jnp.concatenate([b, g], 0) for b, g in zip(bufs, got)]
    return jnp.concatenate(bufs, 0)


def cube_scatter_sum(x, masks):
    devices = 2 ** len(masks)
    parts = row_parts(x.shape[0] // devices, len(masks))
    bufs = [x[devices * s : devices * (s + n)] for s, n in parts]
    for phase in reversed(range(len(masks))):
        got = [
            swap(b[b.shape[0] // 2 :].astype(bf16), "dp", rotated(masks, j)[phase])
            for j, b in enumerate(bufs)
        ]
        bufs = [b[: b.shape[0] // 2].astype(f32) + g.astype(f32) for b, g in zip(bufs, got)]
    return jnp.concatenate(bufs, 0)


def vector_gather(x, masks):
    x = x[None]
    for mask in masks:
        x = jnp.concatenate([x, swap(x, "dp", mask)], 0)
    return x


def vector_scatter(x, masks):
    for mask in reversed(masks):
        half = x.shape[0] // 2
        x = x[:half] + swap(x[half:], "dp", mask)
    return x[0]


def to_cube_rows(x, masks):
    parts = row_parts(x.shape[1], len(masks))
    orders = cube_orders(masks, len(masks))
    return jnp.concatenate(
        [x[o, s : s + n] for (s, n), order in zip(parts, orders) for o in order]
    )


def from_cube_rows(x, masks):
    devices = 2 ** len(masks)
    parts = row_parts(x.shape[0] // devices, len(masks))
    orders = cube_orders(masks, len(masks))
    found = {}
    for j, ((s, n), order) in enumerate(zip(parts, orders)):
        for place, o in enumerate(order):
            first = devices * s + place * n
            found[o, j] = x[first : first + n]
    return jnp.stack(
        [jnp.concatenate([found[o, j] for j in range(len(masks))]) for o in range(devices)]
    )


def dot(a, b, spec):
    return jnp.einsum(spec, a, b, preferred_element_type=f32)


def expert_passes(rows, grads, column, w_gate, w_up, w_down):
    gate_act = dot(rows, w_gate, "td,df->tf")
    up_act = dot(rows, w_up, "td,df->tf")
    sigmoid_gate = jax.nn.sigmoid(gate_act)
    silu_gate = gate_act * sigmoid_gate
    hidden = silu_gate * up_act
    weighted_low = (hidden * column[:, None]).astype(bf16)
    down_in = residual_scale * dot(grads, w_down, "td,fd->tf")
    gate_deriv = jnp.sum(hidden * down_in, axis=1)
    down_in = down_in * column[:, None]
    gate_low = (down_in * up_act * sigmoid_gate * (1.0 + gate_act * (1.0 - sigmoid_gate))).astype(
        bf16
    )
    up_low = (down_in * silu_gate).astype(bf16)
    return weighted_low, gate_deriv, gate_low, up_low


def summed_over_dp(x, kind):
    masks = bit_masks(lax.axis_size("dp"))
    inner, last = masks[:-1], masks[-1:]
    count = 3
    size = x.shape[0] // count
    outs = []
    for j in range(count):
        order = rotated(inner, j) + last
        part = scatter_sum(x[j * size : (j + 1) * size], "dp", order, kind)
        outs.append(gather_blocks(part.astype(kind), "dp", order))
    return jnp.concatenate(outs, 0).astype(f32)


def per_device(
    hidden_in,
    attn_gain,
    w_query,
    key_weight,
    value_weight,
    w_output,
    moe_gain,
    w_router,
    w_gate,
    w_up,
    w_down,
    expert_ids,
    segment_ids,
    out_grad,
):
    tokens_here, model_width = hidden_in.shape
    head_size = HEAD_DIM
    dp_size = lax.axis_size("dp")
    tensor_size = lax.axis_size("tensor")
    experts = w_gate.shape[0] * dp_size
    dp_index = lax.axis_index("dp")
    tensor_index = lax.axis_index("tensor")
    masks = bit_masks(dp_size)
    cube, pair = masks[:-1], masks[-1]
    tensor_masks = bit_masks(tensor_size)
    tensor_down = tensor_masks[::-1]
    rows_here = tokens_here // tensor_size

    def my_rows(x):
        return lax.dynamic_slice_in_dim(x, tensor_index * rows_here, rows_here, 0)

    block = w_gate.shape[2] // tensor_size

    def my_units(x, dim):
        return lax.dynamic_slice_in_dim(x, tensor_index * block, block, dim)

    def relative_gather(x, dim):
        for mask in tensor_masks:
            x = jnp.concatenate([x, swap(x, "tensor", mask)], dim)
        return x

    def relative_scatter(x, dim):
        x = x.astype(f32)
        for mask in reversed(tensor_masks):
            half = x.shape[dim] // 2
            keep = lax.slice_in_dim(x, 0, half, axis=dim)
            give = lax.slice_in_dim(x, half, 2 * half, axis=dim)
            x = keep + swap(give.astype(bf16), "tensor", mask).astype(f32)
        return x

    far_gate = relative_gather(swap(my_units(w_gate[0], 1), "dp", pair), 1)
    far_up = relative_gather(swap(my_units(w_up[0], 1), "dp", pair), 1)
    far_down = relative_gather(swap(my_units(w_down[0], 0), "dp", pair), 0)

    grad_mine = my_rows(out_grad)
    grads = cube_gather(grad_mine, cube)

    inputs = hidden_in.astype(f32)
    scale_in = lax.rsqrt(jnp.mean(inputs * inputs, axis=-1, keepdims=True) + epsilon)
    normed_low = (inputs * scale_in * attn_gain).astype(bf16)
    segment = segment_ids[0]
    tables = rope_tables(segment, head_size)
    heads_flat, query_heads, key_heads, value_heads, log_sums = attend_forward(
        normed_low, segment, tables, w_query, key_weight, value_weight, head_size
    )
    attn_part = jnp.dot(heads_flat, w_output, preferred_element_type=f32)
    attn_total = scatter_sum(attn_part, "tensor", tensor_down, f32)

    inputs_mine = my_rows(hidden_in).astype(f32)
    scale_in_mine = my_rows(scale_in)
    middle = inputs_mine + residual_scale * attn_total
    scale_mid = lax.rsqrt(jnp.mean(middle * middle, axis=-1, keepdims=True) + epsilon)
    routed_low = (middle * scale_mid * moe_gain).astype(bf16)
    rows = cube_gather(routed_low, cube)

    logits = dot(w_router, routed_low, "de,td->et")
    ids_mine = my_rows(expert_ids).T
    expert_range = jnp.arange(experts, dtype=jnp.int32)
    picked = jnp.any(ids_mine[None, :, :] == expert_range[:, None, None], axis=1)
    largest = jnp.max(jnp.where(picked, logits, -jnp.inf), axis=0, keepdims=True)
    raised = jnp.where(picked, jnp.exp(jnp.where(picked, logits - largest, 0.0)), 0.0)
    gate_weights = raised / jnp.sum(raised, axis=0, keepdims=True)
    all_weights = vector_gather(gate_weights, cube)
    near, far = dp_index, dp_index ^ pair

    def column_of(expert):
        picked_row = lax.dynamic_index_in_dim(all_weights, expert, 1, keepdims=False)
        return to_cube_rows(picked_row, cube)

    near_set = (w_gate[0], w_up[0], w_down[0])
    far_set = (far_gate, far_up, far_down)
    near_low, near_deriv, near_gate_low, near_up_low = expert_passes(
        rows, grads, column_of(near), *near_set
    )
    far_low, far_deriv, far_gate_low, far_up_low = expert_passes(
        rows, grads, column_of(far), *far_set
    )
    moe_part = dot(near_low, w_down[0], "tf,fd->td") + dot(far_low, far_down, "tf,fd->td")
    moe_total = cube_scatter_sum(moe_part.astype(bf16), cube)

    one_near = (expert_range == near).astype(f32)[None, :, None]
    one_far = (expert_range == far).astype(f32)[None, :, None]
    deriv_part = (
        one_near * from_cube_rows(near_deriv, cube)[:, None, :]
        + one_far * from_cube_rows(far_deriv, cube)[:, None, :]
    )
    gate_deriv = vector_scatter(deriv_part, cube)

    routed_part = (
        dot(near_gate_low, w_gate[0], "tf,df->td")
        + dot(near_up_low, w_up[0], "tf,df->td")
        + dot(far_gate_low, far_gate, "tf,df->td")
        + dot(far_up_low, far_up, "tf,df->td")
    )
    routed_grad = cube_scatter_sum(routed_part.astype(bf16), cube)

    far_gate_grad = relative_scatter(dot(rows, far_gate_low, "td,tf->df"), 1)
    far_up_grad = relative_scatter(dot(rows, far_up_low, "td,tf->df"), 1)
    far_down_grad = relative_scatter(residual_scale * dot(far_low, grads, "tf,td->fd"), 0)
    near_gate_grad = scatter_sum(
        dot(rows, near_gate_low, "td,tf->df"), "tensor", tensor_down, bf16, 1
    )
    near_up_grad = scatter_sum(dot(rows, near_up_low, "td,tf->df"), "tensor", tensor_down, bf16, 1)
    near_down_grad = scatter_sum(
        residual_scale * dot(near_low, grads, "tf,td->fd"), "tensor", tensor_down, bf16, 0
    )

    def returned(mine, away, dim):
        whole = mine + swap(away.astype(bf16), "dp", pair).astype(f32)
        return gather_blocks(whole, "tensor", tensor_down, dim)[None]

    gate_grad = returned(near_gate_grad, far_gate_grad, 1)
    up_grad = returned(near_up_grad, far_up_grad, 1)
    down_grad = returned(near_down_grad, far_down_grad, 0)

    block_mine = (middle + residual_scale * moe_total).astype(bf16)
    block_out = gather_blocks(block_mine, "tensor", tensor_down)

    chosen_grad = gate_weights * (
        gate_deriv - jnp.sum(gate_weights * gate_deriv, axis=0, keepdims=True)
    )
    logit_grad = chosen_grad.astype(bf16)
    router_part = dot(logit_grad, routed_low, "et,td->ed")
    routed_grad = routed_grad + dot(logit_grad, w_router, "et,de->td")
    gained = moe_gain * routed_grad
    moe_gain_part = jnp.sum(routed_grad * middle * scale_mid, axis=0)
    grad_top = grad_mine.astype(f32)
    middle_grad = (
        grad_top
        + scale_mid * gained
        - middle
        * (scale_mid * scale_mid * scale_mid)
        * jnp.mean(middle * gained, axis=-1, keepdims=True)
    )
    branch_low = gather_blocks(
        (residual_scale * middle_grad).astype(bf16), "tensor", tensor_down
    )
    w_output_grad = summed_over_dp(dot(heads_flat, branch_low, "tc,td->cd"), bf16)
    heads_grad = dot(branch_low, w_output, "td,cd->tc").astype(bf16)
    query_low, key_low, value_low = attend_backward(
        query_heads, key_heads, value_heads, log_sums, heads_grad, segment, tables
    )
    width_q, width_k = query_low.shape[1], key_low.shape[1]
    qkv_low = jnp.concatenate([query_low, key_low, value_low], axis=1)
    qkv_grad = summed_over_dp(dot(normed_low, qkv_low, "td,tc->dc"), bf16)
    qkv_weight = jnp.concatenate([w_query, key_weight, value_weight], axis=1)
    normed_part = dot(qkv_low, qkv_weight, "tc,dc->td")
    normed_grad = scatter_sum(normed_part, "tensor", tensor_down, f32)
    gained_in = attn_gain * normed_grad
    attn_gain_part = jnp.sum(normed_grad * inputs_mine * scale_in_mine, axis=0)
    input_mine = (
        middle_grad
        + scale_in_mine * gained_in
        - inputs_mine
        * (scale_in_mine * scale_in_mine * scale_in_mine)
        * jnp.mean(inputs_mine * gained_in, axis=-1, keepdims=True)
    )
    input_grad = gather_blocks(input_mine, "tensor", tensor_down)

    early = sum_all(
        sum_all(jnp.concatenate([router_part, moe_gain_part[None]], 0), "tensor"), "dp"
    )
    attn_gain_grad = sum_all(sum_all(attn_gain_part[None], "tensor"), "dp")[0]
    return (
        block_out,
        input_grad,
        attn_gain_grad,
        qkv_grad[:, :width_q],
        qkv_grad[:, width_q : width_q + width_k],
        qkv_grad[:, width_q + width_k :],
        w_output_grad,
        early[experts],
        early[:experts].T,
        gate_grad,
        up_grad,
        down_grad,
    )


def solution(mesh):
    placed = (
        P("dp", None),
        P(),
        P(None, "tensor"),
        P(None, "tensor"),
        P(None, "tensor"),
        P("tensor", None),
        P(),
        P(),
        P("dp", None, None),
        P("dp", None, None),
        P("dp", None, None),
        P("dp", None),
        P("dp", None),
        P("dp", None),
    )
    return jax.shard_map(
        per_device,
        mesh=mesh,
        in_specs=placed,
        out_specs=(
            P("dp", None),
            P("dp", None),
            P(),
            P(None, "tensor"),
            P(None, "tensor"),
            P(None, "tensor"),
            P("tensor", None),
            P(),
            P(),
            P("dp", None, None),
            P("dp", None, None),
            P("dp", None, None),
        ),
        check_vma=False,
    )
```

```python
import functools

import jax
import jax.numpy as jnp
from jax import lax
from jax.experimental import pallas as pl
from jax.experimental.pallas import tpu as pltpu
from jax.sharding import PartitionSpec as P

HEAD_DIM = 64

bf16 = jnp.bfloat16
f32 = jnp.float32
epsilon = 1e-06
residual_scale = 0.22
attn_scale = 0.015625
rope_base = 10000.0
masked_score = -1e30


def positions_of(segment):
    position_index = jnp.arange(segment.shape[0], dtype=jnp.int32)
    earlier = jnp.concatenate([segment[:1] - 1, segment[:-1]])
    starts = lax.cummax(jnp.where(segment != earlier, position_index, 0), axis=0)
    return position_index - starts


def rope_tables(segment, head_size):
    position = positions_of(segment).astype(f32)
    frequency = rope_base ** (-jnp.arange(head_size // 2, dtype=f32) * 2.0 / head_size)
    angle = position[:, None] * frequency[None, :]
    return (jnp.cos(angle)[:, None, :], jnp.sin(angle)[:, None, :])


def apply_rotation(heads_in, cosine_table, sine_values):
    middle_index = heads_in.shape[-1] // 2
    first_half = heads_in[..., :middle_index]
    second_half = heads_in[..., middle_index:]
    return jnp.concatenate(
        [
            first_half * cosine_table - second_half * sine_values,
            second_half * cosine_table + first_half * sine_values,
        ],
        axis=-1,
    )


def block_scores(query_heads, key_heads, segment):
    kv_count = key_heads.shape[1]
    length = query_heads.shape[0]
    grouped = query_heads.reshape(length, kv_count, -1, query_heads.shape[2])
    raw_scores = (
        jnp.einsum("qhgd,khd->hgqk", grouped, key_heads, preferred_element_type=f32) * attn_scale
    )
    index = jnp.arange(length, dtype=jnp.int32)
    allowed = (index[:, None] >= index[None, :]) & (segment[:, None] == segment[None, :])
    return (jnp.where(allowed, raw_scores, masked_score), grouped)


def attend_forward(normed, segment, tables, w_query, key_weight, value_weight, head_size):
    length = normed.shape[0]

    def heads(weight):
        return jnp.dot(normed, weight, preferred_element_type=f32).reshape(length, -1, head_size)

    query_heads = apply_rotation(heads(w_query), *tables).astype(bf16)
    key_heads = apply_rotation(heads(key_weight), *tables).astype(bf16)
    value_heads = heads(value_weight).astype(bf16)
    scores, _ = block_scores(query_heads, key_heads, segment)
    largest = jnp.max(scores, axis=-1, keepdims=True)
    weights_raw = jnp.exp(scores - largest)
    totals = jnp.sum(weights_raw, axis=-1, keepdims=True)
    probs_low = (weights_raw / totals).astype(bf16)
    head_out = jnp.einsum("hgqk,khd->qhgd", probs_low, value_heads, preferred_element_type=f32)
    return (
        head_out.reshape(length, -1).astype(bf16),
        query_heads,
        key_heads,
        value_heads,
        (largest + jnp.log(totals))[..., 0],
    )


def attend_backward(query_heads, key_heads, value_heads, log_sums, heads_grad, segment, tables):
    length = query_heads.shape[0]
    cosine_table, sine_values = tables
    scores, grouped = block_scores(query_heads, key_heads, segment)
    probability = jnp.exp(scores - log_sums[..., None])
    probs_low = probability.astype(bf16)
    grad_grouped = heads_grad.reshape(grouped.shape)
    prob_grad = jnp.einsum(
        "qhgd,khd->hgqk", grad_grouped, value_heads, preferred_element_type=f32
    )
    weighted = jnp.sum(probability * prob_grad, axis=-1, keepdims=True)
    score_low = (probability * (prob_grad - weighted)).astype(bf16)
    query_part = (
        jnp.einsum("hgqk,khd->qhgd", score_low, key_heads, preferred_element_type=f32) * attn_scale
    ).reshape(query_heads.shape)
    key_sum = (
        jnp.einsum("hgqk,qhgd->khd", score_low, grouped, preferred_element_type=f32) * attn_scale
    )
    value_sum = jnp.einsum(
        "hgqk,qhgd->khd", probs_low, grad_grouped, preferred_element_type=f32
    )
    query_low = apply_rotation(query_part, cosine_table, -sine_values).astype(bf16)
    key_low = apply_rotation(key_sum, cosine_table, -sine_values).astype(bf16)
    return (
        query_low.reshape(length, -1),
        key_low.reshape(length, -1),
        value_sum.astype(bf16).reshape(length, -1),
    )


def bit_masks(size):
    masks = []
    while size > 1:
        size //= 2
        masks.append(size)
    return masks[::-1]


def swap(x, axis, mask):
    return lax.ppermute(x, axis, [(i, i ^ mask) for i in range(lax.axis_size(axis))])


def bit_of(axis, mask):
    return (lax.axis_index(axis) // mask) % 2


def halves_by_bit(x, axis, mask, dim=0):
    half = x.shape[dim] // 2
    bit = bit_of(axis, mask)
    mine = lax.dynamic_slice_in_dim(x, bit * half, half, dim)
    other = lax.dynamic_slice_in_dim(x, (1 - bit) * half, half, dim)
    return mine, other


def join_by_bit(mine, other, axis, mask, dim=0):
    return jnp.where(
        bit_of(axis, mask) == 0,
        jnp.concatenate([mine, other], dim),
        jnp.concatenate([other, mine], dim),
    )


def scatter_sum(x, axis, masks, kind, dim=0):
    x = x.astype(f32)
    for mask in masks:
        mine, other = halves_by_bit(x, axis, mask, dim)
        x = mine + swap(other.astype(kind), axis, mask).astype(f32)
    return x


def gather_blocks(x, axis, masks, dim=0):
    for mask in reversed(masks):
        x = join_by_bit(x, swap(x, axis, mask), axis, mask, dim)
    return x


def sum_all(x, axis):
    for mask in bit_masks(lax.axis_size(axis)):
        x = x + swap(x, axis, mask)
    return x


def rotated(masks, j):
    j = j % len(masks)
    return masks[j:] + masks[:j]


def row_parts(rows, count):
    units = rows // 16
    sizes = [16 * (units // count + (1 if i < units % count else 0)) for i in range(count)]
    starts = [sum(sizes[:i]) for i in range(count)]
    return list(zip(starts, sizes))


def cube_orders(masks, count):
    orders = []
    for j in range(count):
        order = [0]
        for mask in rotated(masks, j):
            order = order + [o ^ mask for o in order]
        orders.append(order)
    return orders


def peer_of(mask):
    me = lax.axis_index("dp")
    bit = (me // mask) % 2
    return me + mask * (1 - 2 * bit), bit


def remote(src, dst, send, recv, mask):
    return pltpu.make_async_remote_copy(
        src_ref=src,
        dst_ref=dst,
        send_sem=send,
        recv_sem=recv,
        device_id={"dp": peer_of(mask)[0]},
        device_id_type=pl.DeviceIdType.MESH,
    )


def greet(masks):
    barrier = pltpu.get_barrier_semaphore()
    for mask in masks:
        pl.semaphore_signal(
            barrier,
            inc=1,
            device_id={"dp": peer_of(mask)[0]},
            device_id_type=pl.DeviceIdType.MESH,
        )
    pl.semaphore_wait(barrier, len(masks))


def gather_kernel(masks, parts, n, *refs):
    ins, outs = refs[:n], refs[n:2 * n]
    local, send, recv = refs[2 * n:]
    greet(masks)
    size = 2 ** len(masks)
    locals_ = []
    for a in range(n):
        for j, (s, m) in enumerate(parts):
            c = pltpu.make_async_copy(ins[a].at[pl.ds(s, m)], outs[a].at[pl.ds(size * s, m)], local.at[a, j])
            c.start()
            locals_.append(c)
    sent = []
    copies = {}
    for phase in range(len(masks)):
        for a in range(n):
            for j, (s, m) in enumerate(parts):
                mask = rotated(masks, j)[phase]
                count = 2 ** phase * m
                if phase == 0:
                    src = ins[a].at[pl.ds(s, m)]
                else:
                    copies[a, j, phase - 1].wait_recv()
                    if phase == 1:
                        locals_[a * len(parts) + j].wait()
                    src = outs[a].at[pl.ds(size * s, count)]
                c = remote(src, outs[a].at[pl.ds(size * s + count, count)],
                           send.at[a, j, phase], recv.at[a, j, phase], mask)
                c.start()
                copies[a, j, phase] = c
    for (a, j, phase), c in copies.items():
        if phase == len(masks) - 1:
            c.wait_recv()
    for c in copies.values():
        c.wait_send()

def cube_gather(arrays, masks, collective_id, mult=1, space=pl.ANY):
    n = len(arrays)
    rows = arrays[0].shape[0]
    parts = row_parts(rows, mult*len(masks))
    size = 2 ** len(masks)
    return pl.pallas_call(
        functools.partial(gather_kernel, masks, parts, n),
        out_shape=[jax.ShapeDtypeStruct((size * rows,) + x.shape[1:], x.dtype) for x in arrays],
        in_specs=[pl.BlockSpec(memory_space=pl.ANY)] * n,
        out_specs=[pl.BlockSpec(memory_space=space)] * n,
        scratch_shapes=[pltpu.SemaphoreType.DMA((n, len(parts))),
                        pltpu.SemaphoreType.DMA((n, len(parts), len(masks))),
                        pltpu.SemaphoreType.DMA((n, len(parts), len(masks)))],
        compiler_params=pltpu.CompilerParams(collective_id=collective_id, has_side_effects=True, vmem_limit_bytes=40<<20),
    )(*arrays)

def tiles(rows):
    return 16

def add_rows(dst, dst0, a, a0, b, b0, rows, out_dtype):
    step = 16
    def body(i, _):
        r = pl.multiple_of(i * step, step)
        x = a[pl.ds(a0 + r, step), :].astype(f32) + b[pl.ds(b0 + r, step), :].astype(f32)
        dst[pl.ds(dst0 + r, step), :] = x.astype(out_dtype)
        return 0
    lax.fori_loop(0, rows // step, body, 0, unroll=False)

def scatter_kernel(masks, parts, n, *refs):
    ins, outs = refs[:n], refs[n:2 * n]
    lows, gots, local, send, recv = refs[2 * n:]
    k = len(masks)
    size = 2 ** k
    half = size // 2
    rows = sum(m for _, m in parts)
    for a in range(n):
        for j, (s, m) in enumerate(parts):
            pltpu.make_async_copy(ins[a].at[pl.ds(size * s, half * m)], lows.at[a, pl.ds(half * s, half * m)], local.at[a, j]).start()
    greet(masks)
    copies = {}
    def got_at(a, j, phase):
        s, m = parts[j]
        count = 2 ** phase * m
        base = rows * (size - 2 ** (phase + 1))
        return base + 2 ** phase * s, count
    for phase in reversed(range(k)):
        for a in range(n):
            for j, (s, m) in enumerate(parts):
                count = 2 ** phase * m
                mask = rotated(masks, j)[phase]
                if phase == k - 1:
                    src = ins[a].at[pl.ds(size * s + count, count)]
                else:
                    g0, c0 = got_at(a, j, phase + 1)
                    copies[a, j, phase + 1].wait_recv()
                    if phase == k - 2:
                        pltpu.make_async_copy(ins[a].at[pl.ds(size * s, half * m)], lows.at[a, pl.ds(half * s, half * m)], local.at[a, j]).wait()
                    low = lows.at[a]
                    got = gots.at[a]
                    add_rows(low, half * s + count, low, half * s + count, got, g0 + count, count, bf16)
                    src = lows.at[a, pl.ds(half * s + count, count)]
                o0, _ = got_at(a, j, phase)
                c = remote(src, gots.at[a, pl.ds(o0, count)], send.at[a, j, phase], recv.at[a, j, phase], mask)
                c.start()
                copies[a, j, phase] = c
                if phase < k - 1:
                    add_rows(low, half * s, low, half * s, got, g0, count, bf16)
    for a in range(n):
        for j, (s, m) in enumerate(parts):
            copies[a, j, 0].wait_recv()
            g0, _ = got_at(a, j, 0)
            add_rows(outs[a], s, lows.at[a], half * s, gots.at[a], g0, m, f32)
    for c in copies.values():
        c.wait_send()

def cube_scatter(arrays, masks, collective_id, mult=1):
    n = len(arrays)
    size = 2 ** len(masks)
    rows, width = arrays[0].shape[0] // size, arrays[0].shape[1]
    parts = row_parts(rows, mult*len(masks))
    k = len(masks)
    return pl.pallas_call(
        functools.partial(scatter_kernel, masks, parts, n),
        out_shape=[jax.ShapeDtypeStruct((rows, width), f32) for x in arrays],
        in_specs=[pl.BlockSpec(memory_space=pl.ANY)] * n,
        out_specs=[pl.BlockSpec(memory_space=pltpu.VMEM)] * n,
        scratch_shapes=[pltpu.VMEM((n, size // 2 * rows, width), bf16),
                        pltpu.VMEM((n, (size - 1) * rows, width), bf16),
                        pltpu.SemaphoreType.DMA((n, len(parts))),
                        pltpu.SemaphoreType.DMA((n, len(parts), k)),
                        pltpu.SemaphoreType.DMA((n, len(parts), k))],
        compiler_params=pltpu.CompilerParams(collective_id=collective_id, has_side_effects=True,
                                             vmem_limit_bytes=40 << 20),
    )(*arrays)

def reduce_kernel(orders, x_ref, small_ref, out_ref, small_out, acc, got, small_got, load, send, recv, small_send, small_recv):
    k = len(orders[0])
    nparts = len(orders)
    size = x_ref.shape[0] // nparts
    width = x_ref.shape[1]
    for j in range(nparts):
        pltpu.make_async_copy(x_ref.at[pl.ds(j * size, size)], acc.at[pl.ds(j * size, size)], load.at[j]).start()
    greet(sorted(orders[0]))
    small_out[...] = small_ref[...]
    copies = {}
    where = [j * size for j in range(nparts)]
    small_copies = []
    for step in range(k):
        count = size >> (step + 1)
        for j in range(nparts):
            mask = orders[j][step]
            _, bit = peer_of(mask)
            if step == 0:
                pltpu.make_async_copy(x_ref.at[pl.ds(j * size, size)], acc.at[pl.ds(j * size, size)], load.at[j]).wait()
            keep = pl.multiple_of(where[j] + bit * count, 16)
            give = pl.multiple_of(where[j] + (1 - bit) * count, 16)
            if step > 0:
                prev = copies[j, step - 1]
                prev.wait_recv()
                p0 = j * size + (size - (size >> (step - 1)))
                add_rows(acc, give, acc, give, got, p0 + pl.multiple_of((1 - bit) * count, 16), count, bf16)
            g0 = j * size + (size - (size >> step))
            c = remote(acc.at[pl.ds(give, count)], got.at[pl.ds(g0, count)], send.at[j, step], recv.at[j, step], mask)
            c.start()
            copies[j, step] = c
            if step > 0:
                add_rows(acc, keep, acc, keep, got, p0 + pl.multiple_of(bit * count, 16), count, bf16)
            where[j] = keep
        mask = orders[0][step]
        if step > 0:
            small_copies[-1].wait_send()
            small_copies[-1].wait_recv()
            small_out[...] += small_got[step - 1]
        c = remote(small_out, small_got.at[step], small_send.at[step], small_recv.at[step], mask)
        c.start()
        small_copies.append(c)
    back = {}
    for step in reversed(range(k)):
        count = size >> (step + 1)
        for j in range(nparts):
            mask = orders[j][step]
            _, bit = peer_of(mask)
            if step == k - 1:
                copies[j, step].wait_recv()
                p0 = j * size + (size - (size >> step))
                add_rows(out_ref, where[j], acc, where[j], got, p0, count, bf16)
            else:
                back[j, step + 1].wait_recv()
            here = where[j]
            c = remote(out_ref.at[pl.ds(here, count)], out_ref.at[pl.ds(here, count)], send.at[j, k + step], recv.at[j, k + step], mask)
            c.start()
            back[j, step] = c
            where[j] = pl.multiple_of(here - bit * count, 16)
    small_copies[-1].wait_send()
    small_copies[-1].wait_recv()
    small_out[...] += small_got[k - 1]
    for j in range(nparts):
        back[j, 0].wait_recv()
    for c in copies.values():
        c.wait_send()
    for c in back.values():
        c.wait_send()

def all_reduce(x, small, masks, collective_id, nparts=3):
    inner, last = masks[:-1], masks[-1:]
    orders = [rotated(inner, j) + last for j in range(nparts)]
    k = len(masks)
    rows, width = x.shape
    vm = pl.BlockSpec(memory_space=pltpu.VMEM)
    return pl.pallas_call(
        functools.partial(reduce_kernel, orders),
        out_shape=[jax.ShapeDtypeStruct(x.shape, bf16), jax.ShapeDtypeStruct(small.shape, f32)],
        in_specs=[pl.BlockSpec(memory_space=pl.ANY), vm],
        out_specs=[vm, vm],
        scratch_shapes=[pltpu.VMEM(x.shape, bf16), pltpu.VMEM(x.shape, bf16),
                        pltpu.VMEM((k,) + small.shape, f32),
                        pltpu.SemaphoreType.DMA((nparts,)),
                        pltpu.SemaphoreType.DMA((nparts, 2 * k)), pltpu.SemaphoreType.DMA((nparts, 2 * k)),
                        pltpu.SemaphoreType.DMA((k,)), pltpu.SemaphoreType.DMA((k,))],
        compiler_params=pltpu.CompilerParams(collective_id=collective_id, has_side_effects=True,
                                             vmem_limit_bytes=40 << 20),
    )(x, small)


def vector_gather(x, masks):
    x = x[None]
    for mask in masks:
        x = jnp.concatenate([x, swap(x, "dp", mask)], 0)
    return x


def vector_scatter(x, masks):
    for mask in reversed(masks):
        half = x.shape[0] // 2
        x = x[:half] + swap(x[half:], "dp", mask)
    return x[0]


def to_cube_rows(x, masks):
    parts = row_parts(x.shape[1], 2 * len(masks))
    orders = cube_orders(masks, 2 * len(masks))
    return jnp.concatenate(
        [x[o, s : s + n] for (s, n), order in zip(parts, orders) for o in order]
    )


def from_cube_rows(x, masks):
    devices = 2 ** len(masks)
    parts = row_parts(x.shape[0] // devices, 2 * len(masks))
    orders = cube_orders(masks, 2 * len(masks))
    found = {}
    for j, ((s, n), order) in enumerate(zip(parts, orders)):
        for place, o in enumerate(order):
            first = devices * s + place * n
            found[o, j] = x[first : first + n]
    return jnp.stack(
        [jnp.concatenate([found[o, j] for j in range(2 * len(masks))]) for o in range(devices)]
    )


def dot(a, b, spec):
    return jnp.einsum(spec, a, b, preferred_element_type=f32)


def expert_passes(rows, grads, column, w_gate, w_up, w_down):
    gate_act = dot(rows, w_gate, "td,df->tf")
    up_act = dot(rows, w_up, "td,df->tf")
    sigmoid_gate = jax.nn.sigmoid(gate_act)
    silu_gate = gate_act * sigmoid_gate
    hidden = silu_gate * up_act
    weighted_low = (hidden * column[:, None]).astype(bf16)
    down_in = residual_scale * dot(grads, w_down, "td,fd->tf")
    gate_deriv = jnp.sum(hidden * down_in, axis=1)
    down_in = down_in * column[:, None]
    gate_low = (down_in * up_act * sigmoid_gate * (1.0 + gate_act * (1.0 - sigmoid_gate))).astype(
        bf16
    )
    up_low = (down_in * silu_gate).astype(bf16)
    return weighted_low, gate_deriv, gate_low, up_low


def per_device(
    hidden_in,
    attn_gain,
    w_query,
    key_weight,
    value_weight,
    w_output,
    moe_gain,
    w_router,
    w_gate,
    w_up,
    w_down,
    expert_ids,
    segment_ids,
    out_grad,
):
    tokens_here, model_width = hidden_in.shape
    head_size = HEAD_DIM
    dp_size = lax.axis_size("dp")
    tensor_size = lax.axis_size("tensor")
    experts = w_gate.shape[0] * dp_size
    dp_index = lax.axis_index("dp")
    tensor_index = lax.axis_index("tensor")
    masks = bit_masks(dp_size)
    cube, pair = masks[:-1], masks[-1]
    tensor_masks = bit_masks(tensor_size)
    tensor_down = tensor_masks[::-1]
    rows_here = tokens_here // tensor_size

    def my_rows(x):
        return lax.dynamic_slice_in_dim(x, tensor_index * rows_here, rows_here, 0)

    block = w_gate.shape[2] // tensor_size

    def my_units(x, dim):
        return lax.dynamic_slice_in_dim(x, tensor_index * block, block, dim)

    def relative_gather(x, dim):
        for mask in tensor_masks:
            x = jnp.concatenate([x, swap(x, "tensor", mask)], dim)
        return x

    def relative_scatter(x, dim):
        x = x.astype(f32)
        for mask in reversed(tensor_masks):
            half = x.shape[dim] // 2
            keep = lax.slice_in_dim(x, 0, half, axis=dim)
            give = lax.slice_in_dim(x, half, 2 * half, axis=dim)
            x = keep + swap(give.astype(bf16), "tensor", mask).astype(f32)
        return x

    far_gate = relative_gather(swap(my_units(w_gate[0], 1), "dp", pair), 1)
    far_up = relative_gather(swap(my_units(w_up[0], 1), "dp", pair), 1)
    far_down = relative_gather(swap(my_units(w_down[0], 0), "dp", pair), 0)

    grad_mine = my_rows(out_grad)

    inputs = hidden_in.astype(f32)
    scale_in = lax.rsqrt(jnp.mean(inputs * inputs, axis=-1, keepdims=True) + epsilon)
    normed_low = (inputs * scale_in * attn_gain).astype(bf16)
    segment = segment_ids[0]
    tables = rope_tables(segment, head_size)
    heads_flat, query_heads, key_heads, value_heads, log_sums = attend_forward(
        normed_low, segment, tables, w_query, key_weight, value_weight, head_size
    )
    attn_part = jnp.dot(heads_flat, w_output, preferred_element_type=f32)
    attn_total = scatter_sum(attn_part, "tensor", tensor_down, f32)

    inputs_mine = my_rows(hidden_in).astype(f32)
    scale_in_mine = my_rows(scale_in)
    middle = inputs_mine + residual_scale * attn_total
    scale_mid = lax.rsqrt(jnp.mean(middle * middle, axis=-1, keepdims=True) + epsilon)
    routed_low = (middle * scale_mid * moe_gain).astype(bf16)
    rows, grads = cube_gather([routed_low, grad_mine], cube, 0, 2)

    logits = dot(w_router, routed_low, "de,td->et")
    ids_mine = my_rows(expert_ids).T
    expert_range = jnp.arange(experts, dtype=jnp.int32)
    picked = jnp.any(ids_mine[None, :, :] == expert_range[:, None, None], axis=1)
    largest = jnp.max(jnp.where(picked, logits, -jnp.inf), axis=0, keepdims=True)
    raised = jnp.where(picked, jnp.exp(jnp.where(picked, logits - largest, 0.0)), 0.0)
    gate_weights = raised / jnp.sum(raised, axis=0, keepdims=True)
    all_weights = vector_gather(gate_weights, cube)
    near, far = dp_index, dp_index ^ pair

    def column_of(expert):
        picked_row = lax.dynamic_index_in_dim(all_weights, expert, 1, keepdims=False)
        return to_cube_rows(picked_row, cube)

    near_set = (w_gate[0], w_up[0], w_down[0])
    far_set = (far_gate, far_up, far_down)
    near_low, near_deriv, near_gate_low, near_up_low = expert_passes(
        rows, grads, column_of(near), *near_set
    )
    far_low, far_deriv, far_gate_low, far_up_low = expert_passes(
        rows, grads, column_of(far), *far_set
    )
    moe_part = dot(near_low, w_down[0], "tf,fd->td") + dot(far_low, far_down, "tf,fd->td")

    one_near = (expert_range == near).astype(f32)[None, :, None]
    one_far = (expert_range == far).astype(f32)[None, :, None]
    deriv_part = (
        one_near * from_cube_rows(near_deriv, cube)[:, None, :]
        + one_far * from_cube_rows(far_deriv, cube)[:, None, :]
    )
    gate_deriv = vector_scatter(deriv_part, cube)

    routed_part = (
        dot(near_gate_low, w_gate[0], "tf,df->td")
        + dot(near_up_low, w_up[0], "tf,df->td")
        + dot(far_gate_low, far_gate, "tf,df->td")
        + dot(far_up_low, far_up, "tf,df->td")
    )
    moe_total, routed_grad = cube_scatter(
        [moe_part.astype(bf16), routed_part.astype(bf16)], cube, 1, 2
    )

    far_gate_grad = relative_scatter(dot(rows, far_gate_low, "td,tf->df"), 1)
    far_up_grad = relative_scatter(dot(rows, far_up_low, "td,tf->df"), 1)
    far_down_grad = relative_scatter(residual_scale * dot(far_low, grads, "tf,td->fd"), 0)
    near_gate_grad = scatter_sum(
        dot(rows, near_gate_low, "td,tf->df"), "tensor", tensor_down, bf16, 1
    )
    near_up_grad = scatter_sum(dot(rows, near_up_low, "td,tf->df"), "tensor", tensor_down, bf16, 1)
    near_down_grad = scatter_sum(
        residual_scale * dot(near_low, grads, "tf,td->fd"), "tensor", tensor_down, bf16, 0
    )

    def returned(mine, away, dim):
        whole = mine + swap(away.astype(bf16), "dp", pair).astype(f32)
        return gather_blocks(whole, "tensor", tensor_down, dim)[None]

    gate_grad = returned(near_gate_grad, far_gate_grad, 1)
    up_grad = returned(near_up_grad, far_up_grad, 1)
    down_grad = returned(near_down_grad, far_down_grad, 0)

    block_mine = (middle + residual_scale * moe_total).astype(bf16)
    block_out = gather_blocks(block_mine, "tensor", tensor_down)

    chosen_grad = gate_weights * (
        gate_deriv - jnp.sum(gate_weights * gate_deriv, axis=0, keepdims=True)
    )
    logit_grad = chosen_grad.astype(bf16)
    router_part = dot(logit_grad, routed_low, "et,td->ed")
    routed_grad = routed_grad + dot(logit_grad, w_router, "et,de->td")
    gained = moe_gain * routed_grad
    moe_gain_part = jnp.sum(routed_grad * middle * scale_mid, axis=0)
    grad_top = grad_mine.astype(f32)
    middle_grad = (
        grad_top
        + scale_mid * gained
        - middle
        * (scale_mid * scale_mid * scale_mid)
        * jnp.mean(middle * gained, axis=-1, keepdims=True)
    )
    branch_low = gather_blocks(
        (residual_scale * middle_grad).astype(bf16), "tensor", tensor_down
    )
    heads_grad = dot(branch_low, w_output, "td,cd->tc").astype(bf16)
    query_low, key_low, value_low = attend_backward(
        query_heads, key_heads, value_heads, log_sums, heads_grad, segment, tables
    )
    width_q, width_k = query_low.shape[1], key_low.shape[1]
    qkv_low = jnp.concatenate([query_low, key_low, value_low], axis=1)
    heads_width = heads_flat.shape[1]
    w_output_part = [
        dot(heads_flat, branch_low[:, i : i + heads_width], "tc,td->cd")
        for i in range(0, model_width, heads_width)
    ]
    attention_part = jnp.concatenate(
        [dot(normed_low, qkv_low, "td,tc->dc"), jnp.concatenate(w_output_part, 0)], 1
    ).astype(bf16)
    qkv_weight = jnp.concatenate([w_query, key_weight, value_weight], axis=1)
    normed_part = dot(qkv_low, qkv_weight, "tc,dc->td")
    normed_grad = scatter_sum(normed_part, "tensor", tensor_down, f32)
    gained_in = attn_gain * normed_grad
    attn_gain_part = jnp.sum(normed_grad * inputs_mine * scale_in_mine, axis=0)
    input_mine = (
        middle_grad
        + scale_in_mine * gained_in
        - inputs_mine
        * (scale_in_mine * scale_in_mine * scale_in_mine)
        * jnp.mean(inputs_mine * gained_in, axis=-1, keepdims=True)
    )
    input_grad = gather_blocks(input_mine, "tensor", tensor_down)

    small = jnp.concatenate([router_part, moe_gain_part[None], attn_gain_part[None]], 0)
    small = jnp.pad(small, ((0, -small.shape[0] % 8), (0, 0)))
    for mask in tensor_masks:
        small = small + swap(small, "tensor", mask)
    attention_grad, small = all_reduce(attention_part, small, masks, 2)
    attention_grad = attention_grad.astype(f32)
    qkv_width = qkv_low.shape[1]
    qkv_grad = attention_grad[:, :qkv_width]
    w_output_grad = jnp.concatenate(
        [
            attention_grad[i : i + heads_width, qkv_width:]
            for i in range(0, model_width, heads_width)
        ],
        1,
    )
    return (
        block_out,
        input_grad,
        small[experts + 1],
        qkv_grad[:, :width_q],
        qkv_grad[:, width_q : width_q + width_k],
        qkv_grad[:, width_q + width_k :],
        w_output_grad,
        small[experts],
        small[:experts].T,
        gate_grad,
        up_grad,
        down_grad,
    )


def solution(mesh):
    placed = (
        P("dp", None),
        P(),
        P(None, "tensor"),
        P(None, "tensor"),
        P(None, "tensor"),
        P("tensor", None),
        P(),
        P(),
        P("dp", None, None),
        P("dp", None, None),
        P("dp", None, None),
        P("dp", None),
        P("dp", None),
        P("dp", None),
    )
    return jax.shard_map(
        per_device,
        mesh=mesh,
        in_specs=placed,
        out_specs=(
            P("dp", None),
            P("dp", None),
            P(),
            P(None, "tensor"),
            P(None, "tensor"),
            P(None, "tensor"),
            P("tensor", None),
            P(),
            P(),
            P("dp", None, None),
            P("dp", None, None),
            P("dp", None, None),
        ),
        check_vma=False,
    )
```

```python
import functools

import jax
import jax.numpy as jnp
from jax import lax
from jax.experimental import pallas as pl
from jax.experimental.pallas import tpu as pltpu
from jax.sharding import PartitionSpec as P

HEAD_DIM = 64

bf16 = jnp.bfloat16
f32 = jnp.float32
MESH = pl.DeviceIdType.MESH
epsilon = 1e-06
residual_scale = 0.22
attn_scale = 0.015625
rope_base = 10000.0
masked_score = -1e30


def positions_of(segment):
    position_index = jnp.arange(segment.shape[0], dtype=jnp.int32)
    earlier = jnp.concatenate([segment[:1] - 1, segment[:-1]])
    starts = lax.cummax(jnp.where(segment != earlier, position_index, 0), axis=0)
    return position_index - starts


def rope_tables(segment, head_size):
    position = positions_of(segment).astype(f32)
    frequency = rope_base ** (-jnp.arange(head_size // 2, dtype=f32) * 2.0 / head_size)
    angle = position[:, None] * frequency[None, :]
    return (jnp.cos(angle)[:, None, :], jnp.sin(angle)[:, None, :])


def apply_rotation(heads_in, cosine_table, sine_values):
    middle_index = heads_in.shape[-1] // 2
    first_half = heads_in[..., :middle_index]
    second_half = heads_in[..., middle_index:]
    return jnp.concatenate(
        [
            first_half * cosine_table - second_half * sine_values,
            second_half * cosine_table + first_half * sine_values,
        ],
        axis=-1,
    )


def block_scores(query_heads, key_heads, segment):
    kv_count = key_heads.shape[1]
    length = query_heads.shape[0]
    grouped = query_heads.reshape(length, kv_count, -1, query_heads.shape[2])
    raw_scores = (
        jnp.einsum("qhgd,khd->hgqk", grouped, key_heads, preferred_element_type=f32) * attn_scale
    )
    index = jnp.arange(length, dtype=jnp.int32)
    allowed = (index[:, None] >= index[None, :]) & (segment[:, None] == segment[None, :])
    return (jnp.where(allowed, raw_scores, masked_score), grouped)


def attend_forward(normed, segment, tables, w_query, key_weight, value_weight, head_size):
    length = normed.shape[0]

    def heads(weight):
        return jnp.dot(normed, weight, preferred_element_type=f32).reshape(length, -1, head_size)

    query_heads = apply_rotation(heads(w_query), *tables).astype(bf16)
    key_heads = apply_rotation(heads(key_weight), *tables).astype(bf16)
    value_heads = heads(value_weight).astype(bf16)
    scores, _ = block_scores(query_heads, key_heads, segment)
    largest = jnp.max(scores, axis=-1, keepdims=True)
    weights_raw = jnp.exp(scores - largest)
    totals = jnp.sum(weights_raw, axis=-1, keepdims=True)
    probs_low = (weights_raw / totals).astype(bf16)
    head_out = jnp.einsum("hgqk,khd->qhgd", probs_low, value_heads, preferred_element_type=f32)
    return (
        head_out.reshape(length, -1).astype(bf16),
        query_heads,
        key_heads,
        value_heads,
        (largest + jnp.log(totals))[..., 0],
    )


def attend_backward(query_heads, key_heads, value_heads, log_sums, heads_grad, segment, tables):
    length = query_heads.shape[0]
    cosine_table, sine_values = tables
    scores, grouped = block_scores(query_heads, key_heads, segment)
    probability = jnp.exp(scores - log_sums[..., None])
    probs_low = probability.astype(bf16)
    grad_grouped = heads_grad.reshape(grouped.shape)
    prob_grad = jnp.einsum(
        "qhgd,khd->hgqk", grad_grouped, value_heads, preferred_element_type=f32
    )
    weighted = jnp.sum(probability * prob_grad, axis=-1, keepdims=True)
    score_low = (probability * (prob_grad - weighted)).astype(bf16)
    query_part = (
        jnp.einsum("hgqk,khd->qhgd", score_low, key_heads, preferred_element_type=f32) * attn_scale
    ).reshape(query_heads.shape)
    key_sum = (
        jnp.einsum("hgqk,qhgd->khd", score_low, grouped, preferred_element_type=f32) * attn_scale
    )
    value_sum = jnp.einsum(
        "hgqk,qhgd->khd", probs_low, grad_grouped, preferred_element_type=f32
    )
    query_low = apply_rotation(query_part, cosine_table, -sine_values).astype(bf16)
    key_low = apply_rotation(key_sum, cosine_table, -sine_values).astype(bf16)
    return (
        query_low.reshape(length, -1),
        key_low.reshape(length, -1),
        value_sum.astype(bf16).reshape(length, -1),
    )


def bit_masks(size):
    masks = []
    while size > 1:
        size //= 2
        masks.append(size)
    return masks[::-1]


def swap(x, axis, mask):
    return lax.ppermute(x, axis, [(i, i ^ mask) for i in range(lax.axis_size(axis))])


def bit_of(axis, mask):
    return (lax.axis_index(axis) // mask) % 2


def halves_by_bit(x, axis, mask, dim=0):
    half = x.shape[dim] // 2
    bit = bit_of(axis, mask)
    mine = lax.dynamic_slice_in_dim(x, bit * half, half, dim)
    other = lax.dynamic_slice_in_dim(x, (1 - bit) * half, half, dim)
    return mine, other


def join_by_bit(mine, other, axis, mask, dim=0):
    return jnp.where(
        bit_of(axis, mask) == 0,
        jnp.concatenate([mine, other], dim),
        jnp.concatenate([other, mine], dim),
    )


def scatter_sum(x, axis, masks, kind, dim=0):
    x = x.astype(f32)
    for mask in masks:
        mine, other = halves_by_bit(x, axis, mask, dim)
        x = mine + swap(other.astype(kind), axis, mask).astype(f32)
    return x


def gather_blocks(x, axis, masks, dim=0):
    for mask in reversed(masks):
        x = join_by_bit(x, swap(x, axis, mask), axis, mask, dim)
    return x


def rotated(masks, j):
    j = j % len(masks)
    return masks[j:] + masks[:j]


def peer_of(mask):
    me = lax.axis_index("dp")
    bit = (me // mask) % 2
    return me + mask * (1 - 2 * bit), bit


def greet(masks):
    barrier = pltpu.get_barrier_semaphore()
    for mask in masks:
        pl.semaphore_signal(
            barrier, inc=1, device_id={"dp": peer_of(mask)[0]}, device_id_type=MESH
        )
    pl.semaphore_wait(barrier, len(masks))


def remote(src, dst, send, recv, mask):
    return remote_to(src, dst, send, recv, peer_of(mask)[0])


def add_rows(dst, dst0, a, a0, b, b0, rows, out_dtype):
    step = 16

    def body(i, _):
        r = pl.multiple_of(i * step, step)
        x = a[pl.ds(a0 + r, step), :].astype(f32) + b[pl.ds(b0 + r, step), :].astype(f32)
        dst[pl.ds(dst0 + r, step), :] = x.astype(out_dtype)
        return 0

    lax.fori_loop(0, rows // step, body, 0)


def group_sizes(dp_size):
    a = 4
    return a, dp_size // (2 * a)


class Spot:
    def __init__(self, a, b):
        me = lax.axis_index("dp")
        self.a, self.b = a, b
        self.n = a * b
        self.me = me
        self.A = me // (2 * b)
        self.B = (me // 2) % b
        self.block = me // 2
        self.pair = me % 2
        self.devices = (me + 2 * b, me - 2 * b, me + 2, me - 2)
        self.exists = (self.A < a - 1, self.A > 0, self.B < b - 1, self.B > 0)
        self.some = me + 2 * (1 - 2 * (self.B % 2))

    def greet(self):
        barrier = pltpu.get_barrier_semaphore()
        for device, there in zip(self.devices, self.exists):

            @pl.when(there)
            def _(device=device):
                pl.semaphore_signal(
                    barrier, inc=1, device_id={"dp": device}, device_id_type=MESH
                )

        a, b = self.a, self.b
        ups = 2 - (self.A + 1) // a - (self.B + 1) // b
        downs = (self.A + a - 1) // a + (self.B + b - 1) // b
        pl.semaphore_wait(barrier, ups + downs)


def is_at(x, value):
    return 1 // (1 + (x - value) * (x - value))


def by_distance(size, place, k):
    found = 0
    for p in range(size):
        order = sorted(range(size), key=lambda q: (abs(q - p), q))
        for j, q in enumerate(order):
            if q > 0:
                found = found + q * is_at(place, p) * is_at(k, j)
    return found


def visit_order(a, b):
    pairs = [(k, l) for k in range(a) for l in range(b)]
    return sorted(pairs, key=lambda kl: kl[0] + (2 * kl[1] + 0.5 if kl[1] else 0))


def remote_to(src, dst, send, recv, device):
    return pltpu.make_async_remote_copy(
        src_ref=src,
        dst_ref=dst,
        send_sem=send,
        recv_sem=recv,
        device_id={"dp": device},
        device_id_type=MESH,
    )


PIECES = 2
SUM_PIECES = 4


class LineGather:
    def __init__(self, spot, buf, rows, send, recv):
        self.spot, self.buf, self.rows, self.send, self.recv = spot, buf, rows, send, recv

    def coords(self, i):
        s = self.spot
        visits = visit_order(s.a, s.b)
        k = sum(v[0] * is_at(i, j) for j, v in enumerate(visits) if v[0])
        l = sum(v[1] * is_at(i, j) for j, v in enumerate(visits) if v[1])
        return by_distance(s.a, s.A, k), by_distance(s.b, s.B, l)

    def row0(self, i):
        A, B = self.coords(i)
        return pl.multiple_of((A * self.spot.b + B) * self.rows, 16)

    def copies(self, block, way, device):
        size = self.rows // PIECES
        return [
            remote_to(there, there, self.send.at[block, way, p], self.recv.at[block, p], device)
            for p in range(PIECES)
            for there in [self.buf.at[pl.ds(pl.multiple_of(block * self.rows + p * size, 16), size)]]
        ]

    def each_way(self, i, act):
        s = self.spot
        A, B = self.coords(i)
        block = A * s.b + B
        same = B == s.B
        conditions = (
            same & (A <= s.A) & s.exists[0],
            same & (A >= s.A) & s.exists[1],
            (B <= s.B) & s.exists[2],
            (B >= s.B) & s.exists[3],
        )
        for way, (condition, device) in enumerate(zip(conditions, s.devices)):

            @pl.when(condition)
            def _(way=way, device=device):
                for c in self.copies(block, way, device):
                    act(c)

    def wait(self, i):
        A, B = self.coords(i)
        for c in self.copies(A * self.spot.b + B, 0, self.spot.some):
            c.wait_recv()

    def forward(self, i):
        self.each_way(i, lambda c: c.start())

    def finish(self):
        def one(i, _):
            self.each_way(i, lambda c: c.wait_send())
            return 0

        lax.fori_loop(0, self.spot.n, one, 0)


def add_into(dst, d0, src, s0, rows, step=16):
    def body(i, _):
        r = pl.multiple_of(i * step, step)
        total = dst[pl.ds(d0 + r, step), :].astype(f32) + src[pl.ds(s0 + r, step), :].astype(f32)
        dst[pl.ds(d0 + r, step), :] = total.astype(dst.dtype)
        return 0

    lax.fori_loop(0, rows // step, body, 0)


class LineSum:
    def __init__(self, size, place, up, down, part, row_of, rows, got, send, recv, some):
        self.size, self.place, self.up, self.down = size, place, up, down
        self.part, self.row_of, self.rows, self.got = part, row_of, rows, got
        self.send, self.recv, self.some = send, recv, some

    def up_slot(self, place, c):
        return c - place

    def down_slot(self, place, c):
        return c + (self.size - place) * ((place + self.size - 1) // self.size)

    def copies(self, c, slot, send, device):
        size = self.rows // SUM_PIECES
        return [
            remote_to(
                self.part.at[pl.ds(pl.multiple_of(self.row_of(c) + p * size, 16), size)],
                self.got.at[pl.ds(pl.multiple_of(slot * self.rows + p * size, 16), size)],
                send.at[p],
                self.recv.at[slot, p],
                device,
            )
            for p in range(SUM_PIECES)
        ]

    def take(self, c, slot, p, dst=None, d0=None):
        if dst is None:
            dst, d0 = self.part, self.row_of(c)
        size = self.rows // SUM_PIECES
        self.copies(c, slot, self.send.at[0, 0], self.some)[p].wait_recv()
        from_row = pl.multiple_of(slot * self.rows + p * size, 16)
        add_into(dst, d0 + p * size, self.got, from_row, size)

    def up_copies(self, k):
        c = self.size - 1 - k
        return self.copies(c, self.up_slot(self.place + 1, c), self.send.at[k, 0], self.up)

    def down_copies(self, k):
        return self.copies(k, self.down_slot(self.place - 1, k), self.send.at[k, 1], self.down)

    def step_up(self, k):
        c = self.size - 1 - k

        @pl.when(c > self.place)
        def _():
            for p, copy in enumerate(self.up_copies(k)):

                @pl.when(self.place > 0)
                def _(p=p):
                    self.take(c, self.up_slot(self.place, c), p)

                copy.start()

    def step_down(self, k):
        @pl.when(k < self.place)
        def _():
            for p, copy in enumerate(self.down_copies(k)):

                @pl.when(self.place < self.size - 1)
                def _(p=p):
                    self.take(k, self.down_slot(self.place, k), p)

                copy.start()

    def step(self, k):
        self.step_up(k)
        self.step_down(k)

    def end(self, out=None):
        p = self.place
        d0 = None
        if out is not None:
            out[...] = self.part[pl.ds(self.row_of(p), self.rows), :].astype(out.dtype)
            d0 = 0

        @pl.when(p > 0)
        def _():
            for j in range(SUM_PIECES):
                self.take(p, self.up_slot(p, p), j, out, d0)

        @pl.when(p < self.size - 1)
        def _():
            for j in range(SUM_PIECES):
                self.take(p, self.down_slot(p, p), j, out, d0)

        for k in range(self.size - 1):

            @pl.when(self.size - 1 - k > p)
            def _(k=k):
                for c in self.up_copies(k):
                    c.wait_send()

            @pl.when(k < p)
            def _(k=k):
                for c in self.down_copies(k):
                    c.wait_send()


def slots_of(size):
    return 1 if size == 2 else size + 1


class GroupSum:
    def __init__(self, spot, part, rows, got_b, got_a, send_b, recv_b, send_a, recv_a):
        self.spot, self.part, self.rows = spot, part, rows
        a, b = spot.a, spot.b
        slots_b = slots_of(b)

        def b_line(A):
            return LineSum(
                b, spot.B, spot.devices[2], spot.devices[3], part,
                lambda B: pl.multiple_of((A * b + B) * rows, 16), rows,
                got_b.at[pl.ds(pl.multiple_of(A * slots_b * rows, 16), slots_b * rows)],
                send_b.at[A], recv_b.at[A], spot.some,
            )

        self.b_line = b_line
        self.a_line = LineSum(
            a, spot.A, spot.devices[0], spot.devices[1], part,
            lambda A: pl.multiple_of((A * b + spot.B) * rows, 16), rows,
            got_a, send_a, recv_a, spot.some,
        )

    def ready(self, A, B):
        if self.spot.b == 2:
            line = self.b_line(A)

            @pl.when(B != self.spot.B)
            def _():
                line.step(0)

    def along_b(self):
        if self.spot.b > 2:

            def one(A, _):
                for k in range(self.spot.b - 1):
                    self.b_line(A).step(k)
                return 0

            lax.fori_loop(0, self.spot.a, one, 0)

    def flow(self, fills):
        a, line = self.spot.a, self.a_line
        fills = list(fills)

        def fill():
            if fills:
                fills.pop(0)()

        for k in range(a - 1):
            if 2 * k < a:
                self.b_line(a - 1 - k).end()
            line.step_up(k)
            fill()
            if 2 * k < a and a - 1 - k != k:
                self.b_line(k).end()
            line.step_down(k)
            fill()
        while fills:
            fill()

    def order(self, j):
        a = self.spot.a
        places = sorted(range(a), key=lambda c: (min(c, a - 1 - c), -c))
        return sum(c * is_at(j, i) for i, c in enumerate(places) if c)

    def steps_a(self):
        return self.spot.a - 1

    @staticmethod
    def scratch(a, b, rows, width):
        return [
            pltpu.VMEM((a * slots_of(b) * rows, width), bf16),
            pltpu.VMEM((slots_of(a) * rows, width), bf16),
            pltpu.SemaphoreType.DMA((a, b - 1, 2, SUM_PIECES)),
            pltpu.SemaphoreType.DMA((a, slots_of(b), SUM_PIECES)),
            pltpu.SemaphoreType.DMA((a - 1, 2, SUM_PIECES)),
            pltpu.SemaphoreType.DMA((slots_of(a), SUM_PIECES)),
        ]


def sum_kernel(a, b, rows, x_ref, out_ref, part, load, *scratch):
    spot = Spot(a, b)
    n = spot.n
    total = GroupSum(spot, part, rows, *scratch)

    def loading(A, B):
        at = pl.ds(pl.multiple_of((A * b + B) * rows, 16), rows)
        return pltpu.make_async_copy(x_ref.at[at], part.at[at], load.at[A * b + B])

    order = sorted(range(a), key=lambda c: (min(c, a - 1 - c), -c))
    for A in order:
        for B in range(b):
            loading(A, B).start()
    spot.greet()
    for A in order:
        for B in range(b):
            loading(A, B).wait()
            total.ready(A, B)
    total.along_b()
    total.flow([])
    total.a_line.end(out_ref)


def group_sum(x, dp_size, collective_id):
    a, b = group_sizes(dp_size)
    n = a * b
    rows, width = x.shape[0] // n, x.shape[1]
    return pl.pallas_call(
        functools.partial(sum_kernel, a, b, rows),
        out_shape=jax.ShapeDtypeStruct((rows, width), f32),
        in_specs=[pl.BlockSpec(memory_space=pl.ANY)],
        out_specs=pl.BlockSpec(memory_space=pltpu.VMEM),
        scratch_shapes=[pltpu.VMEM(x.shape, bf16), pltpu.SemaphoreType.DMA((n,))]
        + GroupSum.scratch(a, b, rows, width),
        compiler_params=pltpu.CompilerParams(
            collective_id=collective_id, has_side_effects=True, vmem_limit_bytes=40 << 20
        ),
    )(x)


LANES = 128
LOW_AT = 64


def mm(x, y, dims):
    return lax.dot_general(x, y, (dims, ((), ())), preferred_element_type=f32)


NN, NT, TN = ((1,), (0,)), ((1,), (1,)), ((0,), (0,))


def experts_kernel(
    a, b, rows, width,
    x_ref, grads_ref, picked_ref, router_ref, near_gate, near_up, near_down, far_gate, far_up, far_down,
    moe_ref, out_ref, o_near_gate, o_near_up, o_near_down, o_far_gate, o_far_up, o_far_down,
    xs, gs, weights, downs, lows, part, extras, stage, local, load, send, recv, stage_sem, store, *scratch,
):
    spot = Spot(a, b)
    n = spot.n
    gather = LineGather(spot, xs, rows, send, recv)
    total = GroupSum(spot, part, rows, *scratch)
    mine = pltpu.make_async_copy(
        x_ref, xs.at[pl.ds(pl.multiple_of(spot.block * rows, 16), rows)], local.at[0]
    )
    mine.start()
    sources = (near_gate, near_up, far_gate, far_up)
    arriving = [
        pltpu.make_async_copy(src, weights.at[k], local.at[1 + k]) for k, src in enumerate(sources)
    ] + [
        pltpu.make_async_copy(src, downs.at[k], local.at[5 + k])
        for k, src in enumerate((near_down, far_down))
    ]

    def grads_copy(i):
        at = pl.ds(gather.row0(i), rows)
        return pltpu.make_async_copy(grads_ref.at[at], gs.at[at], load.at[i])

    grads_copy(0).start()
    for c in arriving:
        c.start()
    for i in range(1, n):
        grads_copy(i).start()
    spot.greet()
    mine.wait()
    gather.forward(0)
    for c in arriving:
        c.wait()
    lane = lax.broadcasted_iota(jnp.int32, (rows, LANES), 1)
    near, far = spot.me, spot.me + 1 - 2 * spot.pair

    def block(i, _):
        at = pl.ds(gather.row0(i), rows)
        grads_copy(i).wait()
        x = xs[at, :]
        chosen = picked_ref[at, :] > 0
        logits = jnp.where(chosen, mm(x, router_ref[...], NN), masked_score)
        raised = jnp.where(chosen, jnp.exp(logits - jnp.max(logits, axis=1, keepdims=True)), 0.0)
        gates = raised / jnp.sum(raised, axis=1, keepdims=True)
        extra = jnp.zeros((rows, LANES), f32)
        for e, expert in enumerate((near, far)):
            if e == 1:

                @pl.when(i + 1 < n)
                def _():
                    gather.wait(i + 1)
                    gather.forward(i + 1)

            column = jnp.sum(jnp.where(lane == expert, gates, 0.0), axis=1, keepdims=True)
            x = xs[at, :]
            gate_act = mm(x, weights[2 * e], NN)
            up_act = mm(x, weights[2 * e + 1], NN)
            down_in = residual_scale * mm(gs[at, :], downs[e], NT)
            sigmoid_gate = jax.nn.sigmoid(gate_act)
            silu_gate = gate_act * sigmoid_gate
            hidden = silu_gate * up_act
            deriv = jnp.sum(hidden * down_in, axis=1, keepdims=True)
            high = deriv.astype(bf16).astype(f32)
            extra += jnp.where(lane == expert, high, 0.0)
            extra += jnp.where(lane == expert + LOW_AT, deriv - high, 0.0)
            down_in = down_in * column
            lows[3 * e, at, :] = (hidden * column).astype(bf16)
            lows[3 * e + 1, at, :] = (
                down_in * up_act * sigmoid_gate * (1.0 + gate_act * (1.0 - sigmoid_gate))
            ).astype(bf16)
            lows[3 * e + 2, at, :] = (down_in * silu_gate).astype(bf16)

        extras[at, :] = extra.astype(bf16)
        return 0

    lax.fori_loop(0, n, block, 0)

    def rows_of(A, B):
        return pl.ds(pl.multiple_of((A * b + B) * rows, 16), rows)

    def back_block(A, B):
        at = rows_of(A, B)
        back = mm(lows[1, at, :], weights[0], NT) + mm(lows[2, at, :], weights[1], NT)
        back += mm(lows[4, at, :], weights[2], NT) + mm(lows[5, at, :], weights[3], NT)
        part[at, pl.ds(0, width)] = back.astype(bf16)
        part[at, pl.ds(width, LANES)] = extras[at, :]
        total.ready(A, B)

    def back_others(i, _):
        A = total.order(i // (b - 1))
        B = by_distance(b, spot.B, 1 + i % (b - 1))
        back_block(A, B)
        return 0

    def back_own(i, _):
        back_block(total.order(i), spot.B)
        return 0

    def stage_copy(i):
        at = pl.ds(pl.multiple_of(i * rows, 16), rows)
        return pltpu.make_async_copy(stage.at[i % 2], moe_ref.at[at], stage_sem.at[i % 2])

    def moe_block(i, _):
        at = pl.ds(pl.multiple_of(i * rows, 16), rows)

        @pl.when(i >= 2)
        def _():
            stage_copy(i - 2).wait()

        stage[i % 2] = (mm(lows[0, at, :], downs[0], NN) + mm(lows[3, at, :], downs[1], NN)).astype(
            bf16
        )
        stage_copy(i).start()
        return 0

    lax.fori_loop(0, a * (b - 1), back_others, 0)
    lax.fori_loop(0, 2, back_own, 0)
    if b > 2:
        lax.fori_loop(2, a, back_own, 0)
    total.along_b()
    tile = 256

    def weight_grads(e):
        def wide(k, _):
            at = pl.ds(pl.multiple_of(k * tile, tile), tile)
            x = xs[:, at]
            weights[2 * e, at, :] = mm(x, lows[3 * e + 1], TN).astype(bf16)
            weights[2 * e + 1, at, :] = mm(x, lows[3 * e + 2], TN).astype(bf16)
            downs[e, :, at] = (residual_scale * mm(lows[3 * e], gs[:, at], TN)).astype(bf16)
            return 0

        lax.fori_loop(0, width // tile, wide, 0)
        outs = (o_near_gate, o_near_up, o_near_down) if e == 0 else (o_far_gate, o_far_up, o_far_down)
        copies = [
            pltpu.make_async_copy(weights.at[2 * e], outs[0], store.at[3 * e]),
            pltpu.make_async_copy(weights.at[2 * e + 1], outs[1], store.at[3 * e + 1]),
            pltpu.make_async_copy(downs.at[e], outs[2], store.at[3 * e + 2]),
        ]
        for c in copies:
            c.start()
        return copies

    stored = []

    def moe_all():
        lax.fori_loop(0, n, moe_block, 0)

    total.flow(
        [
            (lambda: lax.fori_loop(2, a, back_own, 0)) if b == 2 else (lambda: None),
            moe_all,
            lambda: stored.extend(weight_grads(1)),
            lambda: stored.extend(weight_grads(0)),
        ]
    )
    line = total.a_line
    line.end(out_ref)
    gather.finish()
    stage_copy(n - 2).wait()
    stage_copy(n - 1).wait()
    for c in stored:
        c.wait()


def experts_call(rows_low, grads, picked, router, near, far, dp_size, collective_id):
    a, b = group_sizes(dp_size)
    n = a * b
    rows, width = rows_low.shape
    units = near[0].shape[1]
    hbm, vmem = pl.BlockSpec(memory_space=pl.ANY), pl.BlockSpec(memory_space=pltpu.VMEM)
    outs = [
        jax.ShapeDtypeStruct((n * rows, width), bf16),
        jax.ShapeDtypeStruct((rows, width + LANES), f32),
    ] + [jax.ShapeDtypeStruct(x.shape, bf16) for x in near + far]
    return pl.pallas_call(
        functools.partial(experts_kernel, a, b, rows, width),
        out_shape=outs,
        in_specs=[hbm, hbm, vmem, vmem] + [hbm] * 6,
        out_specs=[hbm, vmem] + [hbm] * 6,
        scratch_shapes=[
            pltpu.VMEM((n * rows, width), bf16),
            pltpu.VMEM((n * rows, width), bf16),
            pltpu.VMEM((4, width, units), bf16),
            pltpu.VMEM((2, units, width), bf16),
            pltpu.VMEM((6, n * rows, units), bf16),
            pltpu.VMEM((n * rows, width + LANES), bf16),
            pltpu.VMEM((n * rows, LANES), bf16),
            pltpu.VMEM((2, rows, width), bf16),
            pltpu.SemaphoreType.DMA((7,)),
            pltpu.SemaphoreType.DMA((n,)),
            pltpu.SemaphoreType.DMA((n, 4, PIECES)),
            pltpu.SemaphoreType.DMA((n, PIECES)),
            pltpu.SemaphoreType.DMA((2,)),
            pltpu.SemaphoreType.DMA((6,)),
        ]
        + GroupSum.scratch(a, b, rows, width + LANES),
        compiler_params=pltpu.CompilerParams(
            collective_id=collective_id, has_side_effects=True, vmem_limit_bytes=60 << 20
        ),
    )(rows_low, grads, picked, router, *near, *far)


def reduce_schedule(steps, groups):
    sums = [("sum", s) for s in range(steps)]
    backs = [("back", s) for s in reversed(range(steps))]
    lines = [[(g,) + e for e in sums + backs] for g in range(groups)]
    if groups == 1:
        return lines[0]
    first, second = lines
    order = first[: steps - 1]
    first = first[steps - 1 :]
    while first or second:
        if second:
            order.append(second.pop(0))
        if first:
            order.append(first.pop(0))
    return order


def reduce_kernel(orders, groups, x_ref, small_ref, out_ref, small_out, acc, got, small_got, load, send, recv, small_send, small_recv):
    k = len(orders[0])
    nparts = len(orders)
    size = x_ref.shape[0] // nparts
    loads = []
    for j in range(nparts):
        c = pltpu.make_async_copy(x_ref.at[pl.ds(j * size, size)], acc.at[pl.ds(j * size, size)], load.at[j])
        c.start()
        loads.append(c)
    greet(sorted(orders[0]))
    small_out[...] = small_ref[...]
    copies, back, small_copies = {}, {}, []
    where = [j * size for j in range(nparts)]
    per_group = nparts // groups

    def sum_step(j, step):
        count = size >> (step + 1)
        mask = orders[j][step]
        _, bit = peer_of(mask)
        keep = pl.multiple_of(where[j] + bit * count, 16)
        give = pl.multiple_of(where[j] + (1 - bit) * count, 16)
        if step == 0:
            loads[j].wait()
        else:
            copies[j, step - 1].wait_recv()
            p0 = j * size + (size - (size >> (step - 1)))
            add_rows(acc, give, acc, give, got, p0 + pl.multiple_of((1 - bit) * count, 16), count, bf16)
        g0 = j * size + (size - (size >> step))
        c = remote(acc.at[pl.ds(give, count)], got.at[pl.ds(g0, count)], send.at[j, step], recv.at[j, step], mask)
        c.start()
        copies[j, step] = c
        if step > 0:
            add_rows(acc, keep, acc, keep, got, p0 + pl.multiple_of(bit * count, 16), count, bf16)
        where[j] = keep

    def back_step(j, step):
        count = size >> (step + 1)
        mask = orders[j][step]
        _, bit = peer_of(mask)
        if step == k - 1:
            copies[j, step].wait_recv()
            p0 = j * size + (size - (size >> step))
            add_rows(out_ref, where[j], acc, where[j], got, p0, count, bf16)
        else:
            back[j, step + 1].wait_recv()
        here = where[j]
        c = remote(out_ref.at[pl.ds(here, count)], out_ref.at[pl.ds(here, count)], send.at[j, k + step], recv.at[j, k + step], mask)
        c.start()
        back[j, step] = c
        where[j] = pl.multiple_of(here - bit * count, 16)

    def small_step(step):
        if step > 0:
            small_copies[-1].wait_send()
            small_copies[-1].wait_recv()
            small_out[...] += small_got[step - 1]
        if step < k:
            c = remote(small_out, small_got.at[step], small_send.at[step], small_recv.at[step], orders[0][step])
            c.start()
            small_copies.append(c)

    small_done = 0
    for g, kind, step in reduce_schedule(k, groups):
        for j in range(g * per_group, (g + 1) * per_group):
            (sum_step if kind == "sum" else back_step)(j, step)
        if g == groups - 1 and small_done <= k:
            small_step(small_done)
            small_done += 1
    for j in range(nparts):
        back[j, 0].wait_recv()
    for c in copies.values():
        c.wait_send()
    for c in back.values():
        c.wait_send()


def all_reduce(x, small, masks, collective_id):
    inner, last = masks[:-1], masks[-1:]
    groups = 2 if x.shape[0] % (6 * 16 * 2 ** len(masks)) == 0 else 1
    nparts = 3 * groups
    orders = [rotated(inner, j) + last for j in range(nparts)]
    k = len(masks)
    vm = pl.BlockSpec(memory_space=pltpu.VMEM)
    return pl.pallas_call(
        functools.partial(reduce_kernel, orders, groups),
        out_shape=[jax.ShapeDtypeStruct(x.shape, bf16), jax.ShapeDtypeStruct(small.shape, f32)],
        in_specs=[pl.BlockSpec(memory_space=pl.ANY), vm],
        out_specs=[vm, vm],
        scratch_shapes=[
            pltpu.VMEM(x.shape, bf16),
            pltpu.VMEM(x.shape, bf16),
            pltpu.VMEM((k,) + small.shape, f32),
            pltpu.SemaphoreType.DMA((nparts,)),
            pltpu.SemaphoreType.DMA((nparts, 2 * k)),
            pltpu.SemaphoreType.DMA((nparts, 2 * k)),
            pltpu.SemaphoreType.DMA((k,)),
            pltpu.SemaphoreType.DMA((k,)),
        ],
        compiler_params=pltpu.CompilerParams(
            collective_id=collective_id, has_side_effects=True, vmem_limit_bytes=40 << 20
        ),
    )(x, small)


def place_kernel(dims, *refs):
    n = len(dims)
    mine, other, outs = refs[:n], refs[n : 2 * n], refs[2 * n : 3 * n]
    bufs, sems, out_sems = refs[3 * n : 4 * n], refs[4 * n], refs[4 * n + 1]
    me = lax.axis_index("tensor")

    def copy(i, which, src):
        size = src.shape[dims[i]]
        at = pl.multiple_of((me + which - 2 * which * me) * size, size)
        window = (slice(None),) * dims[i] + (pl.ds(at, size),)
        return pltpu.make_async_copy(src, bufs[i].at[window], sems.at[i, which])

    copies = [[copy(i, w, src) for w, src in enumerate((mine[i], other[i]))] for i in range(n)]
    for pair in copies:
        for c in pair:
            c.start()
    back = []
    for i, pair in enumerate(copies):
        for c in pair:
            c.wait()
        c = pltpu.make_async_copy(bufs[i], outs[i], out_sems.at[i])
        c.start()
        back.append(c)
    for c in back:
        c.wait()


def place(mine, other, dims):
    n = len(dims)
    shapes = [x.shape[:d] + (2 * x.shape[d],) + x.shape[d + 1 :] for x, d in zip(mine, dims)]
    return pl.pallas_call(
        functools.partial(place_kernel, dims),
        out_shape=[jax.ShapeDtypeStruct(s, x.dtype) for x, s in zip(mine, shapes)],
        in_specs=[pl.BlockSpec(memory_space=pl.ANY)] * (2 * n),
        out_specs=[pl.BlockSpec(memory_space=pl.ANY)] * n,
        scratch_shapes=[pltpu.VMEM(s, x.dtype) for x, s in zip(mine, shapes)]
        + [pltpu.SemaphoreType.DMA((n, 2)), pltpu.SemaphoreType.DMA((n,))],
        compiler_params=pltpu.CompilerParams(vmem_limit_bytes=24 << 20),
    )(*mine, *other)


def dot(a, b, spec):
    return jnp.einsum(spec, a, b, preferred_element_type=f32)


def per_device(
    hidden_in,
    attn_gain,
    w_query,
    key_weight,
    value_weight,
    w_output,
    moe_gain,
    w_router,
    w_gate,
    w_up,
    w_down,
    expert_ids,
    segment_ids,
    out_grad,
):
    tokens_here, model_width = hidden_in.shape
    head_size = HEAD_DIM
    dp_size = lax.axis_size("dp")
    tensor_size = lax.axis_size("tensor")
    experts = dp_size
    tensor_index = lax.axis_index("tensor")
    masks = bit_masks(dp_size)
    tensor_masks = bit_masks(tensor_size)
    tensor_down = tensor_masks[::-1]
    rows_here = tokens_here // tensor_size
    groups = [list(range(pair, dp_size, 2)) for pair in range(2)]

    def my_rows(x):
        return lax.dynamic_slice_in_dim(x, tensor_index * rows_here, rows_here, 0)

    block = w_gate.shape[2] // tensor_size

    def my_units(x, dim):
        return lax.dynamic_slice_in_dim(x, tensor_index * block, block, dim)

    def relative_gather(x, dim):
        for mask in tensor_masks:
            x = jnp.concatenate([x, swap(x, "tensor", mask)], dim)
        return x

    def relative_scatter(x, dim):
        for mask in reversed(tensor_masks):
            half = x.shape[dim] // 2
            keep = lax.slice_in_dim(x, 0, half, axis=dim)
            give = lax.slice_in_dim(x, half, 2 * half, axis=dim)
            x = keep.astype(f32) + swap(give.astype(bf16), "tensor", mask).astype(f32)
        return x

    far_set = [
        relative_gather(swap(my_units(w_gate[0], 1), "dp", 1), 1),
        relative_gather(swap(my_units(w_up[0], 1), "dp", 1), 1),
        relative_gather(swap(my_units(w_down[0], 0), "dp", 1), 0),
    ]
    grad_mine = my_rows(out_grad)
    grads = lax.all_gather(grad_mine, "dp", axis=0, tiled=True, axis_index_groups=groups)
    ids = lax.all_gather(
        my_rows(expert_ids), "dp", axis=0, tiled=True, axis_index_groups=groups
    )
    lanes = jnp.arange(LANES, dtype=jnp.int32)
    picked = jnp.any(ids[:, :, None] == lanes[None, None, :], axis=1).astype(bf16)
    router_wide = jnp.pad(w_router, ((0, 0), (0, LANES - experts)))

    inputs = hidden_in.astype(f32)
    scale_in = lax.rsqrt(jnp.mean(inputs * inputs, axis=-1, keepdims=True) + epsilon)
    normed_low = (inputs * scale_in * attn_gain).astype(bf16)
    segment = segment_ids[0]
    tables = rope_tables(segment, head_size)
    heads_flat, query_heads, key_heads, value_heads, log_sums = attend_forward(
        normed_low, segment, tables, w_query, key_weight, value_weight, head_size
    )
    attn_part = jnp.dot(heads_flat, w_output, preferred_element_type=f32)
    attn_total = scatter_sum(attn_part, "tensor", tensor_down, f32)

    inputs_mine = my_rows(hidden_in).astype(f32)
    scale_in_mine = my_rows(scale_in)
    middle = inputs_mine + residual_scale * attn_total
    scale_mid = lax.rsqrt(jnp.mean(middle * middle, axis=-1, keepdims=True) + epsilon)
    routed_low = (middle * scale_mid * moe_gain).astype(bf16)

    near_set = [w_gate[0], w_up[0], w_down[0]]
    moe_part, back, *expert_parts = experts_call(
        routed_low, grads, picked, router_wide, near_set, far_set, dp_size, 0
    )
    moe_total = group_sum(moe_part, dp_size, 1)

    dims = (1, 1, 0)
    near_mine = [
        scatter_sum(x, "tensor", tensor_down, bf16, d) for x, d in zip(expert_parts[:3], dims)
    ]
    returning = [
        swap(relative_scatter(x, d).astype(bf16), "dp", 1) for x, d in zip(expert_parts[3:], dims)
    ]

    logits = dot(routed_low, w_router, "td,de->te")
    chosen = jnp.any(
        my_rows(expert_ids)[:, :, None] == jnp.arange(experts, dtype=jnp.int32)[None, None, :],
        axis=1,
    )
    logits = jnp.where(chosen, logits, masked_score)
    raised = jnp.where(chosen, jnp.exp(logits - jnp.max(logits, axis=1, keepdims=True)), 0.0)
    gate_weights = raised / jnp.sum(raised, axis=1, keepdims=True)
    routed_grad = back[:, :model_width]
    gate_deriv = (
        back[:, model_width : model_width + experts]
        + back[:, model_width + LOW_AT : model_width + LOW_AT + experts]
    )
    chosen_grad = gate_weights * (
        gate_deriv - jnp.sum(gate_weights * gate_deriv, axis=1, keepdims=True)
    )
    logit_grad = chosen_grad.astype(bf16)
    router_part = dot(logit_grad, routed_low, "te,td->ed")
    routed_grad = routed_grad + dot(logit_grad, w_router, "te,de->td")
    gained = moe_gain * routed_grad
    moe_gain_part = jnp.sum(routed_grad * middle * scale_mid, axis=0)
    grad_top = grad_mine.astype(f32)
    middle_grad = (
        grad_top
        + scale_mid * gained
        - middle
        * (scale_mid * scale_mid * scale_mid)
        * jnp.mean(middle * gained, axis=-1, keepdims=True)
    )
    branch_low = gather_blocks(
        (residual_scale * middle_grad).astype(bf16), "tensor", tensor_down
    )
    heads_width = heads_flat.shape[1]
    w_output_part = [
        dot(heads_flat, branch_low[:, i : i + heads_width], "tc,td->cd")
        for i in range(0, model_width, heads_width)
    ]
    heads_grad = dot(branch_low, w_output, "td,cd->tc").astype(bf16)
    query_low, key_low, value_low = attend_backward(
        query_heads, key_heads, value_heads, log_sums, heads_grad, segment, tables
    )
    width_q, width_k = query_low.shape[1], key_low.shape[1]
    qkv_low = jnp.concatenate([query_low, key_low, value_low], axis=1)
    qkv_width = qkv_low.shape[1]
    attention_part = jnp.concatenate(
        [dot(normed_low, qkv_low, "td,tc->dc"), jnp.concatenate(w_output_part, 0)], 1
    ).astype(bf16)
    qkv_weight = jnp.concatenate([w_query, key_weight, value_weight], axis=1)
    normed_part = dot(qkv_low, qkv_weight, "tc,dc->td")
    normed_grad = scatter_sum(normed_part, "tensor", tensor_down, f32)
    gained_in = attn_gain * normed_grad
    attn_gain_part = jnp.sum(normed_grad * inputs_mine * scale_in_mine, axis=0)
    input_mine = (
        middle_grad
        + scale_in_mine * gained_in
        - inputs_mine
        * (scale_in_mine * scale_in_mine * scale_in_mine)
        * jnp.mean(inputs_mine * gained_in, axis=-1, keepdims=True)
    )
    input_grad = gather_blocks(input_mine, "tensor", tensor_down)
    block_mine = (middle + residual_scale * moe_total).astype(bf16)
    block_out = gather_blocks(block_mine, "tensor", tensor_down)

    small = jnp.concatenate([router_part, moe_gain_part[None], attn_gain_part[None]], 0)
    small = jnp.pad(small, ((0, -small.shape[0] % 8), (0, 0)))
    for mask in tensor_masks:
        small = small + swap(small, "tensor", mask)
    attention_grad, small = all_reduce(attention_part, small, masks, 2)
    attention_grad, returning = lax.optimization_barrier((attention_grad, returning))
    expert_mine = [mine + away.astype(f32) for mine, away in zip(near_mine, returning)]
    if tensor_size == 2:
        expert_grads = place(expert_mine, [swap(x, "tensor", 1) for x in expert_mine], dims)
    else:
        expert_grads = [
            gather_blocks(x, "tensor", tensor_down, dim) for x, dim in zip(expert_mine, dims)
        ]
    attention_grad = attention_grad.astype(f32)
    w_output_grad = jnp.concatenate(
        [
            attention_grad[i : i + heads_width, qkv_width:]
            for i in range(0, model_width, heads_width)
        ],
        1,
    )
    return (
        block_out,
        input_grad,
        small[experts + 1],
        attention_grad[:, :width_q],
        attention_grad[:, width_q : width_q + width_k],
        attention_grad[:, width_q + width_k : qkv_width],
        w_output_grad,
        small[experts],
        small[:experts].T,
        expert_grads[0][None],
        expert_grads[1][None],
        expert_grads[2][None],
    )


def solution(mesh):
    placed = (
        P("dp", None),
        P(),
        P(None, "tensor"),
        P(None, "tensor"),
        P(None, "tensor"),
        P("tensor", None),
        P(),
        P(),
        P("dp", None, None),
        P("dp", None, None),
        P("dp", None, None),
        P("dp", None),
        P("dp", None),
        P("dp", None),
    )
    return jax.shard_map(
        per_device,
        mesh=mesh,
        in_specs=placed,
        out_specs=(
            P("dp", None),
            P("dp", None),
            P(),
            P(None, "tensor"),
            P(None, "tensor"),
            P(None, "tensor"),
            P("tensor", None),
            P(),
            P(),
            P("dp", None, None),
            P("dp", None, None),
            P("dp", None, None),
        ),
        check_vma=False,
    )
```

```python
import functools

import jax
import jax.numpy as jnp
from jax import lax
from jax.experimental import pallas as pl
from jax.experimental.pallas import tpu as pltpu
from jax.sharding import PartitionSpec as P

HEAD_DIM = 64

bf16 = jnp.bfloat16
f32 = jnp.float32
MESH = pl.DeviceIdType.MESH
epsilon = 1e-06
residual_scale = 0.22
attn_scale = 0.015625
rope_base = 10000.0
masked_score = -1e30


def positions_of(segment):
    position_index = jnp.arange(segment.shape[0], dtype=jnp.int32)
    earlier = jnp.concatenate([segment[:1] - 1, segment[:-1]])
    starts = lax.cummax(jnp.where(segment != earlier, position_index, 0), axis=0)
    return position_index - starts


def rope_tables(segment, head_size):
    position = positions_of(segment).astype(f32)
    frequency = rope_base ** (-jnp.arange(head_size // 2, dtype=f32) * 2.0 / head_size)
    angle = position[:, None] * frequency[None, :]
    return (jnp.cos(angle)[:, None, :], jnp.sin(angle)[:, None, :])


def apply_rotation(heads_in, cosine_table, sine_values):
    middle_index = heads_in.shape[-1] // 2
    first_half = heads_in[..., :middle_index]
    second_half = heads_in[..., middle_index:]
    return jnp.concatenate(
        [
            first_half * cosine_table - second_half * sine_values,
            second_half * cosine_table + first_half * sine_values,
        ],
        axis=-1,
    )


def block_scores(query_heads, key_heads, segment):
    kv_count = key_heads.shape[1]
    length = query_heads.shape[0]
    grouped = query_heads.reshape(length, kv_count, -1, query_heads.shape[2])
    raw_scores = (
        jnp.einsum("qhgd,khd->hgqk", grouped, key_heads, preferred_element_type=f32) * attn_scale
    )
    index = jnp.arange(length, dtype=jnp.int32)
    allowed = (index[:, None] >= index[None, :]) & (segment[:, None] == segment[None, :])
    return (jnp.where(allowed, raw_scores, masked_score), grouped)


def attend_forward(normed, segment, tables, w_query, key_weight, value_weight, head_size):
    length = normed.shape[0]

    def heads(weight):
        return jnp.dot(normed, weight, preferred_element_type=f32).reshape(length, -1, head_size)

    query_heads = apply_rotation(heads(w_query), *tables).astype(bf16)
    key_heads = apply_rotation(heads(key_weight), *tables).astype(bf16)
    value_heads = heads(value_weight).astype(bf16)
    scores, _ = block_scores(query_heads, key_heads, segment)
    largest = jnp.max(scores, axis=-1, keepdims=True)
    weights_raw = jnp.exp(scores - largest)
    totals = jnp.sum(weights_raw, axis=-1, keepdims=True)
    probs_low = (weights_raw / totals).astype(bf16)
    head_out = jnp.einsum("hgqk,khd->qhgd", probs_low, value_heads, preferred_element_type=f32)
    return (
        head_out.reshape(length, -1).astype(bf16),
        query_heads,
        key_heads,
        value_heads,
        (largest + jnp.log(totals))[..., 0],
    )


def attend_backward(query_heads, key_heads, value_heads, log_sums, heads_grad, segment, tables):
    length = query_heads.shape[0]
    cosine_table, sine_values = tables
    scores, grouped = block_scores(query_heads, key_heads, segment)
    probability = jnp.exp(scores - log_sums[..., None])
    probs_low = probability.astype(bf16)
    grad_grouped = heads_grad.reshape(grouped.shape)
    prob_grad = jnp.einsum(
        "qhgd,khd->hgqk", grad_grouped, value_heads, preferred_element_type=f32
    )
    weighted = jnp.sum(probability * prob_grad, axis=-1, keepdims=True)
    score_low = (probability * (prob_grad - weighted)).astype(bf16)
    query_part = (
        jnp.einsum("hgqk,khd->qhgd", score_low, key_heads, preferred_element_type=f32) * attn_scale
    ).reshape(query_heads.shape)
    key_sum = (
        jnp.einsum("hgqk,qhgd->khd", score_low, grouped, preferred_element_type=f32) * attn_scale
    )
    value_sum = jnp.einsum(
        "hgqk,qhgd->khd", probs_low, grad_grouped, preferred_element_type=f32
    )
    query_low = apply_rotation(query_part, cosine_table, -sine_values).astype(bf16)
    key_low = apply_rotation(key_sum, cosine_table, -sine_values).astype(bf16)
    return (
        query_low.reshape(length, -1),
        key_low.reshape(length, -1),
        value_sum.astype(bf16).reshape(length, -1),
    )


def bit_masks(size):
    masks = []
    while size > 1:
        size //= 2
        masks.append(size)
    return masks[::-1]


def swap(x, axis, mask):
    return lax.ppermute(x, axis, [(i, i ^ mask) for i in range(lax.axis_size(axis))])


def bit_of(axis, mask):
    return (lax.axis_index(axis) // mask) % 2


def halves_by_bit(x, axis, mask, dim=0):
    half = x.shape[dim] // 2
    bit = bit_of(axis, mask)
    mine = lax.dynamic_slice_in_dim(x, bit * half, half, dim)
    other = lax.dynamic_slice_in_dim(x, (1 - bit) * half, half, dim)
    return mine, other


def join_by_bit(mine, other, axis, mask, dim=0):
    return jnp.where(
        bit_of(axis, mask) == 0,
        jnp.concatenate([mine, other], dim),
        jnp.concatenate([other, mine], dim),
    )


def scatter_sum(x, axis, masks, kind, dim=0):
    x = x.astype(f32)
    for mask in masks:
        mine, other = halves_by_bit(x, axis, mask, dim)
        x = mine + swap(other.astype(kind), axis, mask).astype(f32)
    return x


def gather_blocks(x, axis, masks, dim=0):
    for mask in reversed(masks):
        x = join_by_bit(x, swap(x, axis, mask), axis, mask, dim)
    return x


def rotated(masks, j):
    j = j % len(masks)
    return masks[j:] + masks[:j]


def peer_of(mask):
    me = lax.axis_index("dp")
    bit = (me // mask) % 2
    return me + mask * (1 - 2 * bit), bit


def greet(masks):
    barrier = pltpu.get_barrier_semaphore()
    for mask in masks:
        pl.semaphore_signal(
            barrier, inc=1, device_id={"dp": peer_of(mask)[0]}, device_id_type=MESH
        )
    pl.semaphore_wait(barrier, len(masks))


def remote(src, dst, send, recv, mask):
    return remote_to(src, dst, send, recv, peer_of(mask)[0])


def add_rows(dst, dst0, a, a0, b, b0, rows, out_dtype):
    step = 16

    def body(i, _):
        r = pl.multiple_of(i * step, step)
        x = a[pl.ds(a0 + r, step), :].astype(f32) + b[pl.ds(b0 + r, step), :].astype(f32)
        dst[pl.ds(dst0 + r, step), :] = x.astype(out_dtype)
        return 0

    lax.fori_loop(0, rows // step, body, 0)


def group_sizes(dp_size):
    a = 4
    return a, dp_size // (2 * a)


class Spot:
    def __init__(self, a, b):
        me = lax.axis_index("dp")
        self.a, self.b = a, b
        self.n = a * b
        self.me = me
        self.A = me // (2 * b)
        self.B = (me // 2) % b
        self.block = me // 2
        self.pair = me % 2
        self.devices = (me + 2 * b, me - 2 * b, me + 2, me - 2)
        self.exists = (self.A < a - 1, self.A > 0, self.B < b - 1, self.B > 0)
        self.some = me + 2 * (1 - 2 * (self.B % 2))

    def greet(self):
        barrier = pltpu.get_barrier_semaphore()
        for device, there in zip(self.devices, self.exists):

            @pl.when(there)
            def _(device=device):
                pl.semaphore_signal(
                    barrier, inc=1, device_id={"dp": device}, device_id_type=MESH
                )

        a, b = self.a, self.b
        ups = 2 - (self.A + 1) // a - (self.B + 1) // b
        downs = (self.A + a - 1) // a + (self.B + b - 1) // b
        pl.semaphore_wait(barrier, ups + downs)


def is_at(x, value):
    return 1 // (1 + (x - value) * (x - value))


def by_distance(size, place, k):
    found = 0
    for p in range(size):
        order = sorted(range(size), key=lambda q: (abs(q - p), q))
        for j, q in enumerate(order):
            if q > 0:
                found = found + q * is_at(place, p) * is_at(k, j)
    return found


def visit_order(a, b):
    pairs = [(k, l) for k in range(a) for l in range(b)]
    return sorted(pairs, key=lambda kl: kl[0] + (2 * kl[1] + 0.5 if kl[1] else 0))


def remote_to(src, dst, send, recv, device):
    return pltpu.make_async_remote_copy(
        src_ref=src,
        dst_ref=dst,
        send_sem=send,
        recv_sem=recv,
        device_id={"dp": device},
        device_id_type=MESH,
    )


PIECES = 2
SUM_PIECES = 4


class LineGather:
    def __init__(self, spot, buf, rows, send, recv):
        self.spot, self.buf, self.rows, self.send, self.recv = spot, buf, rows, send, recv

    def coords(self, i):
        s = self.spot
        visits = visit_order(s.a, s.b)
        k = sum(v[0] * is_at(i, j) for j, v in enumerate(visits) if v[0])
        l = sum(v[1] * is_at(i, j) for j, v in enumerate(visits) if v[1])
        return by_distance(s.a, s.A, k), by_distance(s.b, s.B, l)

    def row0(self, i):
        A, B = self.coords(i)
        return pl.multiple_of((A * self.spot.b + B) * self.rows, 16)

    def copies(self, block, way, device):
        size = self.rows // PIECES
        return [
            remote_to(there, there, self.send.at[block, way, p], self.recv.at[block, p], device)
            for p in range(PIECES)
            for there in [self.buf.at[pl.ds(pl.multiple_of(block * self.rows + p * size, 16), size)]]
        ]

    def each_way(self, i, act):
        s = self.spot
        A, B = self.coords(i)
        block = A * s.b + B
        same = B == s.B
        conditions = (
            same & (A <= s.A) & s.exists[0],
            same & (A >= s.A) & s.exists[1],
            (B <= s.B) & s.exists[2],
            (B >= s.B) & s.exists[3],
        )
        for way, (condition, device) in enumerate(zip(conditions, s.devices)):

            @pl.when(condition)
            def _(way=way, device=device):
                for c in self.copies(block, way, device):
                    act(c)

    def wait(self, i):
        A, B = self.coords(i)
        for c in self.copies(A * self.spot.b + B, 0, self.spot.some):
            c.wait_recv()

    def forward(self, i):
        self.each_way(i, lambda c: c.start())

    def finish(self):
        def one(i, _):
            self.each_way(i, lambda c: c.wait_send())
            return 0

        lax.fori_loop(0, self.spot.n, one, 0)


def add_into(dst, d0, src, s0, rows, step=16):
    def body(i, _):
        r = pl.multiple_of(i * step, step)
        total = dst[pl.ds(d0 + r, step), :].astype(f32) + src[pl.ds(s0 + r, step), :].astype(f32)
        dst[pl.ds(d0 + r, step), :] = total.astype(dst.dtype)
        return 0

    lax.fori_loop(0, rows // step, body, 0)


class LineSum:
    def __init__(self, size, place, up, down, part, row_of, rows, got, send, recv, some):
        self.size, self.place, self.up, self.down = size, place, up, down
        self.part, self.row_of, self.rows, self.got = part, row_of, rows, got
        self.send, self.recv, self.some = send, recv, some

    def up_slot(self, place, c):
        return c - place

    def down_slot(self, place, c):
        return c + (self.size - place) * ((place + self.size - 1) // self.size)

    def copies(self, c, slot, send, device):
        size = self.rows // SUM_PIECES
        return [
            remote_to(
                self.part.at[pl.ds(pl.multiple_of(self.row_of(c) + p * size, 16), size)],
                self.got.at[pl.ds(pl.multiple_of(slot * self.rows + p * size, 16), size)],
                send.at[p],
                self.recv.at[slot, p],
                device,
            )
            for p in range(SUM_PIECES)
        ]

    def take(self, c, slot, p, dst=None, d0=None):
        if dst is None:
            dst, d0 = self.part, self.row_of(c)
        size = self.rows // SUM_PIECES
        self.copies(c, slot, self.send.at[0, 0], self.some)[p].wait_recv()
        from_row = pl.multiple_of(slot * self.rows + p * size, 16)
        add_into(dst, d0 + p * size, self.got, from_row, size)

    def up_copies(self, k):
        c = self.size - 1 - k
        return self.copies(c, self.up_slot(self.place + 1, c), self.send.at[k, 0], self.up)

    def down_copies(self, k):
        return self.copies(k, self.down_slot(self.place - 1, k), self.send.at[k, 1], self.down)

    def step_up(self, k):
        c = self.size - 1 - k

        @pl.when(c > self.place)
        def _():
            for p, copy in enumerate(self.up_copies(k)):

                @pl.when(self.place > 0)
                def _(p=p):
                    self.take(c, self.up_slot(self.place, c), p)

                copy.start()

    def step_down(self, k):
        @pl.when(k < self.place)
        def _():
            for p, copy in enumerate(self.down_copies(k)):

                @pl.when(self.place < self.size - 1)
                def _(p=p):
                    self.take(k, self.down_slot(self.place, k), p)

                copy.start()

    def step(self, k):
        self.step_up(k)
        self.step_down(k)

    def end(self, out=None):
        p = self.place
        d0 = None
        if out is not None:
            out[...] = self.part[pl.ds(self.row_of(p), self.rows), :].astype(out.dtype)
            d0 = 0

        @pl.when(p > 0)
        def _():
            for j in range(SUM_PIECES):
                self.take(p, self.up_slot(p, p), j, out, d0)

        @pl.when(p < self.size - 1)
        def _():
            for j in range(SUM_PIECES):
                self.take(p, self.down_slot(p, p), j, out, d0)

        for k in range(self.size - 1):

            @pl.when(self.size - 1 - k > p)
            def _(k=k):
                for c in self.up_copies(k):
                    c.wait_send()

            @pl.when(k < p)
            def _(k=k):
                for c in self.down_copies(k):
                    c.wait_send()


def slots_of(size):
    return 1 if size == 2 else size + 1


class GroupSum:
    def __init__(self, spot, part, rows, got_b, got_a, send_b, recv_b, send_a, recv_a):
        self.spot, self.part, self.rows = spot, part, rows
        a, b = spot.a, spot.b
        slots_b = slots_of(b)

        def b_line(A):
            return LineSum(
                b, spot.B, spot.devices[2], spot.devices[3], part,
                lambda B: pl.multiple_of((A * b + B) * rows, 16), rows,
                got_b.at[pl.ds(pl.multiple_of(A * slots_b * rows, 16), slots_b * rows)],
                send_b.at[A], recv_b.at[A], spot.some,
            )

        self.b_line = b_line
        self.a_line = LineSum(
            a, spot.A, spot.devices[0], spot.devices[1], part,
            lambda A: pl.multiple_of((A * b + spot.B) * rows, 16), rows,
            got_a, send_a, recv_a, spot.some,
        )

    def ready(self, A, B):
        if self.spot.b == 2:
            line = self.b_line(A)

            @pl.when(B != self.spot.B)
            def _():
                line.step(0)

    def along_b(self):
        if self.spot.b > 2:

            def one(A, _):
                for k in range(self.spot.b - 1):
                    self.b_line(A).step(k)
                return 0

            lax.fori_loop(0, self.spot.a, one, 0)

    def flow(self, fills):
        a, line = self.spot.a, self.a_line
        fills = list(fills)

        def fill():
            if fills:
                fills.pop(0)()

        for k in range(a - 1):
            if 2 * k < a:
                self.b_line(a - 1 - k).end()
            line.step_up(k)
            fill()
            if 2 * k < a and a - 1 - k != k:
                self.b_line(k).end()
            line.step_down(k)
            fill()
        while fills:
            fill()

    def order(self, j):
        a = self.spot.a
        places = sorted(range(a), key=lambda c: (min(c, a - 1 - c), -c))
        return sum(c * is_at(j, i) for i, c in enumerate(places) if c)

    def steps_a(self):
        return self.spot.a - 1

    @staticmethod
    def scratch(a, b, rows, width):
        return [
            pltpu.VMEM((a * slots_of(b) * rows, width), bf16),
            pltpu.VMEM((slots_of(a) * rows, width), bf16),
            pltpu.SemaphoreType.DMA((a, b - 1, 2, SUM_PIECES)),
            pltpu.SemaphoreType.DMA((a, slots_of(b), SUM_PIECES)),
            pltpu.SemaphoreType.DMA((a - 1, 2, SUM_PIECES)),
            pltpu.SemaphoreType.DMA((slots_of(a), SUM_PIECES)),
        ]


LANES = 128
LOW_AT = 64


def mm(x, y, dims):
    return lax.dot_general(x, y, (dims, ((), ())), preferred_element_type=f32)


NN, NT, TN = ((1,), (0,)), ((1,), (1,)), ((0,), (0,))


def experts_kernel(
    a, b, rows, width,
    x_ref, grads_ref, router_ref, near_gate, near_up, near_down, far_gate, far_up, far_down,
    moe_ref, out_ref, o_near_gate, o_near_up, o_near_down, o_far_gate, o_far_up, o_far_down,
    xs, gs, weights, downs, lows, part, extras, stage, local, load, send, recv, stage_sem, store, *scratch,
):
    spot = Spot(a, b)
    n = spot.n
    gather = LineGather(spot, xs, rows, send, recv)
    total = GroupSum(spot, part, rows, *scratch)
    mine = pltpu.make_async_copy(
        x_ref, xs.at[pl.ds(pl.multiple_of(spot.block * rows, 16), rows)], local.at[0]
    )
    mine.start()
    sources = (near_gate, near_up, far_gate, far_up)
    arriving = [
        pltpu.make_async_copy(src, weights.at[k], local.at[1 + k]) for k, src in enumerate(sources)
    ] + [
        pltpu.make_async_copy(src, downs.at[k], local.at[5 + k])
        for k, src in enumerate((near_down, far_down))
    ]

    def grads_copy(i):
        at = pl.ds(gather.row0(i), rows)
        return pltpu.make_async_copy(grads_ref.at[at], gs.at[at], load.at[i])

    grads_copy(0).start()
    for c in arriving:
        c.start()
    for i in range(1, n):
        grads_copy(i).start()
    spot.greet()
    mine.wait()
    gather.forward(0)
    for c in arriving:
        c.wait()
    lane = lax.broadcasted_iota(jnp.int32, (rows, LANES), 1)
    near, far = spot.me, spot.me + 1 - 2 * spot.pair

    def block(i, _):
        at = pl.ds(gather.row0(i), rows)
        grads_copy(i).wait()
        x = xs[at, :]
        chosen = gs[at, pl.ds(width, LANES)] > 0
        logits = jnp.where(chosen, mm(x, router_ref[...], NN), masked_score)
        raised = jnp.where(chosen, jnp.exp(logits - jnp.max(logits, axis=1, keepdims=True)), 0.0)
        gates = raised / jnp.sum(raised, axis=1, keepdims=True)
        extra = jnp.zeros((rows, LANES), f32)
        for e, expert in enumerate((near, far)):
            if e == 1:

                @pl.when(i + 1 < n)
                def _():
                    gather.wait(i + 1)
                    gather.forward(i + 1)

            column = jnp.sum(jnp.where(lane == expert, gates, 0.0), axis=1, keepdims=True)
            x = xs[at, :]
            gate_act = mm(x, weights[2 * e], NN)
            up_act = mm(x, weights[2 * e + 1], NN)
            down_in = residual_scale * mm(gs[at, pl.ds(0, width)], downs[e], NT)
            sigmoid_gate = jax.nn.sigmoid(gate_act)
            silu_gate = gate_act * sigmoid_gate
            hidden = silu_gate * up_act
            deriv = jnp.sum(hidden * down_in, axis=1, keepdims=True)
            high = deriv.astype(bf16).astype(f32)
            extra += jnp.where(lane == expert, high, 0.0)
            extra += jnp.where(lane == expert + LOW_AT, deriv - high, 0.0)
            down_in = down_in * column
            lows[3 * e, at, :] = (hidden * column).astype(bf16)
            lows[3 * e + 1, at, :] = (
                down_in * up_act * sigmoid_gate * (1.0 + gate_act * (1.0 - sigmoid_gate))
            ).astype(bf16)
            lows[3 * e + 2, at, :] = (down_in * silu_gate).astype(bf16)

        extras[at, :] = extra.astype(bf16)
        return 0

    lax.fori_loop(0, n, block, 0)

    def rows_of(A, B):
        return pl.ds(pl.multiple_of((A * b + B) * rows, 16), rows)

    def back_block(A, B):
        at = rows_of(A, B)
        back = mm(lows[1, at, :], weights[0], NT) + mm(lows[2, at, :], weights[1], NT)
        back += mm(lows[4, at, :], weights[2], NT) + mm(lows[5, at, :], weights[3], NT)
        part[at, pl.ds(0, width)] = back.astype(bf16)
        part[at, pl.ds(width, LANES)] = extras[at, :]
        total.ready(A, B)

    def back_others(i, _):
        A = total.order(i // (b - 1))
        B = by_distance(b, spot.B, 1 + i % (b - 1))
        back_block(A, B)
        return 0

    def back_own(i, _):
        back_block(total.order(i), spot.B)
        return 0

    def stage_copy(i):
        at = pl.ds(pl.multiple_of(i * rows, 16), rows)
        return pltpu.make_async_copy(stage.at[i % 2], moe_ref.at[at], stage_sem.at[i % 2])

    def moe_block(i, _):
        at = pl.ds(pl.multiple_of(i * rows, 16), rows)

        @pl.when(i >= 2)
        def _():
            stage_copy(i - 2).wait()

        stage[i % 2] = (mm(lows[0, at, :], downs[0], NN) + mm(lows[3, at, :], downs[1], NN)).astype(
            bf16
        )
        stage_copy(i).start()
        return 0

    lax.fori_loop(0, a * (b - 1), back_others, 0)
    lax.fori_loop(0, 2, back_own, 0)
    if b > 2:
        lax.fori_loop(2, a, back_own, 0)
    total.along_b()
    tile = 256

    def weight_grads(e):
        def wide(k, _):
            at = pl.ds(pl.multiple_of(k * tile, tile), tile)
            x = xs[:, at]
            weights[2 * e, at, :] = mm(x, lows[3 * e + 1], TN).astype(bf16)
            weights[2 * e + 1, at, :] = mm(x, lows[3 * e + 2], TN).astype(bf16)
            downs[e, :, at] = (residual_scale * mm(lows[3 * e], gs[:, at], TN)).astype(bf16)
            return 0

        lax.fori_loop(0, width // tile, wide, 0)
        outs = (o_near_gate, o_near_up, o_near_down) if e == 0 else (o_far_gate, o_far_up, o_far_down)
        copies = [
            pltpu.make_async_copy(weights.at[2 * e], outs[0], store.at[3 * e]),
            pltpu.make_async_copy(weights.at[2 * e + 1], outs[1], store.at[3 * e + 1]),
            pltpu.make_async_copy(downs.at[e], outs[2], store.at[3 * e + 2]),
        ]
        for c in copies:
            c.start()
        return copies

    stored = []

    def moe_all():
        lax.fori_loop(0, n, moe_block, 0)

    total.flow(
        [
            (lambda: lax.fori_loop(2, a, back_own, 0)) if b == 2 else (lambda: None),
            moe_all,
            lambda: stored.extend(weight_grads(1)),
            lambda: stored.extend(weight_grads(0)),
        ]
    )
    line = total.a_line
    line.end(out_ref)
    gather.finish()
    stage_copy(n - 2).wait()
    stage_copy(n - 1).wait()
    for c in stored:
        c.wait()


def experts_call(rows_low, grads, router, near, far, dp_size, collective_id):
    a, b = group_sizes(dp_size)
    n = a * b
    rows, width = rows_low.shape
    units = near[0].shape[1]
    hbm, vmem = pl.BlockSpec(memory_space=pl.ANY), pl.BlockSpec(memory_space=pltpu.VMEM)
    outs = [
        jax.ShapeDtypeStruct((n * rows, width), bf16),
        jax.ShapeDtypeStruct((rows, width + LANES), f32),
    ] + [jax.ShapeDtypeStruct(x.shape, bf16) for x in near + far]
    return pl.pallas_call(
        functools.partial(experts_kernel, a, b, rows, width),
        out_shape=outs,
        in_specs=[hbm, hbm, vmem] + [hbm] * 6,
        out_specs=[hbm, vmem] + [hbm] * 6,
        scratch_shapes=[
            pltpu.VMEM((n * rows, width), bf16),
            pltpu.VMEM((n * rows, width + LANES), bf16),
            pltpu.VMEM((4, width, units), bf16),
            pltpu.VMEM((2, units, width), bf16),
            pltpu.VMEM((6, n * rows, units), bf16),
            pltpu.VMEM((n * rows, width + LANES), bf16),
            pltpu.VMEM((n * rows, LANES), bf16),
            pltpu.VMEM((2, rows, width), bf16),
            pltpu.SemaphoreType.DMA((7,)),
            pltpu.SemaphoreType.DMA((n,)),
            pltpu.SemaphoreType.DMA((n, 4, PIECES)),
            pltpu.SemaphoreType.DMA((n, PIECES)),
            pltpu.SemaphoreType.DMA((2,)),
            pltpu.SemaphoreType.DMA((6,)),
        ]
        + GroupSum.scratch(a, b, rows, width + LANES),
        compiler_params=pltpu.CompilerParams(
            collective_id=collective_id, has_side_effects=True, vmem_limit_bytes=60 << 20
        ),
    )(rows_low, grads, router, *near, *far)


def reduce_schedule(steps, groups):
    sums = [("sum", s) for s in range(steps)]
    backs = [("back", s) for s in reversed(range(steps))]
    lines = [[(g,) + e for e in sums + backs] for g in range(groups)]
    if groups == 1:
        return lines[0]
    first, second = lines
    order = first[: steps - 1]
    first = first[steps - 1 :]
    while first or second:
        if second:
            order.append(second.pop(0))
        if first:
            order.append(first.pop(0))
    return order


def reduce_kernel(orders, groups, x_ref, small_ref, out_ref, small_out, acc, got, small_got, load, send, recv, small_send, small_recv):
    k = len(orders[0])
    nparts = len(orders)
    size = x_ref.shape[0] // nparts
    loads = []
    for j in range(nparts):
        c = pltpu.make_async_copy(x_ref.at[pl.ds(j * size, size)], acc.at[pl.ds(j * size, size)], load.at[j])
        c.start()
        loads.append(c)
    greet(sorted(orders[0]))
    small_out[...] = small_ref[...]
    copies, back, small_copies = {}, {}, []
    where = [j * size for j in range(nparts)]
    per_group = nparts // groups

    def sum_step(j, step):
        count = size >> (step + 1)
        mask = orders[j][step]
        _, bit = peer_of(mask)
        keep = pl.multiple_of(where[j] + bit * count, 16)
        give = pl.multiple_of(where[j] + (1 - bit) * count, 16)
        if step == 0:
            loads[j].wait()
        else:
            copies[j, step - 1].wait_recv()
            p0 = j * size + (size - (size >> (step - 1)))
            add_rows(acc, give, acc, give, got, p0 + pl.multiple_of((1 - bit) * count, 16), count, bf16)
        g0 = j * size + (size - (size >> step))
        c = remote(acc.at[pl.ds(give, count)], got.at[pl.ds(g0, count)], send.at[j, step], recv.at[j, step], mask)
        c.start()
        copies[j, step] = c
        if step > 0:
            add_rows(acc, keep, acc, keep, got, p0 + pl.multiple_of(bit * count, 16), count, bf16)
        where[j] = keep

    def back_step(j, step):
        count = size >> (step + 1)
        mask = orders[j][step]
        _, bit = peer_of(mask)
        if step == k - 1:
            copies[j, step].wait_recv()
            p0 = j * size + (size - (size >> step))
            add_rows(out_ref, where[j], acc, where[j], got, p0, count, bf16)
        else:
            back[j, step + 1].wait_recv()
        here = where[j]
        c = remote(out_ref.at[pl.ds(here, count)], out_ref.at[pl.ds(here, count)], send.at[j, k + step], recv.at[j, k + step], mask)
        c.start()
        back[j, step] = c
        where[j] = pl.multiple_of(here - bit * count, 16)

    def small_step(step):
        if step > 0:
            small_copies[-1].wait_send()
            small_copies[-1].wait_recv()
            small_out[...] += small_got[step - 1]
        if step < k:
            c = remote(small_out, small_got.at[step], small_send.at[step], small_recv.at[step], orders[0][step])
            c.start()
            small_copies.append(c)

    small_done = 0
    for g, kind, step in reduce_schedule(k, groups):
        for j in range(g * per_group, (g + 1) * per_group):
            (sum_step if kind == "sum" else back_step)(j, step)
        if g == groups - 1 and small_done <= k:
            small_step(small_done)
            small_done += 1
    for j in range(nparts):
        back[j, 0].wait_recv()
    for c in copies.values():
        c.wait_send()
    for c in back.values():
        c.wait_send()


def all_reduce(x, small, masks, collective_id):
    inner, last = masks[:-1], masks[-1:]
    groups = 2 if x.shape[0] % (6 * 16 * 2 ** len(masks)) == 0 else 1
    nparts = 3 * groups
    orders = [rotated(inner, j) + last for j in range(nparts)]
    k = len(masks)
    vm = pl.BlockSpec(memory_space=pltpu.VMEM)
    return pl.pallas_call(
        functools.partial(reduce_kernel, orders, groups),
        out_shape=[jax.ShapeDtypeStruct(x.shape, bf16), jax.ShapeDtypeStruct(small.shape, f32)],
        in_specs=[pl.BlockSpec(memory_space=pl.ANY), vm],
        out_specs=[vm, vm],
        scratch_shapes=[
            pltpu.VMEM(x.shape, bf16),
            pltpu.VMEM(x.shape, bf16),
            pltpu.VMEM((k,) + small.shape, f32),
            pltpu.SemaphoreType.DMA((nparts,)),
            pltpu.SemaphoreType.DMA((nparts, 2 * k)),
            pltpu.SemaphoreType.DMA((nparts, 2 * k)),
            pltpu.SemaphoreType.DMA((k,)),
            pltpu.SemaphoreType.DMA((k,)),
        ],
        compiler_params=pltpu.CompilerParams(
            collective_id=collective_id, has_side_effects=True, vmem_limit_bytes=40 << 20
        ),
    )(x, small)


def place_kernel(dims, *refs):
    n = len(dims)
    mine, other, outs = refs[:n], refs[n : 2 * n], refs[2 * n : 3 * n]
    bufs, sems, out_sems = refs[3 * n : 4 * n], refs[4 * n], refs[4 * n + 1]
    me = lax.axis_index("tensor")

    def copy(i, which, src):
        size = src.shape[dims[i]]
        at = pl.multiple_of((me + which - 2 * which * me) * size, size)
        window = (slice(None),) * dims[i] + (pl.ds(at, size),)
        return pltpu.make_async_copy(src, bufs[i].at[window], sems.at[i, which])

    copies = [[copy(i, w, src) for w, src in enumerate((mine[i], other[i]))] for i in range(n)]
    for pair in copies:
        for c in pair:
            c.start()
    back = []
    for i, pair in enumerate(copies):
        for c in pair:
            c.wait()
        c = pltpu.make_async_copy(bufs[i], outs[i], out_sems.at[i])
        c.start()
        back.append(c)
    for c in back:
        c.wait()


def place(mine, other, dims):
    n = len(dims)
    shapes = [x.shape[:d] + (2 * x.shape[d],) + x.shape[d + 1 :] for x, d in zip(mine, dims)]
    return pl.pallas_call(
        functools.partial(place_kernel, dims),
        out_shape=[jax.ShapeDtypeStruct(s, x.dtype) for x, s in zip(mine, shapes)],
        in_specs=[pl.BlockSpec(memory_space=pl.ANY)] * (2 * n),
        out_specs=[pl.BlockSpec(memory_space=pl.ANY)] * n,
        scratch_shapes=[pltpu.VMEM(s, x.dtype) for x, s in zip(mine, shapes)]
        + [pltpu.SemaphoreType.DMA((n, 2)), pltpu.SemaphoreType.DMA((n,))],
        compiler_params=pltpu.CompilerParams(vmem_limit_bytes=24 << 20),
    )(*mine, *other)


def dot(a, b, spec):
    return jnp.einsum(spec, a, b, preferred_element_type=f32)


def per_device(
    hidden_in,
    attn_gain,
    w_query,
    key_weight,
    value_weight,
    w_output,
    moe_gain,
    w_router,
    w_gate,
    w_up,
    w_down,
    expert_ids,
    segment_ids,
    out_grad,
):
    tokens_here, model_width = hidden_in.shape
    head_size = HEAD_DIM
    dp_size = lax.axis_size("dp")
    tensor_size = lax.axis_size("tensor")
    experts = dp_size
    tensor_index = lax.axis_index("tensor")
    masks = bit_masks(dp_size)
    tensor_masks = bit_masks(tensor_size)
    tensor_down = tensor_masks[::-1]
    rows_here = tokens_here // tensor_size
    groups = [list(range(pair, dp_size, 2)) for pair in range(2)]

    def my_rows(x):
        return lax.dynamic_slice_in_dim(x, tensor_index * rows_here, rows_here, 0)

    block = w_gate.shape[2] // tensor_size

    def my_units(x, dim):
        return lax.dynamic_slice_in_dim(x, tensor_index * block, block, dim)

    def relative_gather(x, dim):
        for mask in tensor_masks:
            x = jnp.concatenate([x, swap(x, "tensor", mask)], dim)
        return x

    def relative_scatter(x, dim):
        for mask in reversed(tensor_masks):
            half = x.shape[dim] // 2
            keep = lax.slice_in_dim(x, 0, half, axis=dim)
            give = lax.slice_in_dim(x, half, 2 * half, axis=dim)
            x = keep.astype(f32) + swap(give.astype(bf16), "tensor", mask).astype(f32)
        return x

    far_set = [
        relative_gather(swap(my_units(w_gate[0], 1), "dp", 1), 1),
        relative_gather(swap(my_units(w_up[0], 1), "dp", 1), 1),
        relative_gather(swap(my_units(w_down[0], 0), "dp", 1), 0),
    ]
    grad_mine = my_rows(out_grad)
    lanes = jnp.arange(LANES, dtype=jnp.int32)
    picked_mine = jnp.any(my_rows(expert_ids)[:, :, None] == lanes[None, None, :], axis=1)
    grads = lax.all_gather(
        jnp.concatenate([grad_mine, picked_mine.astype(bf16)], 1),
        "dp",
        axis=0,
        tiled=True,
        axis_index_groups=groups,
    )
    router_wide = jnp.pad(w_router, ((0, 0), (0, LANES - experts)))

    inputs = hidden_in.astype(f32)
    scale_in = lax.rsqrt(jnp.mean(inputs * inputs, axis=-1, keepdims=True) + epsilon)
    normed_low = (inputs * scale_in * attn_gain).astype(bf16)
    segment = segment_ids[0]
    tables = rope_tables(segment, head_size)
    heads_flat, query_heads, key_heads, value_heads, log_sums = attend_forward(
        normed_low, segment, tables, w_query, key_weight, value_weight, head_size
    )
    attn_part = jnp.dot(heads_flat, w_output, preferred_element_type=f32)
    attn_total = scatter_sum(attn_part, "tensor", tensor_down, f32)

    inputs_mine = my_rows(hidden_in).astype(f32)
    scale_in_mine = my_rows(scale_in)
    middle = inputs_mine + residual_scale * attn_total
    scale_mid = lax.rsqrt(jnp.mean(middle * middle, axis=-1, keepdims=True) + epsilon)
    routed_low = (middle * scale_mid * moe_gain).astype(bf16)

    near_set = [w_gate[0], w_up[0], w_down[0]]
    moe_part, back, *expert_parts = experts_call(
        routed_low, grads, router_wide, near_set, far_set, dp_size, 0
    )
    moe_total = lax.psum_scatter(
        moe_part, "dp", scatter_dimension=0, tiled=True, axis_index_groups=groups
    )

    dims = (1, 1, 0)
    near_mine = [
        scatter_sum(x, "tensor", tensor_down, bf16, d) for x, d in zip(expert_parts[:3], dims)
    ]
    far_mine = [relative_scatter(x, d).astype(bf16) for x, d in zip(expert_parts[3:], dims)]
    back, far_mine = lax.optimization_barrier((back, far_mine))
    returning = [swap(x, "dp", 1) for x in far_mine]

    logits = dot(routed_low, w_router, "td,de->te")
    chosen = picked_mine[:, :experts]
    logits = jnp.where(chosen, logits, masked_score)
    raised = jnp.where(chosen, jnp.exp(logits - jnp.max(logits, axis=1, keepdims=True)), 0.0)
    gate_weights = raised / jnp.sum(raised, axis=1, keepdims=True)
    routed_grad = back[:, :model_width]
    gate_deriv = (
        back[:, model_width : model_width + experts]
        + back[:, model_width + LOW_AT : model_width + LOW_AT + experts]
    )
    chosen_grad = gate_weights * (
        gate_deriv - jnp.sum(gate_weights * gate_deriv, axis=1, keepdims=True)
    )
    logit_grad = chosen_grad.astype(bf16)
    router_part = dot(logit_grad, routed_low, "te,td->ed")
    routed_grad = routed_grad + dot(logit_grad, w_router, "te,de->td")
    gained = moe_gain * routed_grad
    moe_gain_part = jnp.sum(routed_grad * middle * scale_mid, axis=0)
    grad_top = grad_mine.astype(f32)
    middle_grad = (
        grad_top
        + scale_mid * gained
        - middle
        * (scale_mid * scale_mid * scale_mid)
        * jnp.mean(middle * gained, axis=-1, keepdims=True)
    )
    branch_low = gather_blocks(
        (residual_scale * middle_grad).astype(bf16), "tensor", tensor_down
    )
    heads_width = heads_flat.shape[1]
    w_output_part = [
        dot(heads_flat, branch_low[:, i : i + heads_width], "tc,td->cd")
        for i in range(0, model_width, heads_width)
    ]
    heads_grad = dot(branch_low, w_output, "td,cd->tc").astype(bf16)
    query_low, key_low, value_low = attend_backward(
        query_heads, key_heads, value_heads, log_sums, heads_grad, segment, tables
    )
    width_q, width_k = query_low.shape[1], key_low.shape[1]
    qkv_low = jnp.concatenate([query_low, key_low, value_low], axis=1)
    qkv_width = qkv_low.shape[1]
    attention_part = jnp.concatenate(
        [dot(normed_low, qkv_low, "td,tc->dc"), jnp.concatenate(w_output_part, 0)], 1
    ).astype(bf16)
    qkv_weight = jnp.concatenate([w_query, key_weight, value_weight], axis=1)
    normed_part = dot(qkv_low, qkv_weight, "tc,dc->td")
    normed_grad = scatter_sum(normed_part, "tensor", tensor_down, f32)
    gained_in = attn_gain * normed_grad
    attn_gain_part = jnp.sum(normed_grad * inputs_mine * scale_in_mine, axis=0)
    input_mine = (
        middle_grad
        + scale_in_mine * gained_in
        - inputs_mine
        * (scale_in_mine * scale_in_mine * scale_in_mine)
        * jnp.mean(inputs_mine * gained_in, axis=-1, keepdims=True)
    )
    input_grad = gather_blocks(input_mine, "tensor", tensor_down)

    small = jnp.concatenate([router_part, moe_gain_part[None], attn_gain_part[None]], 0)
    small = jnp.pad(small, ((0, -small.shape[0] % 8), (0, 0)))
    for mask in tensor_masks:
        small = small + swap(small, "tensor", mask)
    attention_grad, small = all_reduce(attention_part, small, masks, 2)
    attention_grad, returning, moe_total = lax.optimization_barrier(
        (attention_grad, returning, moe_total)
    )
    block_mine = (middle + residual_scale * moe_total.astype(f32)).astype(bf16)
    block_out = gather_blocks(block_mine, "tensor", tensor_down)
    expert_mine = [mine + away.astype(f32) for mine, away in zip(near_mine, returning)]
    if tensor_size == 2:
        expert_grads = place(expert_mine, [swap(x, "tensor", 1) for x in expert_mine], dims)
    else:
        expert_grads = [
            gather_blocks(x, "tensor", tensor_down, dim) for x, dim in zip(expert_mine, dims)
        ]
    attention_grad = attention_grad.astype(f32)
    w_output_grad = jnp.concatenate(
        [
            attention_grad[i : i + heads_width, qkv_width:]
            for i in range(0, model_width, heads_width)
        ],
        1,
    )
    return (
        block_out,
        input_grad,
        small[experts + 1],
        attention_grad[:, :width_q],
        attention_grad[:, width_q : width_q + width_k],
        attention_grad[:, width_q + width_k : qkv_width],
        w_output_grad,
        small[experts],
        small[:experts].T,
        expert_grads[0][None],
        expert_grads[1][None],
        expert_grads[2][None],
    )


def solution(mesh):
    placed = (
        P("dp", None),
        P(),
        P(None, "tensor"),
        P(None, "tensor"),
        P(None, "tensor"),
        P("tensor", None),
        P(),
        P(),
        P("dp", None, None),
        P("dp", None, None),
        P("dp", None, None),
        P("dp", None),
        P("dp", None),
        P("dp", None),
    )
    return jax.shard_map(
        per_device,
        mesh=mesh,
        in_specs=placed,
        out_specs=(
            P("dp", None),
            P("dp", None),
            P(),
            P(None, "tensor"),
            P(None, "tensor"),
            P(None, "tensor"),
            P("tensor", None),
            P(),
            P(),
            P("dp", None, None),
            P("dp", None, None),
            P("dp", None, None),
        ),
        check_vma=False,
    )
```

```python
import functools

import jax
import jax.numpy as jnp
from jax import lax
from jax.experimental import pallas as pl
from jax.experimental.pallas import tpu as pltpu
from jax.sharding import PartitionSpec as P

HEAD_DIM = 64

bf16 = jnp.bfloat16
f32 = jnp.float32
MESH = pl.DeviceIdType.MESH
epsilon = 1e-06
residual_scale = 0.22
attn_scale = 0.015625
rope_base = 10000.0
masked_score = -1e30


def positions_of(segment):
    position_index = jnp.arange(segment.shape[0], dtype=jnp.int32)
    earlier = jnp.concatenate([segment[:1] - 1, segment[:-1]])
    starts = lax.cummax(jnp.where(segment != earlier, position_index, 0), axis=0)
    return position_index - starts


def rope_tables(segment, head_size):
    position = positions_of(segment).astype(f32)
    frequency = rope_base ** (-jnp.arange(head_size // 2, dtype=f32) * 2.0 / head_size)
    angle = position[:, None] * frequency[None, :]
    return (jnp.cos(angle)[:, None, :], jnp.sin(angle)[:, None, :])


def apply_rotation(heads_in, cosine_table, sine_values):
    middle_index = heads_in.shape[-1] // 2
    first_half = heads_in[..., :middle_index]
    second_half = heads_in[..., middle_index:]
    return jnp.concatenate(
        [
            first_half * cosine_table - second_half * sine_values,
            second_half * cosine_table + first_half * sine_values,
        ],
        axis=-1,
    )


def block_scores(query_heads, key_heads, segment):
    kv_count = key_heads.shape[1]
    length = query_heads.shape[0]
    grouped = query_heads.reshape(length, kv_count, -1, query_heads.shape[2])
    raw_scores = (
        jnp.einsum("qhgd,khd->hgqk", grouped, key_heads, preferred_element_type=f32) * attn_scale
    )
    index = jnp.arange(length, dtype=jnp.int32)
    allowed = (index[:, None] >= index[None, :]) & (segment[:, None] == segment[None, :])
    return (jnp.where(allowed, raw_scores, masked_score), grouped)


def attend_forward(normed, segment, tables, w_query, key_weight, value_weight, head_size):
    length = normed.shape[0]

    def heads(weight):
        return jnp.dot(normed, weight, preferred_element_type=f32).reshape(length, -1, head_size)

    query_heads = apply_rotation(heads(w_query), *tables).astype(bf16)
    key_heads = apply_rotation(heads(key_weight), *tables).astype(bf16)
    value_heads = heads(value_weight).astype(bf16)
    scores, _ = block_scores(query_heads, key_heads, segment)
    largest = jnp.max(scores, axis=-1, keepdims=True)
    weights_raw = jnp.exp(scores - largest)
    totals = jnp.sum(weights_raw, axis=-1, keepdims=True)
    probs_low = (weights_raw / totals).astype(bf16)
    head_out = jnp.einsum("hgqk,khd->qhgd", probs_low, value_heads, preferred_element_type=f32)
    return (
        head_out.reshape(length, -1).astype(bf16),
        query_heads,
        key_heads,
        value_heads,
        (largest + jnp.log(totals))[..., 0],
    )


def attend_backward(query_heads, key_heads, value_heads, log_sums, heads_grad, segment, tables):
    length = query_heads.shape[0]
    cosine_table, sine_values = tables
    scores, grouped = block_scores(query_heads, key_heads, segment)
    probability = jnp.exp(scores - log_sums[..., None])
    probs_low = probability.astype(bf16)
    grad_grouped = heads_grad.reshape(grouped.shape)
    prob_grad = jnp.einsum(
        "qhgd,khd->hgqk", grad_grouped, value_heads, preferred_element_type=f32
    )
    weighted = jnp.sum(probability * prob_grad, axis=-1, keepdims=True)
    score_low = (probability * (prob_grad - weighted)).astype(bf16)
    query_part = (
        jnp.einsum("hgqk,khd->qhgd", score_low, key_heads, preferred_element_type=f32) * attn_scale
    ).reshape(query_heads.shape)
    key_sum = (
        jnp.einsum("hgqk,qhgd->khd", score_low, grouped, preferred_element_type=f32) * attn_scale
    )
    value_sum = jnp.einsum(
        "hgqk,qhgd->khd", probs_low, grad_grouped, preferred_element_type=f32
    )
    query_low = apply_rotation(query_part, cosine_table, -sine_values).astype(bf16)
    key_low = apply_rotation(key_sum, cosine_table, -sine_values).astype(bf16)
    return (
        query_low.reshape(length, -1),
        key_low.reshape(length, -1),
        value_sum.astype(bf16).reshape(length, -1),
    )


def bit_masks(size):
    masks = []
    while size > 1:
        size //= 2
        masks.append(size)
    return masks[::-1]


def swap(x, axis, mask):
    return lax.ppermute(x, axis, [(i, i ^ mask) for i in range(lax.axis_size(axis))])


def bit_of(axis, mask):
    return (lax.axis_index(axis) // mask) % 2


def halves_by_bit(x, axis, mask, dim=0):
    half = x.shape[dim] // 2
    bit = bit_of(axis, mask)
    mine = lax.dynamic_slice_in_dim(x, bit * half, half, dim)
    other = lax.dynamic_slice_in_dim(x, (1 - bit) * half, half, dim)
    return mine, other


def join_by_bit(mine, other, axis, mask, dim=0):
    return jnp.where(
        bit_of(axis, mask) == 0,
        jnp.concatenate([mine, other], dim),
        jnp.concatenate([other, mine], dim),
    )


def scatter_sum(x, axis, masks, kind, dim=0):
    x = x.astype(f32)
    for mask in masks:
        mine, other = halves_by_bit(x, axis, mask, dim)
        x = mine + swap(other.astype(kind), axis, mask).astype(f32)
    return x


def gather_blocks(x, axis, masks, dim=0):
    for mask in reversed(masks):
        x = join_by_bit(x, swap(x, axis, mask), axis, mask, dim)
    return x


def rotated(masks, j):
    j = j % len(masks)
    return masks[j:] + masks[:j]


def peer_of(mask):
    me = lax.axis_index("dp")
    bit = (me // mask) % 2
    return me + mask * (1 - 2 * bit), bit


def greet(masks):
    barrier = pltpu.get_barrier_semaphore()
    for mask in masks:
        pl.semaphore_signal(
            barrier, inc=1, device_id={"dp": peer_of(mask)[0]}, device_id_type=MESH
        )
    pl.semaphore_wait(barrier, len(masks))


def remote(src, dst, send, recv, mask):
    return remote_to(src, dst, send, recv, peer_of(mask)[0])


def add_rows(dst, dst0, a, a0, b, b0, rows, out_dtype):
    step = 16

    def body(i, _):
        r = pl.multiple_of(i * step, step)
        x = a[pl.ds(a0 + r, step), :].astype(f32) + b[pl.ds(b0 + r, step), :].astype(f32)
        dst[pl.ds(dst0 + r, step), :] = x.astype(out_dtype)
        return 0

    lax.fori_loop(0, rows // step, body, 0)


def group_sizes(dp_size):
    a = 4
    return a, dp_size // (2 * a)


class Spot:
    def __init__(self, a, b):
        me = lax.axis_index("dp")
        self.a, self.b = a, b
        self.n = a * b
        self.me = me
        self.A = me // (2 * b)
        self.B = (me // 2) % b
        self.block = me // 2
        self.pair = me % 2
        self.devices = (me + 2 * b, me - 2 * b, me + 2, me - 2)
        self.exists = (self.A < a - 1, self.A > 0, self.B < b - 1, self.B > 0)
        self.some = me + 2 * (1 - 2 * (self.B % 2))

    def greet(self):
        barrier = pltpu.get_barrier_semaphore()
        for device, there in zip(self.devices, self.exists):

            @pl.when(there)
            def _(device=device):
                pl.semaphore_signal(
                    barrier, inc=1, device_id={"dp": device}, device_id_type=MESH
                )

        a, b = self.a, self.b
        ups = 2 - (self.A + 1) // a - (self.B + 1) // b
        downs = (self.A + a - 1) // a + (self.B + b - 1) // b
        pl.semaphore_wait(barrier, ups + downs)


def is_at(x, value):
    return 1 // (1 + (x - value) * (x - value))


def by_distance(size, place, k):
    found = 0
    for p in range(size):
        order = sorted(range(size), key=lambda q: (abs(q - p), q))
        for j, q in enumerate(order):
            if q > 0:
                found = found + q * is_at(place, p) * is_at(k, j)
    return found


def visit_order(a, b):
    pairs = [(k, l) for k in range(a) for l in range(b)]
    return sorted(pairs, key=lambda kl: kl[0] + (2 * kl[1] + 0.5 if kl[1] else 0))


def remote_to(src, dst, send, recv, device):
    return pltpu.make_async_remote_copy(
        src_ref=src,
        dst_ref=dst,
        send_sem=send,
        recv_sem=recv,
        device_id={"dp": device},
        device_id_type=MESH,
    )


PIECES = 2
SUM_PIECES = 4


class LineGather:
    def __init__(self, spot, buf, rows, send, recv):
        self.spot, self.buf, self.rows, self.send, self.recv = spot, buf, rows, send, recv

    def coords(self, i):
        s = self.spot
        visits = visit_order(s.a, s.b)
        k = sum(v[0] * is_at(i, j) for j, v in enumerate(visits) if v[0])
        l = sum(v[1] * is_at(i, j) for j, v in enumerate(visits) if v[1])
        return by_distance(s.a, s.A, k), by_distance(s.b, s.B, l)

    def row0(self, i):
        A, B = self.coords(i)
        return pl.multiple_of((A * self.spot.b + B) * self.rows, 16)

    def copies(self, block, way, device):
        size = self.rows // PIECES
        return [
            remote_to(there, there, self.send.at[block, way, p], self.recv.at[block, p], device)
            for p in range(PIECES)
            for there in [self.buf.at[pl.ds(pl.multiple_of(block * self.rows + p * size, 16), size)]]
        ]

    def each_way(self, i, act):
        s = self.spot
        A, B = self.coords(i)
        block = A * s.b + B
        same = B == s.B
        conditions = (
            same & (A <= s.A) & s.exists[0],
            same & (A >= s.A) & s.exists[1],
            (B <= s.B) & s.exists[2],
            (B >= s.B) & s.exists[3],
        )
        for way, (condition, device) in enumerate(zip(conditions, s.devices)):

            @pl.when(condition)
            def _(way=way, device=device):
                for c in self.copies(block, way, device):
                    act(c)

    def wait(self, i):
        A, B = self.coords(i)
        for c in self.copies(A * self.spot.b + B, 0, self.spot.some):
            c.wait_recv()

    def forward(self, i):
        self.each_way(i, lambda c: c.start())

    def finish(self):
        def one(i, _):
            self.each_way(i, lambda c: c.wait_send())
            return 0

        lax.fori_loop(0, self.spot.n, one, 0)


def add_into(dst, d0, src, s0, rows, step=16):
    def body(i, _):
        r = pl.multiple_of(i * step, step)
        total = dst[pl.ds(d0 + r, step), :].astype(f32) + src[pl.ds(s0 + r, step), :].astype(f32)
        dst[pl.ds(d0 + r, step), :] = total.astype(dst.dtype)
        return 0

    lax.fori_loop(0, rows // step, body, 0)


class LineSum:
    def __init__(self, size, place, up, down, part, row_of, rows, got, send, recv, some):
        self.size, self.place, self.up, self.down = size, place, up, down
        self.part, self.row_of, self.rows, self.got = part, row_of, rows, got
        self.send, self.recv, self.some = send, recv, some

    def up_slot(self, place, c):
        return c - place

    def down_slot(self, place, c):
        return c + (self.size - place) * ((place + self.size - 1) // self.size)

    def copies(self, c, slot, send, device):
        size = self.rows // SUM_PIECES
        return [
            remote_to(
                self.part.at[pl.ds(pl.multiple_of(self.row_of(c) + p * size, 16), size)],
                self.got.at[pl.ds(pl.multiple_of(slot * self.rows + p * size, 16), size)],
                send.at[p],
                self.recv.at[slot, p],
                device,
            )
            for p in range(SUM_PIECES)
        ]

    def take(self, c, slot, p, dst=None, d0=None):
        if dst is None:
            dst, d0 = self.part, self.row_of(c)
        size = self.rows // SUM_PIECES
        self.copies(c, slot, self.send.at[0, 0], self.some)[p].wait_recv()
        from_row = pl.multiple_of(slot * self.rows + p * size, 16)
        add_into(dst, d0 + p * size, self.got, from_row, size)

    def up_copies(self, k):
        c = self.size - 1 - k
        return self.copies(c, self.up_slot(self.place + 1, c), self.send.at[k, 0], self.up)

    def down_copies(self, k):
        return self.copies(k, self.down_slot(self.place - 1, k), self.send.at[k, 1], self.down)

    def step_up(self, k):
        c = self.size - 1 - k

        @pl.when(c > self.place)
        def _():
            for p, copy in enumerate(self.up_copies(k)):

                @pl.when(self.place > 0)
                def _(p=p):
                    self.take(c, self.up_slot(self.place, c), p)

                copy.start()

    def step_down(self, k):
        @pl.when(k < self.place)
        def _():
            for p, copy in enumerate(self.down_copies(k)):

                @pl.when(self.place < self.size - 1)
                def _(p=p):
                    self.take(k, self.down_slot(self.place, k), p)

                copy.start()

    def step(self, k):
        self.step_up(k)
        self.step_down(k)

    def end(self, out=None):
        p = self.place
        d0 = None
        if out is not None:
            out[...] = self.part[pl.ds(self.row_of(p), self.rows), :].astype(out.dtype)
            d0 = 0

        @pl.when(p > 0)
        def _():
            for j in range(SUM_PIECES):
                self.take(p, self.up_slot(p, p), j, out, d0)

        @pl.when(p < self.size - 1)
        def _():
            for j in range(SUM_PIECES):
                self.take(p, self.down_slot(p, p), j, out, d0)

        for k in range(self.size - 1):

            @pl.when(self.size - 1 - k > p)
            def _(k=k):
                for c in self.up_copies(k):
                    c.wait_send()

            @pl.when(k < p)
            def _(k=k):
                for c in self.down_copies(k):
                    c.wait_send()


def slots_of(size):
    return 1 if size == 2 else size + 1


class GroupSum:
    def __init__(self, spot, part, rows, got_b, got_a, send_b, recv_b, send_a, recv_a):
        self.spot, self.part, self.rows = spot, part, rows
        a, b = spot.a, spot.b
        slots_b = slots_of(b)

        def b_line(A):
            return LineSum(
                b, spot.B, spot.devices[2], spot.devices[3], part,
                lambda B: pl.multiple_of((A * b + B) * rows, 16), rows,
                got_b.at[pl.ds(pl.multiple_of(A * slots_b * rows, 16), slots_b * rows)],
                send_b.at[A], recv_b.at[A], spot.some,
            )

        self.b_line = b_line
        self.a_line = LineSum(
            a, spot.A, spot.devices[0], spot.devices[1], part,
            lambda A: pl.multiple_of((A * b + spot.B) * rows, 16), rows,
            got_a, send_a, recv_a, spot.some,
        )

    def ready(self, A, B):
        if self.spot.b == 2:
            line = self.b_line(A)

            @pl.when(B != self.spot.B)
            def _():
                line.step(0)

    def along_b(self):
        if self.spot.b > 2:

            def one(A, _):
                for k in range(self.spot.b - 1):
                    self.b_line(A).step(k)
                return 0

            lax.fori_loop(0, self.spot.a, one, 0)

    def flow(self, fills):
        a, line = self.spot.a, self.a_line
        fills = list(fills)

        def fill():
            if fills:
                fills.pop(0)()

        for k in range(a - 1):
            if 2 * k < a:
                self.b_line(a - 1 - k).end()
            line.step_up(k)
            fill()
            if 2 * k < a and a - 1 - k != k:
                self.b_line(k).end()
            line.step_down(k)
            fill()
        while fills:
            fill()

    def order(self, j):
        a = self.spot.a
        places = sorted(range(a), key=lambda c: (min(c, a - 1 - c), -c))
        return sum(c * is_at(j, i) for i, c in enumerate(places) if c)

    def steps_a(self):
        return self.spot.a - 1

    @staticmethod
    def scratch(a, b, rows, width):
        return [
            pltpu.VMEM((a * slots_of(b) * rows, width), bf16),
            pltpu.VMEM((slots_of(a) * rows, width), bf16),
            pltpu.SemaphoreType.DMA((a, b - 1, 2, SUM_PIECES)),
            pltpu.SemaphoreType.DMA((a, slots_of(b), SUM_PIECES)),
            pltpu.SemaphoreType.DMA((a - 1, 2, SUM_PIECES)),
            pltpu.SemaphoreType.DMA((slots_of(a), SUM_PIECES)),
        ]


LANES = 128
LOW_AT = 64


def mm(x, y, dims):
    return lax.dot_general(x, y, (dims, ((), ())), preferred_element_type=f32)


NN, NT, TN = ((1,), (0,)), ((1,), (1,)), ((0,), (0,))


def experts_kernel(
    a, b, rows, width,
    x_ref, grads_ref, router_ref, near_gate, near_up, near_down, far_gate, far_up, far_down,
    moe_ref, out_ref, o_near_gate, o_near_up, o_near_down, o_far_gate, o_far_up, o_far_down,
    xs, gs, weights, downs, lows, part, extras, stage, local, load, send, recv, stage_sem, store, *scratch,
):
    spot = Spot(a, b)
    n = spot.n
    gather = LineGather(spot, xs, rows, send, recv)
    total = GroupSum(spot, part, rows, *scratch)
    mine = pltpu.make_async_copy(
        x_ref, xs.at[pl.ds(pl.multiple_of(spot.block * rows, 16), rows)], local.at[0]
    )
    mine.start()
    sources = (near_gate, near_up, far_gate, far_up)
    arriving = [
        pltpu.make_async_copy(src, weights.at[k], local.at[1 + k]) for k, src in enumerate(sources)
    ] + [
        pltpu.make_async_copy(src, downs.at[k], local.at[5 + k])
        for k, src in enumerate((near_down, far_down))
    ]

    def grads_copy(i):
        at = pl.ds(gather.row0(i), rows)
        return pltpu.make_async_copy(grads_ref.at[at], gs.at[at], load.at[i])

    grads_copy(0).start()
    for c in arriving:
        c.start()
    for i in range(1, n):
        grads_copy(i).start()
    spot.greet()
    mine.wait()
    gather.forward(0)
    for c in arriving:
        c.wait()
    lane = lax.broadcasted_iota(jnp.int32, (rows, LANES), 1)
    near, far = spot.me, spot.me + 1 - 2 * spot.pair

    def block(i, _):
        at = pl.ds(gather.row0(i), rows)
        grads_copy(i).wait()
        x = xs[at, :]
        chosen = gs[at, pl.ds(width, LANES)] > 0
        logits = jnp.where(chosen, mm(x, router_ref[...], NN), masked_score)
        raised = jnp.where(chosen, jnp.exp(logits - jnp.max(logits, axis=1, keepdims=True)), 0.0)
        gates = raised / jnp.sum(raised, axis=1, keepdims=True)
        extra = jnp.zeros((rows, LANES), f32)
        for e, expert in enumerate((near, far)):
            if e == 1:

                @pl.when(i + 1 < n)
                def _():
                    gather.wait(i + 1)
                    gather.forward(i + 1)

            column = jnp.sum(jnp.where(lane == expert, gates, 0.0), axis=1, keepdims=True)
            x = xs[at, :]
            gate_act = mm(x, weights[2 * e], NN)
            up_act = mm(x, weights[2 * e + 1], NN)
            down_in = residual_scale * mm(gs[at, pl.ds(0, width)], downs[e], NT)
            sigmoid_gate = jax.nn.sigmoid(gate_act)
            silu_gate = gate_act * sigmoid_gate
            hidden = silu_gate * up_act
            deriv = jnp.sum(hidden * down_in, axis=1, keepdims=True)
            high = deriv.astype(bf16).astype(f32)
            extra += jnp.where(lane == expert, high, 0.0)
            extra += jnp.where(lane == expert + LOW_AT, deriv - high, 0.0)
            down_in = down_in * column
            lows[3 * e, at, :] = (hidden * column).astype(bf16)
            lows[3 * e + 1, at, :] = (
                down_in * up_act * sigmoid_gate * (1.0 + gate_act * (1.0 - sigmoid_gate))
            ).astype(bf16)
            lows[3 * e + 2, at, :] = (down_in * silu_gate).astype(bf16)

        extras[at, :] = extra.astype(bf16)
        return 0

    lax.fori_loop(0, n, block, 0)

    def rows_of(A, B):
        return pl.ds(pl.multiple_of((A * b + B) * rows, 16), rows)

    def back_block(A, B):
        at = rows_of(A, B)
        back = mm(lows[1, at, :], weights[0], NT) + mm(lows[2, at, :], weights[1], NT)
        back += mm(lows[4, at, :], weights[2], NT) + mm(lows[5, at, :], weights[3], NT)
        part[at, pl.ds(0, width)] = back.astype(bf16)
        part[at, pl.ds(width, LANES)] = extras[at, :]
        total.ready(A, B)

    def back_others(i, _):
        A = total.order(i // (b - 1))
        B = by_distance(b, spot.B, 1 + i % (b - 1))
        back_block(A, B)
        return 0

    def back_own(i, _):
        back_block(total.order(i), spot.B)
        return 0

    def stage_copy(i):
        at = pl.ds(pl.multiple_of(i * rows, 16), rows)
        return pltpu.make_async_copy(stage.at[i % 2], moe_ref.at[at], stage_sem.at[i % 2])

    def moe_block(i, _):
        at = pl.ds(pl.multiple_of(i * rows, 16), rows)

        @pl.when(i >= 2)
        def _():
            stage_copy(i - 2).wait()

        stage[i % 2] = (mm(lows[0, at, :], downs[0], NN) + mm(lows[3, at, :], downs[1], NN)).astype(
            bf16
        )
        stage_copy(i).start()
        return 0

    lax.fori_loop(0, a * (b - 1), back_others, 0)
    lax.fori_loop(0, 2, back_own, 0)
    if b > 2:
        lax.fori_loop(2, a, back_own, 0)
    total.along_b()
    tile = 256

    def weight_grads(e):
        def wide(k, _):
            at = pl.ds(pl.multiple_of(k * tile, tile), tile)
            x = xs[:, at]
            weights[2 * e, at, :] = mm(x, lows[3 * e + 1], TN).astype(bf16)
            weights[2 * e + 1, at, :] = mm(x, lows[3 * e + 2], TN).astype(bf16)
            downs[e, :, at] = (residual_scale * mm(lows[3 * e], gs[:, at], TN)).astype(bf16)
            return 0

        lax.fori_loop(0, width // tile, wide, 0)
        outs = (o_near_gate, o_near_up, o_near_down) if e == 0 else (o_far_gate, o_far_up, o_far_down)
        copies = [
            pltpu.make_async_copy(weights.at[2 * e], outs[0], store.at[3 * e]),
            pltpu.make_async_copy(weights.at[2 * e + 1], outs[1], store.at[3 * e + 1]),
            pltpu.make_async_copy(downs.at[e], outs[2], store.at[3 * e + 2]),
        ]
        for c in copies:
            c.start()
        return copies

    stored = []

    def moe_all():
        lax.fori_loop(0, n, moe_block, 0)

    total.flow(
        [
            (lambda: lax.fori_loop(2, a, back_own, 0)) if b == 2 else (lambda: None),
            moe_all,
            lambda: stored.extend(weight_grads(1)),
            lambda: stored.extend(weight_grads(0)),
        ]
    )
    line = total.a_line
    line.end(out_ref)
    gather.finish()
    stage_copy(n - 2).wait()
    stage_copy(n - 1).wait()
    for c in stored:
        c.wait()


def experts_call(rows_low, grads, router, near, far, dp_size, collective_id):
    a, b = group_sizes(dp_size)
    n = a * b
    rows, width = rows_low.shape
    units = near[0].shape[1]
    hbm, vmem = pl.BlockSpec(memory_space=pl.ANY), pl.BlockSpec(memory_space=pltpu.VMEM)
    outs = [
        jax.ShapeDtypeStruct((n * rows, width), bf16),
        jax.ShapeDtypeStruct((rows, width + LANES), f32),
    ] + [jax.ShapeDtypeStruct(x.shape, bf16) for x in near + far]
    return pl.pallas_call(
        functools.partial(experts_kernel, a, b, rows, width),
        out_shape=outs,
        in_specs=[hbm, hbm, vmem] + [hbm] * 6,
        out_specs=[hbm, vmem] + [hbm] * 6,
        scratch_shapes=[
            pltpu.VMEM((n * rows, width), bf16),
            pltpu.VMEM((n * rows, width + LANES), bf16),
            pltpu.VMEM((4, width, units), bf16),
            pltpu.VMEM((2, units, width), bf16),
            pltpu.VMEM((6, n * rows, units), bf16),
            pltpu.VMEM((n * rows, width + LANES), bf16),
            pltpu.VMEM((n * rows, LANES), bf16),
            pltpu.VMEM((2, rows, width), bf16),
            pltpu.SemaphoreType.DMA((7,)),
            pltpu.SemaphoreType.DMA((n,)),
            pltpu.SemaphoreType.DMA((n, 4, PIECES)),
            pltpu.SemaphoreType.DMA((n, PIECES)),
            pltpu.SemaphoreType.DMA((2,)),
            pltpu.SemaphoreType.DMA((6,)),
        ]
        + GroupSum.scratch(a, b, rows, width + LANES),
        compiler_params=pltpu.CompilerParams(
            collective_id=collective_id, has_side_effects=True, vmem_limit_bytes=60 << 20
        ),
    )(rows_low, grads, router, *near, *far)


def reduce_schedule(steps, groups):
    sums = [("sum", s) for s in range(steps)]
    backs = [("back", s) for s in reversed(range(steps))]
    lines = [[(g,) + e for e in sums + backs] for g in range(groups)]
    if groups == 1:
        return lines[0]
    first, second = lines
    order = first[: steps - 1]
    first = first[steps - 1 :]
    while first or second:
        if second:
            order.append(second.pop(0))
        if first:
            order.append(first.pop(0))
    return order


def place_kernel(dims, *refs):
    n = len(dims)
    mine, other, outs = refs[:n], refs[n : 2 * n], refs[2 * n : 3 * n]
    bufs, sems, out_sems = refs[3 * n : 4 * n], refs[4 * n], refs[4 * n + 1]
    me = lax.axis_index("tensor")

    def copy(i, which, src):
        size = src.shape[dims[i]]
        at = pl.multiple_of((me + which - 2 * which * me) * size, size)
        window = (slice(None),) * dims[i] + (pl.ds(at, size),)
        return pltpu.make_async_copy(src, bufs[i].at[window], sems.at[i, which])

    copies = [[copy(i, w, src) for w, src in enumerate((mine[i], other[i]))] for i in range(n)]
    for pair in copies:
        for c in pair:
            c.start()
    back = []
    for i, pair in enumerate(copies):
        for c in pair:
            c.wait()
        c = pltpu.make_async_copy(bufs[i], outs[i], out_sems.at[i])
        c.start()
        back.append(c)
    for c in back:
        c.wait()


def place(mine, other, dims):
    n = len(dims)
    shapes = [x.shape[:d] + (2 * x.shape[d],) + x.shape[d + 1 :] for x, d in zip(mine, dims)]
    return pl.pallas_call(
        functools.partial(place_kernel, dims),
        out_shape=[jax.ShapeDtypeStruct(s, x.dtype) for x, s in zip(mine, shapes)],
        in_specs=[pl.BlockSpec(memory_space=pl.ANY)] * (2 * n),
        out_specs=[pl.BlockSpec(memory_space=pl.ANY)] * n,
        scratch_shapes=[pltpu.VMEM(s, x.dtype) for x, s in zip(mine, shapes)]
        + [pltpu.SemaphoreType.DMA((n, 2)), pltpu.SemaphoreType.DMA((n,))],
        compiler_params=pltpu.CompilerParams(vmem_limit_bytes=24 << 20),
    )(*mine, *other)


class AllReduce:
    def __init__(self, orders, groups, acc, got, out, send, recv):
        self.orders, self.groups = orders, groups
        self.acc, self.got, self.out, self.send, self.recv = acc, got, out, send, recv
        self.k = len(orders[0])
        self.size = acc.shape[0] // len(orders)
        self.where = [j * self.size for j in range(len(orders))]
        self.sums, self.backs = {}, {}

    def sum_step(self, j, step):
        count = self.size >> (step + 1)
        mask = self.orders[j][step]
        _, bit = peer_of(mask)
        keep = pl.multiple_of(self.where[j] + bit * count, 16)
        give = pl.multiple_of(self.where[j] + (1 - bit) * count, 16)
        acc, got = self.acc, self.got
        if step > 0:
            self.sums[j, step - 1].wait_recv()
            p0 = j * self.size + (self.size - (self.size >> (step - 1)))
            add_rows(acc, give, acc, give, got, p0 + pl.multiple_of((1 - bit) * count, 16), count, bf16)
        g0 = j * self.size + (self.size - (self.size >> step))
        c = remote(
            acc.at[pl.ds(give, count)],
            got.at[pl.ds(g0, count)],
            self.send.at[j, step],
            self.recv.at[j, step],
            mask,
        )
        c.start()
        self.sums[j, step] = c
        if step > 0:
            add_rows(acc, keep, acc, keep, got, p0 + pl.multiple_of(bit * count, 16), count, bf16)
        self.where[j] = keep

    def back_step(self, j, step):
        count = self.size >> (step + 1)
        mask = self.orders[j][step]
        _, bit = peer_of(mask)
        here = self.where[j]
        if step == self.k - 1:
            self.sums[j, step].wait_recv()
            p0 = j * self.size + (self.size - (self.size >> step))
            add_rows(self.out, here, self.acc, here, self.got, p0, count, bf16)
        else:
            self.backs[j, step + 1].wait_recv()
        there = self.out.at[pl.ds(here, count)]
        c = remote(
            there, there, self.send.at[j, self.k + step], self.recv.at[j, self.k + step], mask
        )
        c.start()
        self.backs[j, step] = c
        self.where[j] = pl.multiple_of(here - bit * count, 16)

    def events(self):
        per_group = len(self.orders) // self.groups

        def event(g, kind, step):
            for j in range(g * per_group, (g + 1) * per_group):
                (self.sum_step if kind == "sum" else self.back_step)(j, step)

        return [
            functools.partial(event, *e) for e in reduce_schedule(self.k, self.groups)
        ]

    def finish(self):
        for j in range(len(self.orders)):
            self.backs[j, 0].wait_recv()
        for c in list(self.sums.values()) + list(self.backs.values()):
            c.wait_send()


def sum_orders(dp_size, rows, most):
    masks = bit_masks(dp_size)
    groups = most if rows % (3 * most * 16 * dp_size) == 0 else 1
    return [rotated(masks[:-1], j) + masks[-1:] for j in range(3 * groups)], groups


def turn(x, cosine, sine):
    lane = lax.broadcasted_iota(jnp.int32, x.shape, 1)
    swapped = jnp.where(lane % HEAD_DIM < HEAD_DIM // 2, pltpu.roll(x, 128 - 32, 1), pltpu.roll(x, 32, 1))
    return x * cosine + swapped * sine


def mask_bias(bias, seg_col, seg_row):
    length = bias.shape[0]
    row = lax.broadcasted_iota(jnp.int32, bias.shape, 0)
    col = lax.broadcasted_iota(jnp.int32, bias.shape, 1)
    allowed = (row >= col) & (seg_col[...] == seg_row[...])
    bias[...] = jnp.where(allowed, 0.0, masked_score)


def attention_back_kernel(
    dp_size, tensor_size, orders_o, groups_o, orders_q, groups_q,
    back, middle, scale_mid, routed, grad_top, picked, router, moe_gain,
    heads, q_ref, k_ref, v_ref, w_out, w_query, w_key, w_value, normed, cosine, sine,
    seg_col, seg_row, hidden, gain, scale_in,
    out_o, out_q, out_input, small_out,
    branch, middle_grad, bias, heads_grad, qkv_low, scratch_q, scratch_k, scratch_v,
    acc_o, got_o, acc_q, got_q, shares, got_shares, small_got,
    send_o, recv_o, send_q, recv_q, small_send, small_recv, share_send, share_recv, in_send, in_recv, branch_send, branch_recv,
):
    length, width = normed.shape
    q_width, k_width = q_ref.shape[1], k_ref.shape[1]
    rows = hidden.shape[0]
    per_kv = q_width // k_width
    core = lax.axis_index("tensor")
    tensor_masks = bit_masks(tensor_size)

    def mate(m):
        bit = (core // m) % 2
        return core + m * (1 - 2 * bit)

    barrier = pltpu.get_barrier_semaphore()
    masks = bit_masks(dp_size)
    others = [(core + m) % tensor_size for m in range(1, tensor_size)]
    for mask in masks:
        pl.semaphore_signal(
            barrier, inc=1, device_id={"dp": peer_of(mask)[0]}, device_id_type=MESH
        )
    for other in others:
        pl.semaphore_signal(barrier, inc=1, device_id={"tensor": other}, device_id_type=MESH)
    mine = pl.ds(pl.multiple_of(core * rows, 16), rows)
    experts = dp_size
    x = routed[...]
    chosen = picked[...] > 0
    logits = jnp.where(chosen, mm(x, router[...], NN), masked_score)
    raised = jnp.where(chosen, jnp.exp(logits - jnp.max(logits, axis=1, keepdims=True)), 0.0)
    gates = raised / jnp.sum(raised, axis=1, keepdims=True)
    derivs = back[:, pl.ds(width, LANES)]
    derivs = jnp.where(chosen, derivs + pltpu.roll(derivs, LANES - LOW_AT, 1), 0.0)
    logit_grad = (
        gates * (derivs - jnp.sum(gates * derivs, axis=1, keepdims=True))
    ).astype(bf16)
    small_out[...] = jnp.zeros(small_out.shape, f32)
    small_out[pl.ds(0, experts), :] = mm(logit_grad, x, TN)[:experts]
    routed_grad = back[:, pl.ds(0, width)] + mm(logit_grad, router[...], NT)
    mid = middle[...]
    r2 = scale_mid[...]
    small_out[pl.ds(experts, 1), :] = jnp.sum(routed_grad * mid * r2, axis=0, keepdims=True)
    gained = moe_gain[...] * routed_grad
    middle_grad[...] = (
        grad_top[...].astype(f32)
        + r2 * gained
        - mid * (r2 * r2 * r2) * jnp.mean(mid * gained, axis=1, keepdims=True)
    )
    branch[mine, :] = (residual_scale * middle_grad[...]).astype(bf16)
    pl.semaphore_wait(barrier, len(masks) + len(others))
    branch_copies = []
    for m, other in enumerate(others):
        c = pltpu.make_async_remote_copy(
            src_ref=branch.at[mine], dst_ref=branch.at[mine], send_sem=branch_send.at[m],
            recv_sem=branch_recv.at[m], device_id={"tensor": other}, device_id_type=MESH,
        )
        c.start()
        branch_copies.append(c)
    mask_bias(bias, seg_col, seg_row)
    for c in branch_copies:
        c.wait()
    for i in range(width // q_width):
        at = pl.ds(i * q_width, q_width)
        acc_o[at, :] = mm(heads[...], branch[:, at], TN).astype(bf16)
    sum_o = AllReduce(orders_o, groups_o, acc_o, got_o, out_o, send_o, recv_o)
    events_o = sum_o.events()
    events_o.pop(0)()
    heads_grad[...] = mm(branch[...], w_out[...], NT).astype(bf16)
    half = length // 2
    spans = ((0, half, half), (half, half, length))
    count = 0
    for pair in range(k_width // 128):
        k_tile = k_ref[:, pair * 128 : pair * 128 + 128]
        v_tile = v_ref[:, pair * 128 : pair * 128 + 128]
        for g in range(2):
            kg = k_tile[:, g * HEAD_DIM : (g + 1) * HEAD_DIM]
            vg = v_tile[:, g * HEAD_DIM : (g + 1) * HEAD_DIM]
            side = pl.ds(g * HEAD_DIM, HEAD_DIM)
            for h in range(per_kv):
                head = (pair * 2 + g) * per_kv + h
                lanes = pl.ds(head * HEAD_DIM, HEAD_DIM)
                for start, size, cols in spans:
                    at = pl.ds(start, size)
                    qh = q_ref[at, lanes]
                    oh = heads_grad[at, lanes]
                    scores = mm(qh, kg[:cols], NT) * attn_scale + bias[at, pl.ds(0, cols)]
                    raised = jnp.exp(scores - jnp.max(scores, axis=1, keepdims=True))
                    probability = raised * (1.0 / jnp.sum(raised, axis=1, keepdims=True))
                    prob_grad = mm(oh, vg[:cols], NT)
                    weighted = jnp.sum(probability * prob_grad, axis=1, keepdims=True)
                    score_low = (probability * (prob_grad - weighted)).astype(bf16)
                    probs_low = probability.astype(bf16)
                    scratch_q[at, lanes] = mm(score_low, kg[:cols], NN) * attn_scale
                    dk = mm(score_low, qh, TN) * attn_scale
                    dv = mm(probs_low, oh, TN)
                    upto = pl.ds(0, cols)
                    if h == 0 and start == 0:
                        scratch_k[upto, side] = dk
                        scratch_v[upto, side] = dv
                        scratch_k[pl.ds(cols, length - cols), side] = jnp.zeros((length - cols, HEAD_DIM), f32)
                        scratch_v[pl.ds(cols, length - cols), side] = jnp.zeros((length - cols, HEAD_DIM), f32)
                    else:
                        scratch_k[upto, side] += dk
                        scratch_v[upto, side] += dv
                count += 1
                if count % 2 == 0 and len(events_o) > 1:
                    events_o.pop(0)()
        at = pl.ds(q_width + pair * 128, 128)
        qkv_low[:, at] = turn(scratch_k[...], cosine[...], -sine[...]).astype(bf16)
        at = pl.ds(q_width + k_width + pair * 128, 128)
        qkv_low[:, at] = scratch_v[...].astype(bf16)
    for i in range(q_width // 128):
        at = pl.ds(i * 128, 128)
        qkv_low[:, at] = turn(scratch_q[:, at], cosine[...], -sine[...]).astype(bf16)
    chunk = width // len(orders_q)
    for i in range(len(orders_q)):
        at = pl.ds(i * chunk, chunk)
        acc_q[at, :] = mm(normed[:, at], qkv_low[...], TN).astype(bf16)
    sum_q = AllReduce(orders_q, groups_q, acc_q, got_q, out_q, send_q, recv_q)
    events_q = sum_q.events()
    events_q.pop(0)()
    while events_o:
        events_o.pop(0)()

    def shares_of(t):
        at = pl.ds(pl.multiple_of(t * rows, 16), rows)
        low = qkv_low[at, :]
        return (
            mm(low[:, :q_width], w_query[...], NT)
            + mm(low[:, q_width : q_width + k_width], w_key[...], NT)
            + mm(low[:, q_width + k_width :], w_value[...], NT)
        )

    share_copies = []
    for m, other in enumerate(others):
        shares[m] = shares_of(other)
        slot = tensor_size - 2 - m
        c = pltpu.make_async_remote_copy(
            src_ref=shares.at[m], dst_ref=got_shares.at[slot], send_sem=share_send.at[m],
            recv_sem=share_recv.at[slot], device_id={"tensor": other}, device_id_type=MESH,
        )
        c.start()
        share_copies.append(c)
    normed_grad = shares_of(core)
    events_q.pop(0)()
    out_input[mine, :] = normed_grad
    for m, c in enumerate(share_copies):
        c.wait_send()
        slot = tensor_size - 2 - m
        pltpu.make_async_remote_copy(
            src_ref=shares.at[m], dst_ref=got_shares.at[slot], send_sem=share_send.at[m],
            recv_sem=share_recv.at[slot], device_id={"tensor": others[m]}, device_id_type=MESH,
        ).wait_recv()
        out_input[mine, :] += got_shares[slot]
    normed_grad = out_input[mine, :]
    inputs = hidden[...].astype(f32)
    r1 = scale_in[...]
    gained = gain[...] * normed_grad
    small_out[pl.ds(small_out.shape[0] - 1, 1), :] = jnp.sum(normed_grad * inputs * r1, axis=0, keepdims=True)
    out_input[mine, :] = (
        middle_grad[...]
        + r1 * gained
        - inputs * (r1 * r1 * r1) * jnp.mean(inputs * gained, axis=1, keepdims=True)
    )
    in_copies = []
    for m, other in enumerate(others):
        c = pltpu.make_async_remote_copy(
            src_ref=out_input.at[mine], dst_ref=out_input.at[mine], send_sem=in_send.at[m],
            recv_sem=in_recv.at[m], device_id={"tensor": other}, device_id_type=MESH,
        )
        c.start()
        in_copies.append(c)
    ways = [("dp", m) for m in masks] + [("tensor", m) for m in tensor_masks]
    small_copies = []

    def small_step(step):
        if step > 0:
            small_copies[-1].wait_send()
            small_copies[-1].wait_recv()
            small_out[...] += small_got[step - 1]
        if step < len(ways):
            axis, m = ways[step]
            device = {"dp": peer_of(m)[0]} if axis == "dp" else {"tensor": mate(m)}
            c = pltpu.make_async_remote_copy(
                src_ref=small_out, dst_ref=small_got.at[step], send_sem=small_send.at[step],
                recv_sem=small_recv.at[step], device_id=device, device_id_type=MESH,
            )
            c.start()
            small_copies.append(c)

    steps = len(ways) + 1
    done = 0
    while events_q:
        if done < steps:
            small_step(done)
            done += 1
        events_q.pop(0)()
    while done < steps:
        small_step(done)
        done += 1
    sum_o.finish()
    sum_q.finish()
    for c in in_copies:
        c.wait()


def attention_back(
    back, middle, scale_mid, routed, grad_top, picked, router, moe_gain,
    heads, q, k, v, w_out, w_query, w_key, w_value, normed, cosine, sine, seg,
    hidden, gain, scale_in, dp_size, tensor_size, collective_id,
):
    length, width = normed.shape
    small = jax.ShapeDtypeStruct(((dp_size + 2 + 7) // 8 * 8, width), f32)
    q_width, k_width = q.shape[1], k.shape[1]
    rows = hidden.shape[0]
    orders_o, groups_o = sum_orders(dp_size, width, 1)
    orders_q, groups_q = sum_orders(dp_size, width, 2)
    steps = len(bit_masks(dp_size))
    small_steps = steps + len(bit_masks(tensor_size))
    qkv_width = q_width + 2 * k_width
    others = tensor_size - 1
    vmem = pl.BlockSpec(memory_space=pltpu.VMEM)
    dma = pltpu.SemaphoreType.DMA
    return pl.pallas_call(
        functools.partial(
            attention_back_kernel, dp_size, tensor_size, orders_o, groups_o, orders_q, groups_q
        ),
        out_shape=[
            jax.ShapeDtypeStruct((width, q_width), bf16),
            jax.ShapeDtypeStruct((width, qkv_width), bf16),
            jax.ShapeDtypeStruct((length, width), f32),
            jax.ShapeDtypeStruct(small.shape, f32),
        ],
        in_specs=[vmem] * 24,
        out_specs=[vmem] * 4,
        scratch_shapes=[
            pltpu.VMEM((length, width), bf16),
            pltpu.VMEM((rows, width), f32),
            pltpu.VMEM((length, length), f32),
            pltpu.VMEM((length, q_width), bf16),
            pltpu.VMEM((length, qkv_width), bf16),
            pltpu.VMEM((length, q_width), f32),
            pltpu.VMEM((length, 128), f32),
            pltpu.VMEM((length, 128), f32),
            pltpu.VMEM((width, q_width), bf16),
            pltpu.VMEM((width, q_width), bf16),
            pltpu.VMEM((width, qkv_width), bf16),
            pltpu.VMEM((width, qkv_width), bf16),
            pltpu.VMEM((others, rows, width), f32),
            pltpu.VMEM((others, rows, width), f32),
            pltpu.VMEM((small_steps,) + small.shape, f32),
            dma((len(orders_o), 2 * steps)),
            dma((len(orders_o), 2 * steps)),
            dma((len(orders_q), 2 * steps)),
            dma((len(orders_q), 2 * steps)),
            dma((small_steps,)),
            dma((small_steps,)),
            dma((others,)),
            dma((others,)),
            dma((others,)),
            dma((others,)),
            dma((others,)),
            dma((others,)),
        ],
        compiler_params=pltpu.CompilerParams(
            collective_id=collective_id, has_side_effects=True, vmem_limit_bytes=60 << 20
        ),
    )(
        back, middle, scale_mid, routed, grad_top, picked, router, moe_gain[None],
        heads, q, k, v, w_out, w_query, w_key, w_value, normed, cosine, sine,
        seg[:, None], seg[None, :], hidden, gain[None], scale_in,
    )


def dot(a, b, spec):
    return jnp.einsum(spec, a, b, preferred_element_type=f32)


def per_device(
    hidden_in,
    attn_gain,
    w_query,
    key_weight,
    value_weight,
    w_output,
    moe_gain,
    w_router,
    w_gate,
    w_up,
    w_down,
    expert_ids,
    segment_ids,
    out_grad,
):
    tokens_here, model_width = hidden_in.shape
    head_size = HEAD_DIM
    dp_size = lax.axis_size("dp")
    tensor_size = lax.axis_size("tensor")
    experts = dp_size
    tensor_index = lax.axis_index("tensor")
    masks = bit_masks(dp_size)
    tensor_masks = bit_masks(tensor_size)
    tensor_down = tensor_masks[::-1]
    rows_here = tokens_here // tensor_size
    groups = [list(range(pair, dp_size, 2)) for pair in range(2)]

    def my_rows(x):
        return lax.dynamic_slice_in_dim(x, tensor_index * rows_here, rows_here, 0)

    block = w_gate.shape[2] // tensor_size

    def my_units(x, dim):
        return lax.dynamic_slice_in_dim(x, tensor_index * block, block, dim)

    def relative_gather(x, dim):
        for mask in tensor_masks:
            x = jnp.concatenate([x, swap(x, "tensor", mask)], dim)
        return x

    def relative_scatter(x, dim):
        for mask in reversed(tensor_masks):
            half = x.shape[dim] // 2
            keep = lax.slice_in_dim(x, 0, half, axis=dim)
            give = lax.slice_in_dim(x, half, 2 * half, axis=dim)
            x = keep.astype(f32) + swap(give.astype(bf16), "tensor", mask).astype(f32)
        return x

    far_set = [
        relative_gather(swap(my_units(w_gate[0], 1), "dp", 1), 1),
        relative_gather(swap(my_units(w_up[0], 1), "dp", 1), 1),
        relative_gather(swap(my_units(w_down[0], 0), "dp", 1), 0),
    ]
    grad_mine = my_rows(out_grad)
    lanes = jnp.arange(LANES, dtype=jnp.int32)
    picked_mine = jnp.any(my_rows(expert_ids)[:, :, None] == lanes[None, None, :], axis=1)
    picked_low = picked_mine.astype(bf16)
    grads = lax.all_gather(
        jnp.concatenate([grad_mine, picked_low], 1),
        "dp",
        axis=0,
        tiled=True,
        axis_index_groups=groups,
    )
    router_wide = jnp.pad(w_router, ((0, 0), (0, LANES - experts)))

    inputs = hidden_in.astype(f32)
    scale_in = lax.rsqrt(jnp.mean(inputs * inputs, axis=-1, keepdims=True) + epsilon)
    normed_low = (inputs * scale_in * attn_gain).astype(bf16)
    segment = segment_ids[0]
    tables = rope_tables(segment, head_size)
    heads_flat, query_heads, key_heads, value_heads, log_sums = attend_forward(
        normed_low, segment, tables, w_query, key_weight, value_weight, head_size
    )
    attn_part = jnp.dot(heads_flat, w_output, preferred_element_type=f32)
    attn_total = scatter_sum(attn_part, "tensor", tensor_down, f32)

    inputs_mine = my_rows(hidden_in).astype(f32)
    scale_in_mine = my_rows(scale_in)
    middle = inputs_mine + residual_scale * attn_total
    scale_mid = lax.rsqrt(jnp.mean(middle * middle, axis=-1, keepdims=True) + epsilon)
    routed_low = (middle * scale_mid * moe_gain).astype(bf16)

    near_set = [w_gate[0], w_up[0], w_down[0]]
    moe_part, back, *expert_parts = experts_call(
        routed_low, grads, router_wide, near_set, far_set, dp_size, 0
    )
    moe_total = lax.psum_scatter(
        moe_part, "dp", scatter_dimension=0, tiled=True, axis_index_groups=groups
    )

    dims = (1, 1, 0)
    near_mine = [
        scatter_sum(x, "tensor", tensor_down, bf16, d) for x, d in zip(expert_parts[:3], dims)
    ]
    far_mine = [relative_scatter(x, d).astype(bf16) for x, d in zip(expert_parts[3:], dims)]
    back, far_mine = lax.optimization_barrier((back, far_mine))
    returning = [swap(x, "dp", 1) for x in far_mine]

    heads_width = heads_flat.shape[1]
    width_q, width_k = query_heads.shape[1] * head_size, key_heads.shape[1] * head_size
    qkv_width = width_q + 2 * width_k
    w_output_sum, qkv_grad, input_grad, small = attention_back(
        back,
        middle,
        scale_mid,
        routed_low,
        grad_mine,
        picked_low,
        router_wide,
        moe_gain,
        heads_flat,
        query_heads.reshape(tokens_here, -1),
        key_heads.reshape(tokens_here, -1),
        value_heads.reshape(tokens_here, -1),
        w_output,
        w_query,
        key_weight,
        value_weight,
        normed_low,
        jnp.tile(tables[0][:, 0, :], (1, 4)),
        jnp.tile(jnp.concatenate([-tables[1][:, 0, :], tables[1][:, 0, :]], 1), (1, 2)),
        segment,
        my_rows(hidden_in),
        attn_gain,
        scale_in_mine,
        dp_size,
        tensor_size,
        2,
    )
    w_output_sum, returning, moe_total = lax.optimization_barrier(
        (w_output_sum, returning, moe_total)
    )
    block_mine = (middle + residual_scale * moe_total.astype(f32)).astype(bf16)
    block_out = gather_blocks(block_mine, "tensor", tensor_down)
    expert_mine = [mine + away.astype(f32) for mine, away in zip(near_mine, returning)]
    if tensor_size == 2:
        expert_grads = place(expert_mine, [swap(x, "tensor", 1) for x in expert_mine], dims)
    else:
        expert_grads = [
            gather_blocks(x, "tensor", tensor_down, dim) for x, dim in zip(expert_mine, dims)
        ]
    w_output_sum, qkv_grad = w_output_sum.astype(f32), qkv_grad.astype(f32)
    w_output_grad = jnp.concatenate(
        [w_output_sum[i : i + heads_width] for i in range(0, model_width, heads_width)], 1
    )
    return (
        block_out,
        input_grad,
        small[-1],
        qkv_grad[:, :width_q],
        qkv_grad[:, width_q : width_q + width_k],
        qkv_grad[:, width_q + width_k : qkv_width],
        w_output_grad,
        small[experts],
        small[:experts].T,
        expert_grads[0][None],
        expert_grads[1][None],
        expert_grads[2][None],
    )


def solution(mesh):
    placed = (
        P("dp", None),
        P(),
        P(None, "tensor"),
        P(None, "tensor"),
        P(None, "tensor"),
        P("tensor", None),
        P(),
        P(),
        P("dp", None, None),
        P("dp", None, None),
        P("dp", None, None),
        P("dp", None),
        P("dp", None),
        P("dp", None),
    )
    return jax.shard_map(
        per_device,
        mesh=mesh,
        in_specs=placed,
        out_specs=(
            P("dp", None),
            P("dp", None),
            P(),
            P(None, "tensor"),
            P(None, "tensor"),
            P(None, "tensor"),
            P("tensor", None),
            P(),
            P(),
            P("dp", None, None),
            P("dp", None, None),
            P("dp", None, None),
        ),
        check_vma=False,
    )
```

```python
import functools

import jax
import jax.numpy as jnp
from jax import lax
from jax.experimental import pallas as pl
from jax.experimental.pallas import tpu as pltpu
from jax.sharding import PartitionSpec as P

HEAD_DIM = 64

bf16 = jnp.bfloat16
f32 = jnp.float32
MESH = pl.DeviceIdType.MESH
epsilon = 1e-06
residual_scale = 0.22
attn_scale = 0.015625
rope_base = 10000.0
masked_score = -1e30


def positions_of(segment):
    position_index = jnp.arange(segment.shape[0], dtype=jnp.int32)
    earlier = jnp.concatenate([segment[:1] - 1, segment[:-1]])
    starts = lax.cummax(jnp.where(segment != earlier, position_index, 0), axis=0)
    return position_index - starts


def rope_tables(segment, head_size):
    position = positions_of(segment).astype(f32)
    frequency = rope_base ** (-jnp.arange(head_size // 2, dtype=f32) * 2.0 / head_size)
    angle = position[:, None] * frequency[None, :]
    return (jnp.cos(angle)[:, None, :], jnp.sin(angle)[:, None, :])


def apply_rotation(heads_in, cosine_table, sine_values):
    middle_index = heads_in.shape[-1] // 2
    first_half = heads_in[..., :middle_index]
    second_half = heads_in[..., middle_index:]
    return jnp.concatenate(
        [
            first_half * cosine_table - second_half * sine_values,
            second_half * cosine_table + first_half * sine_values,
        ],
        axis=-1,
    )


def block_scores(query_heads, key_heads, segment):
    kv_count = key_heads.shape[1]
    length = query_heads.shape[0]
    grouped = query_heads.reshape(length, kv_count, -1, query_heads.shape[2])
    raw_scores = (
        jnp.einsum("qhgd,khd->hgqk", grouped, key_heads, preferred_element_type=f32) * attn_scale
    )
    index = jnp.arange(length, dtype=jnp.int32)
    allowed = (index[:, None] >= index[None, :]) & (segment[:, None] == segment[None, :])
    return (jnp.where(allowed, raw_scores, masked_score), grouped)


def attend_forward(normed, segment, tables, w_query, key_weight, value_weight, head_size):
    length = normed.shape[0]

    def heads(weight):
        return jnp.dot(normed, weight, preferred_element_type=f32).reshape(length, -1, head_size)

    query_heads = apply_rotation(heads(w_query), *tables).astype(bf16)
    key_heads = apply_rotation(heads(key_weight), *tables).astype(bf16)
    value_heads = heads(value_weight).astype(bf16)
    scores, _ = block_scores(query_heads, key_heads, segment)
    largest = jnp.max(scores, axis=-1, keepdims=True)
    weights_raw = jnp.exp(scores - largest)
    totals = jnp.sum(weights_raw, axis=-1, keepdims=True)
    probs_low = (weights_raw / totals).astype(bf16)
    head_out = jnp.einsum("hgqk,khd->qhgd", probs_low, value_heads, preferred_element_type=f32)
    return (
        head_out.reshape(length, -1).astype(bf16),
        query_heads,
        key_heads,
        value_heads,
        (largest + jnp.log(totals))[..., 0],
    )


def attend_backward(query_heads, key_heads, value_heads, log_sums, heads_grad, segment, tables):
    length = query_heads.shape[0]
    cosine_table, sine_values = tables
    scores, grouped = block_scores(query_heads, key_heads, segment)
    probability = jnp.exp(scores - log_sums[..., None])
    probs_low = probability.astype(bf16)
    grad_grouped = heads_grad.reshape(grouped.shape)
    prob_grad = jnp.einsum(
        "qhgd,khd->hgqk", grad_grouped, value_heads, preferred_element_type=f32
    )
    weighted = jnp.sum(probability * prob_grad, axis=-1, keepdims=True)
    score_low = (probability * (prob_grad - weighted)).astype(bf16)
    query_part = (
        jnp.einsum("hgqk,khd->qhgd", score_low, key_heads, preferred_element_type=f32) * attn_scale
    ).reshape(query_heads.shape)
    key_sum = (
        jnp.einsum("hgqk,qhgd->khd", score_low, grouped, preferred_element_type=f32) * attn_scale
    )
    value_sum = jnp.einsum(
        "hgqk,qhgd->khd", probs_low, grad_grouped, preferred_element_type=f32
    )
    query_low = apply_rotation(query_part, cosine_table, -sine_values).astype(bf16)
    key_low = apply_rotation(key_sum, cosine_table, -sine_values).astype(bf16)
    return (
        query_low.reshape(length, -1),
        key_low.reshape(length, -1),
        value_sum.astype(bf16).reshape(length, -1),
    )


def bit_masks(size):
    masks = []
    while size > 1:
        size //= 2
        masks.append(size)
    return masks[::-1]


def swap(x, axis, mask):
    return lax.ppermute(x, axis, [(i, i ^ mask) for i in range(lax.axis_size(axis))])


def bit_of(axis, mask):
    return (lax.axis_index(axis) // mask) % 2


def halves_by_bit(x, axis, mask, dim=0):
    half = x.shape[dim] // 2
    bit = bit_of(axis, mask)
    mine = lax.dynamic_slice_in_dim(x, bit * half, half, dim)
    other = lax.dynamic_slice_in_dim(x, (1 - bit) * half, half, dim)
    return mine, other


def join_by_bit(mine, other, axis, mask, dim=0):
    return jnp.where(
        bit_of(axis, mask) == 0,
        jnp.concatenate([mine, other], dim),
        jnp.concatenate([other, mine], dim),
    )


def scatter_sum(x, axis, masks, kind, dim=0):
    x = x.astype(f32)
    for mask in masks:
        mine, other = halves_by_bit(x, axis, mask, dim)
        x = mine + swap(other.astype(kind), axis, mask).astype(f32)
    return x


def gather_blocks(x, axis, masks, dim=0):
    for mask in reversed(masks):
        x = join_by_bit(x, swap(x, axis, mask), axis, mask, dim)
    return x


def rotated(masks, j):
    j = j % len(masks)
    return masks[j:] + masks[:j]


def peer_of(mask):
    me = lax.axis_index("dp")
    bit = (me // mask) % 2
    return me + mask * (1 - 2 * bit), bit


def greet(masks):
    barrier = pltpu.get_barrier_semaphore()
    for mask in masks:
        pl.semaphore_signal(
            barrier, inc=1, device_id={"dp": peer_of(mask)[0]}, device_id_type=MESH
        )
    pl.semaphore_wait(barrier, len(masks))


def remote(src, dst, send, recv, mask):
    return remote_to(src, dst, send, recv, peer_of(mask)[0])


def add_rows(dst, dst0, a, a0, b, b0, rows, out_dtype):
    step = 16

    def body(i, _):
        r = pl.multiple_of(i * step, step)
        x = a[pl.ds(a0 + r, step), :].astype(f32) + b[pl.ds(b0 + r, step), :].astype(f32)
        dst[pl.ds(dst0 + r, step), :] = x.astype(out_dtype)
        return 0

    lax.fori_loop(0, rows // step, body, 0)


def group_sizes(dp_size):
    a = 4
    return a, dp_size // (2 * a)


class Spot:
    def __init__(self, a, b):
        me = lax.axis_index("dp")
        self.a, self.b = a, b
        self.n = a * b
        self.me = me
        self.A = me // (2 * b)
        self.B = (me // 2) % b
        self.block = me // 2
        self.pair = me % 2
        self.devices = (me + 2 * b, me - 2 * b, me + 2, me - 2)
        self.exists = (self.A < a - 1, self.A > 0, self.B < b - 1, self.B > 0)
        self.some = me + 2 * (1 - 2 * (self.B % 2))

    def greet(self, further=()):
        barrier = pltpu.get_barrier_semaphore()
        for device in further:
            pl.semaphore_signal(barrier, inc=1, device_id=device, device_id_type=MESH)
        for device, there in zip(self.devices, self.exists):

            @pl.when(there)
            def _(device=device):
                pl.semaphore_signal(
                    barrier, inc=1, device_id={"dp": device}, device_id_type=MESH
                )

        a, b = self.a, self.b
        ups = 2 - (self.A + 1) // a - (self.B + 1) // b
        downs = (self.A + a - 1) // a + (self.B + b - 1) // b
        pl.semaphore_wait(barrier, ups + downs + len(further))


def xor4(x, y):
    return ((x // 2 + y // 2) % 2) * 2 + (x % 2 + y % 2) % 2


def is_at(x, value):
    return 1 // (1 + (x - value) * (x - value))


def by_distance(size, place, k):
    found = 0
    for p in range(size):
        order = sorted(range(size), key=lambda q: (abs(q - p), q))
        for j, q in enumerate(order):
            if q > 0:
                found = found + q * is_at(place, p) * is_at(k, j)
    return found


def visit_order(a, b):
    pairs = [(k, l) for k in range(a) for l in range(b)]
    return sorted(pairs, key=lambda kl: kl[0] + (2 * kl[1] + 0.5 if kl[1] else 0))


def remote_to(src, dst, send, recv, device):
    return pltpu.make_async_remote_copy(
        src_ref=src,
        dst_ref=dst,
        send_sem=send,
        recv_sem=recv,
        device_id={"dp": device},
        device_id_type=MESH,
    )


PIECES = 2
SUM_PIECES = 4


class LineGather:
    def __init__(self, spot, buf, rows, send, recv):
        self.spot, self.buf, self.rows, self.send, self.recv = spot, buf, rows, send, recv

    def coords(self, i):
        s = self.spot
        visits = visit_order(s.a, s.b)
        k = sum(v[0] * is_at(i, j) for j, v in enumerate(visits) if v[0])
        l = sum(v[1] * is_at(i, j) for j, v in enumerate(visits) if v[1])
        return by_distance(s.a, s.A, k), by_distance(s.b, s.B, l)

    def row0(self, i):
        A, B = self.coords(i)
        return pl.multiple_of((A * self.spot.b + B) * self.rows, 16)

    def copies(self, block, way, device):
        size = self.rows // PIECES
        return [
            remote_to(there, there, self.send.at[block, way, p], self.recv.at[block, p], device)
            for p in range(PIECES)
            for there in [self.buf.at[pl.ds(pl.multiple_of(block * self.rows + p * size, 16), size)]]
        ]

    def each_way(self, i, act):
        s = self.spot
        A, B = self.coords(i)
        block = A * s.b + B
        same = B == s.B
        conditions = (
            same & (A <= s.A) & s.exists[0],
            same & (A >= s.A) & s.exists[1],
            (B <= s.B) & s.exists[2],
            (B >= s.B) & s.exists[3],
        )
        for way, (condition, device) in enumerate(zip(conditions, s.devices)):

            @pl.when(condition)
            def _(way=way, device=device):
                for c in self.copies(block, way, device):
                    act(c)

    def wait(self, i):
        A, B = self.coords(i)
        for c in self.copies(A * self.spot.b + B, 0, self.spot.some):
            c.wait_recv()

    def forward(self, i):
        self.each_way(i, lambda c: c.start())

    def finish(self):
        def one(i, _):
            self.each_way(i, lambda c: c.wait_send())
            return 0

        lax.fori_loop(0, self.spot.n, one, 0)


def add_into(dst, d0, src, s0, rows, step=16):
    def body(i, _):
        r = pl.multiple_of(i * step, step)
        total = dst[pl.ds(d0 + r, step), :].astype(f32) + src[pl.ds(s0 + r, step), :].astype(f32)
        dst[pl.ds(d0 + r, step), :] = total.astype(dst.dtype)
        return 0

    lax.fori_loop(0, rows // step, body, 0)


class LineSum:
    def __init__(self, size, place, up, down, part, row_of, rows, got, send, recv, some):
        self.size, self.place, self.up, self.down = size, place, up, down
        self.part, self.row_of, self.rows, self.got = part, row_of, rows, got
        self.send, self.recv, self.some = send, recv, some

    def up_slot(self, place, c):
        return c - place

    def down_slot(self, place, c):
        return c + (self.size - place) * ((place + self.size - 1) // self.size)

    def copies(self, c, slot, send, device):
        size = self.rows // SUM_PIECES
        return [
            remote_to(
                self.part.at[pl.ds(pl.multiple_of(self.row_of(c) + p * size, 16), size)],
                self.got.at[pl.ds(pl.multiple_of(slot * self.rows + p * size, 16), size)],
                send.at[p],
                self.recv.at[slot, p],
                device,
            )
            for p in range(SUM_PIECES)
        ]

    def take(self, c, slot, p, dst=None, d0=None):
        if dst is None:
            dst, d0 = self.part, self.row_of(c)
        size = self.rows // SUM_PIECES
        self.copies(c, slot, self.send.at[0, 0], self.some)[p].wait_recv()
        from_row = pl.multiple_of(slot * self.rows + p * size, 16)
        add_into(dst, d0 + p * size, self.got, from_row, size)

    def up_copies(self, k):
        c = self.size - 1 - k
        return self.copies(c, self.up_slot(self.place + 1, c), self.send.at[k, 0], self.up)

    def down_copies(self, k):
        return self.copies(k, self.down_slot(self.place - 1, k), self.send.at[k, 1], self.down)

    def step_up(self, k):
        c = self.size - 1 - k

        @pl.when(c > self.place)
        def _():
            for p, copy in enumerate(self.up_copies(k)):

                @pl.when(self.place > 0)
                def _(p=p):
                    self.take(c, self.up_slot(self.place, c), p)

                copy.start()

    def step_down(self, k):
        @pl.when(k < self.place)
        def _():
            for p, copy in enumerate(self.down_copies(k)):

                @pl.when(self.place < self.size - 1)
                def _(p=p):
                    self.take(k, self.down_slot(self.place, k), p)

                copy.start()

    def step(self, k):
        self.step_up(k)
        self.step_down(k)

    def end(self, out=None):
        p = self.place
        d0 = None
        if out is not None:
            out[...] = self.part[pl.ds(self.row_of(p), self.rows), :].astype(out.dtype)
            d0 = 0

        @pl.when(p > 0)
        def _():
            for j in range(SUM_PIECES):
                self.take(p, self.up_slot(p, p), j, out, d0)

        @pl.when(p < self.size - 1)
        def _():
            for j in range(SUM_PIECES):
                self.take(p, self.down_slot(p, p), j, out, d0)

        for k in range(self.size - 1):

            @pl.when(self.size - 1 - k > p)
            def _(k=k):
                for c in self.up_copies(k):
                    c.wait_send()

            @pl.when(k < p)
            def _(k=k):
                for c in self.down_copies(k):
                    c.wait_send()


def slots_of(size):
    return 1 if size == 2 else size + 1


class GroupSum:
    def __init__(self, spot, part, rows, got_b, got_a, send_b, recv_b, send_a, recv_a):
        self.spot, self.part, self.rows = spot, part, rows
        a, b = spot.a, spot.b
        slots_b = slots_of(b)

        def b_line(A):
            return LineSum(
                b, spot.B, spot.devices[2], spot.devices[3], part,
                lambda B: pl.multiple_of((A * b + B) * rows, 16), rows,
                got_b.at[pl.ds(pl.multiple_of(A * slots_b * rows, 16), slots_b * rows)],
                send_b.at[A], recv_b.at[A], spot.some,
            )

        self.b_line = b_line
        self.a_line = LineSum(
            a, spot.A, spot.devices[0], spot.devices[1], part,
            lambda A: pl.multiple_of((A * b + spot.B) * rows, 16), rows,
            got_a, send_a, recv_a, spot.some,
        )

    def ready(self, A, B):
        if self.spot.b == 2:
            line = self.b_line(A)

            @pl.when(B != self.spot.B)
            def _():
                line.step(0)

    def along_b(self):
        if self.spot.b > 2:

            def one(A, _):
                for k in range(self.spot.b - 1):
                    self.b_line(A).step(k)
                return 0

            lax.fori_loop(0, self.spot.a, one, 0)

    def flow(self, fills):
        a, line = self.spot.a, self.a_line
        fills = list(fills)

        def fill():
            if fills:
                fills.pop(0)()

        for k in range(a - 1):
            if 2 * k < a:
                self.b_line(a - 1 - k).end()
            line.step_up(k)
            fill()
            if 2 * k < a and a - 1 - k != k:
                self.b_line(k).end()
            line.step_down(k)
            fill()
        while fills:
            fill()

    def order(self, j):
        a = self.spot.a
        places = sorted(range(a), key=lambda c: (min(c, a - 1 - c), -c))
        return sum(c * is_at(j, i) for i, c in enumerate(places) if c)

    def steps_a(self):
        return self.spot.a - 1

    @staticmethod
    def scratch(a, b, rows, width):
        return [
            pltpu.VMEM((a * slots_of(b) * rows, width), bf16),
            pltpu.VMEM((slots_of(a) * rows, width), bf16),
            pltpu.SemaphoreType.DMA((a, b - 1, 2, SUM_PIECES)),
            pltpu.SemaphoreType.DMA((a, slots_of(b), SUM_PIECES)),
            pltpu.SemaphoreType.DMA((a - 1, 2, SUM_PIECES)),
            pltpu.SemaphoreType.DMA((slots_of(a), SUM_PIECES)),
        ]


LANES = 128
LOW_AT = 64


def mm(x, y, dims):
    return lax.dot_general(x, y, (dims, ((), ())), preferred_element_type=f32)


NN, NT, TN = ((1,), (0,)), ((1,), (1,)), ((0,), (0,))


def experts_kernel(
    a, b, rows, width, cores,
    x_ref, grads_ref, router_ref, near_gate, near_up, near_down, far_gate, far_up, far_down,
    moe_ref, out_ref, o_near_gate, o_near_up, o_near_down, o_far_gate, o_far_up, o_far_down,
    xs, gs, weights, downs, lows, part, extras, stage, got_wide, got_down,
    local, load, send, recv, stage_sem, store, core_send, core_recv, *scratch,
):
    spot = Spot(a, b)
    n = spot.n
    gather = LineGather(spot, xs, rows, send, recv)
    total = GroupSum(spot, part, rows, *scratch)
    mine = pltpu.make_async_copy(
        x_ref, xs.at[pl.ds(pl.multiple_of(spot.block * rows, 16), rows)], local.at[0]
    )
    mine.start()
    sources = (near_gate, near_up, far_gate, far_up)
    arriving = [
        pltpu.make_async_copy(src, weights.at[k], local.at[1 + k]) for k, src in enumerate(sources)
    ] + [
        pltpu.make_async_copy(src, downs.at[k], local.at[5 + k])
        for k, src in enumerate((near_down, far_down))
    ]

    def grads_copy(i):
        at = pl.ds(gather.row0(i), rows)
        return pltpu.make_async_copy(grads_ref.at[at], gs.at[at], load.at[i])

    grads_copy(0).start()
    for c in arriving:
        c.start()
    for i in range(1, n):
        grads_copy(i).start()
    core = lax.axis_index("tensor")
    mates = [xor4(core, m) for m in range(1, cores)]
    spot.greet([{"tensor": mate} for mate in mates])
    mine.wait()
    gather.forward(0)
    for c in arriving:
        c.wait()
    lane = lax.broadcasted_iota(jnp.int32, (rows, LANES), 1)
    near, far = spot.me, spot.me + 1 - 2 * spot.pair

    def block(i, _):
        at = pl.ds(gather.row0(i), rows)
        grads_copy(i).wait()
        x = xs[at, :]
        chosen = gs[at, pl.ds(width, LANES)] > 0
        logits = jnp.where(chosen, mm(x, router_ref[...], NN), masked_score)
        raised = jnp.where(chosen, jnp.exp(logits - jnp.max(logits, axis=1, keepdims=True)), 0.0)
        gates = raised / jnp.sum(raised, axis=1, keepdims=True)
        extra = jnp.zeros((rows, LANES), f32)
        for e, expert in enumerate((near, far)):
            if e == 1:

                @pl.when(i + 1 < n)
                def _():
                    gather.wait(i + 1)
                    gather.forward(i + 1)

            column = jnp.sum(jnp.where(lane == expert, gates, 0.0), axis=1, keepdims=True)
            x = xs[at, :]
            gate_act = mm(x, weights[2 * e], NN)
            up_act = mm(x, weights[2 * e + 1], NN)
            down_in = residual_scale * mm(gs[at, pl.ds(0, width)], downs[e], NT)
            sigmoid_gate = jax.nn.sigmoid(gate_act)
            silu_gate = gate_act * sigmoid_gate
            hidden = silu_gate * up_act
            deriv = jnp.sum(hidden * down_in, axis=1, keepdims=True)
            high = deriv.astype(bf16).astype(f32)
            extra += jnp.where(lane == expert, high, 0.0)
            extra += jnp.where(lane == expert + LOW_AT, deriv - high, 0.0)
            down_in = down_in * column
            lows[3 * e, at, :] = (hidden * column).astype(bf16)
            lows[3 * e + 1, at, :] = (
                down_in * up_act * sigmoid_gate * (1.0 + gate_act * (1.0 - sigmoid_gate))
            ).astype(bf16)
            lows[3 * e + 2, at, :] = (down_in * silu_gate).astype(bf16)

        extras[at, :] = extra.astype(bf16)
        return 0

    lax.fori_loop(0, n, block, 0)

    def rows_of(A, B):
        return pl.ds(pl.multiple_of((A * b + B) * rows, 16), rows)

    def back_block(A, B):
        at = rows_of(A, B)
        back = mm(lows[1, at, :], weights[0], NT) + mm(lows[2, at, :], weights[1], NT)
        back += mm(lows[4, at, :], weights[2], NT) + mm(lows[5, at, :], weights[3], NT)
        part[at, pl.ds(0, width)] = back.astype(bf16)
        part[at, pl.ds(width, LANES)] = extras[at, :]
        total.ready(A, B)

    def back_others(i, _):
        A = total.order(i // (b - 1))
        B = by_distance(b, spot.B, 1 + i % (b - 1))
        back_block(A, B)
        return 0

    def back_own(i, _):
        back_block(total.order(i), spot.B)
        return 0

    def stage_copy(i):
        at = pl.ds(pl.multiple_of(i * rows, 16), rows)
        return pltpu.make_async_copy(stage.at[i % 2], moe_ref.at[at], stage_sem.at[i % 2])

    def moe_block(i, _):
        at = pl.ds(pl.multiple_of(i * rows, 16), rows)

        @pl.when(i >= 2)
        def _():
            stage_copy(i - 2).wait()

        stage[i % 2] = (mm(lows[0, at, :], downs[0], NN) + mm(lows[3, at, :], downs[1], NN)).astype(
            bf16
        )
        stage_copy(i).start()
        return 0

    lax.fori_loop(0, a * (b - 1), back_others, 0)
    lax.fori_loop(0, 2, back_own, 0)
    if b > 2:
        lax.fori_loop(2, a, back_own, 0)
    total.along_b()
    tile = 256

    def weight_grads(e):
        def wide(k, _):
            at = pl.ds(pl.multiple_of(k * tile, tile), tile)
            x = xs[:, at]
            weights[2 * e, at, :] = mm(x, lows[3 * e + 1], TN).astype(bf16)
            weights[2 * e + 1, at, :] = mm(x, lows[3 * e + 2], TN).astype(bf16)
            downs[e, :, at] = (residual_scale * mm(lows[3 * e], gs[:, at], TN)).astype(bf16)
            return 0

        lax.fori_loop(0, width // tile, wide, 0)
        give(e)

    units = lows.shape[2] // cores

    def blocks(e, k):
        at = pl.ds(pl.multiple_of(k * units, units), units)
        return (weights.at[2 * e, :, at], weights.at[2 * e + 1, :, at], downs.at[e, at, :])

    def own(e):
        return blocks(e, core if e == 0 else 0)

    def gifts(e):
        copies = []
        for m, mate in enumerate(mates):
            landing = (got_wide.at[e, m, 0], got_wide.at[e, m, 1], got_down.at[e, m])
            for i, (src, dst) in enumerate(zip(blocks(e, mate if e == 0 else m + 1), landing)):
                copies.append(
                    pltpu.make_async_remote_copy(
                        src_ref=src,
                        dst_ref=dst,
                        send_sem=core_send.at[e, m, i],
                        recv_sem=core_recv.at[e, m, i],
                        device_id={"tensor": mate},
                        device_id_type=MESH,
                    )
                )
        return copies

    def give(e):
        for c in gifts(e):
            c.start()

    def collect(e):
        for c in gifts(e):
            c.wait()
        outs = (o_near_gate, o_near_up, o_near_down) if e == 0 else (o_far_gate, o_far_up, o_far_down)
        for i, (view, out) in enumerate(zip(own(e), outs)):

            def chunk(k, _, i=i, view=view):
                size = view.shape[0] // 8
                at = pl.ds(pl.multiple_of(k * size, 16), size)
                total = view[at, :].astype(f32)
                for m in range(len(mates)):
                    got = got_wide[e, m, i, at, :] if i < 2 else got_down[e, m, at, :]
                    total += got.astype(f32)
                view[at, :] = total.astype(bf16)
                return 0

            lax.fori_loop(0, 8, chunk, 0)
            c = pltpu.make_async_copy(view, out, store.at[3 * e + i])
            c.start()
            stored.append(c)

    stored = []

    def moe_all():
        lax.fori_loop(0, n, moe_block, 0)

    total.flow(
        [
            (lambda: lax.fori_loop(2, a, back_own, 0)) if b == 2 else (lambda: None),
            moe_all,
            lambda: weight_grads(1),
            lambda: weight_grads(0),
            lambda: collect(1),
            lambda: collect(0),
        ]
    )
    line = total.a_line
    line.end(out_ref)
    gather.finish()
    stage_copy(n - 2).wait()
    stage_copy(n - 1).wait()
    for c in stored:
        c.wait()


def experts_call(rows_low, grads, router, near, far, dp_size, cores, collective_id):
    a, b = group_sizes(dp_size)
    n = a * b
    rows, width = rows_low.shape
    units = near[0].shape[1]
    hbm, vmem = pl.BlockSpec(memory_space=pl.ANY), pl.BlockSpec(memory_space=pltpu.VMEM)
    outs = [
        jax.ShapeDtypeStruct((n * rows, width), bf16),
        jax.ShapeDtypeStruct((rows, width + LANES), f32),
    ] + [
        jax.ShapeDtypeStruct(shape, bf16)
        for shape in 2 * [(width, units // cores), (width, units // cores), (units // cores, width)]
    ]
    return pl.pallas_call(
        functools.partial(experts_kernel, a, b, rows, width, cores),
        out_shape=outs,
        in_specs=[hbm, hbm, vmem] + [hbm] * 6,
        out_specs=[hbm, vmem] + [hbm] * 6,
        scratch_shapes=[
            pltpu.VMEM((n * rows, width), bf16),
            pltpu.VMEM((n * rows, width + LANES), bf16),
            pltpu.VMEM((4, width, units), bf16),
            pltpu.VMEM((2, units, width), bf16),
            pltpu.VMEM((6, n * rows, units), bf16),
            pltpu.VMEM((n * rows, width + LANES), bf16),
            pltpu.VMEM((n * rows, LANES), bf16),
            pltpu.VMEM((2, rows, width), bf16),
            pltpu.VMEM((2, cores - 1, 2, width, units // cores), bf16),
            pltpu.VMEM((2, cores - 1, units // cores, width), bf16),
            pltpu.SemaphoreType.DMA((7,)),
            pltpu.SemaphoreType.DMA((n,)),
            pltpu.SemaphoreType.DMA((n, 4, PIECES)),
            pltpu.SemaphoreType.DMA((n, PIECES)),
            pltpu.SemaphoreType.DMA((2,)),
            pltpu.SemaphoreType.DMA((6,)),
            pltpu.SemaphoreType.DMA((2, cores - 1, 3)),
            pltpu.SemaphoreType.DMA((2, cores - 1, 3)),
        ]
        + GroupSum.scratch(a, b, rows, width + LANES),
        compiler_params=pltpu.CompilerParams(
            collective_id=collective_id, has_side_effects=True, vmem_limit_bytes=62 << 20
        ),
    )(rows_low, grads, router, *near, *far)


def reduce_schedule(steps, groups):
    sums = [("sum", s) for s in range(steps)]
    backs = [("back", s) for s in reversed(range(steps))]
    lines = [[(g,) + e for e in sums + backs] for g in range(groups)]
    if groups == 1:
        return lines[0]
    first, second = lines
    order = first[: steps - 1]
    first = first[steps - 1 :]
    while first or second:
        if second:
            order.append(second.pop(0))
        if first:
            order.append(first.pop(0))
    return order


def place_kernel(dims, *refs):
    n = len(dims)
    mine, other, outs = refs[:n], refs[n : 2 * n], refs[2 * n : 3 * n]
    bufs, sems, out_sems = refs[3 * n : 4 * n], refs[4 * n], refs[4 * n + 1]
    me = lax.axis_index("tensor")

    def copy(i, which, src):
        size = src.shape[dims[i]]
        at = pl.multiple_of((me + which - 2 * which * me) * size, size)
        window = (slice(None),) * dims[i] + (pl.ds(at, size),)
        return pltpu.make_async_copy(src, bufs[i].at[window], sems.at[i, which])

    copies = [[copy(i, w, src) for w, src in enumerate((mine[i], other[i]))] for i in range(n)]
    for pair in copies:
        for c in pair:
            c.start()
    back = []
    for i, pair in enumerate(copies):
        for c in pair:
            c.wait()
        c = pltpu.make_async_copy(bufs[i], outs[i], out_sems.at[i])
        c.start()
        back.append(c)
    for c in back:
        c.wait()


def place(mine, other, dims):
    n = len(dims)
    shapes = [x.shape[:d] + (2 * x.shape[d],) + x.shape[d + 1 :] for x, d in zip(mine, dims)]
    return pl.pallas_call(
        functools.partial(place_kernel, dims),
        out_shape=[jax.ShapeDtypeStruct(s, x.dtype) for x, s in zip(mine, shapes)],
        in_specs=[pl.BlockSpec(memory_space=pl.ANY)] * (2 * n),
        out_specs=[pl.BlockSpec(memory_space=pl.ANY)] * n,
        scratch_shapes=[pltpu.VMEM(s, x.dtype) for x, s in zip(mine, shapes)]
        + [pltpu.SemaphoreType.DMA((n, 2)), pltpu.SemaphoreType.DMA((n,))],
        compiler_params=pltpu.CompilerParams(vmem_limit_bytes=24 << 20),
    )(*mine, *other)


class AllReduce:
    def __init__(self, orders, groups, acc, got, out, send, recv):
        self.orders, self.groups = orders, groups
        self.acc, self.got, self.out, self.send, self.recv = acc, got, out, send, recv
        self.k = len(orders[0])
        self.size = acc.shape[0] // len(orders)
        self.where = [j * self.size for j in range(len(orders))]
        self.sums, self.backs = {}, {}

    def sum_step(self, j, step):
        count = self.size >> (step + 1)
        mask = self.orders[j][step]
        _, bit = peer_of(mask)
        keep = pl.multiple_of(self.where[j] + bit * count, 16)
        give = pl.multiple_of(self.where[j] + (1 - bit) * count, 16)
        acc, got = self.acc, self.got
        if step > 0:
            self.sums[j, step - 1].wait_recv()
            p0 = j * self.size + (self.size - (self.size >> (step - 1)))
            add_rows(acc, give, acc, give, got, p0 + pl.multiple_of((1 - bit) * count, 16), count, bf16)
        g0 = j * self.size + (self.size - (self.size >> step))
        c = remote(
            acc.at[pl.ds(give, count)],
            got.at[pl.ds(g0, count)],
            self.send.at[j, step],
            self.recv.at[j, step],
            mask,
        )
        c.start()
        self.sums[j, step] = c
        if step > 0:
            add_rows(acc, keep, acc, keep, got, p0 + pl.multiple_of(bit * count, 16), count, bf16)
        self.where[j] = keep

    def back_step(self, j, step):
        count = self.size >> (step + 1)
        mask = self.orders[j][step]
        _, bit = peer_of(mask)
        here = self.where[j]
        if step == self.k - 1:
            self.sums[j, step].wait_recv()
            p0 = j * self.size + (self.size - (self.size >> step))
            add_rows(self.out, here, self.acc, here, self.got, p0, count, bf16)
        else:
            self.backs[j, step + 1].wait_recv()
        there = self.out.at[pl.ds(here, count)]
        c = remote(
            there, there, self.send.at[j, self.k + step], self.recv.at[j, self.k + step], mask
        )
        c.start()
        self.backs[j, step] = c
        self.where[j] = pl.multiple_of(here - bit * count, 16)

    def events(self):
        per_group = len(self.orders) // self.groups

        def event(g, kind, step):
            for j in range(g * per_group, (g + 1) * per_group):
                (self.sum_step if kind == "sum" else self.back_step)(j, step)

        return [
            functools.partial(event, *e) for e in reduce_schedule(self.k, self.groups)
        ]

    def finish(self):
        for j in range(len(self.orders)):
            self.backs[j, 0].wait_recv()
        for c in list(self.sums.values()) + list(self.backs.values()):
            c.wait_send()


def sum_orders(dp_size, rows, most):
    masks = bit_masks(dp_size)
    groups = most if rows % (3 * most * 16 * dp_size) == 0 else 1
    return [rotated(masks[:-1], j) + masks[-1:] for j in range(3 * groups)], groups


def turn(x, cosine, sine):
    lane = lax.broadcasted_iota(jnp.int32, x.shape, 1)
    swapped = jnp.where(lane % HEAD_DIM < HEAD_DIM // 2, pltpu.roll(x, 128 - 32, 1), pltpu.roll(x, 32, 1))
    return x * cosine + swapped * sine


def mask_bias(bias, seg_col, seg_row):
    length = bias.shape[0]
    row = lax.broadcasted_iota(jnp.int32, bias.shape, 0)
    col = lax.broadcasted_iota(jnp.int32, bias.shape, 1)
    allowed = (row >= col) & (seg_col[...] == seg_row[...])
    bias[...] = jnp.where(allowed, 0.0, masked_score)


def attention_back_kernel(
    dp_size, tensor_size, orders_o, groups_o, orders_q, groups_q,
    back, middle, scale_mid, routed, grad_top, picked, router, moe_gain,
    heads, q_ref, k_ref, v_ref, w_out, w_query, w_key, w_value, normed, cosine, sine,
    seg_col, seg_row, hidden, gain, scale_in,
    out_o, out_q, out_input, small_out,
    branch, middle_grad, bias, heads_grad, qkv_low, scratch_q, scratch_k, scratch_v,
    acc_o, got_o, acc_q, got_q, shares, got_shares, small_got,
    send_o, recv_o, send_q, recv_q, small_send, small_recv, share_send, share_recv, in_send, in_recv, branch_send, branch_recv,
):
    length, width = normed.shape
    q_width, k_width = q_ref.shape[1], k_ref.shape[1]
    rows = hidden.shape[0]
    per_kv = q_width // k_width
    core = lax.axis_index("tensor")
    tensor_masks = bit_masks(tensor_size)

    def mate(m):
        bit = (core // m) % 2
        return core + m * (1 - 2 * bit)

    barrier = pltpu.get_barrier_semaphore()
    masks = bit_masks(dp_size)
    others = [(core + m) % tensor_size for m in range(1, tensor_size)]
    for mask in masks:
        pl.semaphore_signal(
            barrier, inc=1, device_id={"dp": peer_of(mask)[0]}, device_id_type=MESH
        )
    for other in others:
        pl.semaphore_signal(barrier, inc=1, device_id={"tensor": other}, device_id_type=MESH)
    mine = pl.ds(pl.multiple_of(core * rows, 16), rows)
    experts = dp_size
    x = routed[...]
    chosen = picked[...] > 0
    logits = jnp.where(chosen, mm(x, router[...], NN), masked_score)
    raised = jnp.where(chosen, jnp.exp(logits - jnp.max(logits, axis=1, keepdims=True)), 0.0)
    gates = raised / jnp.sum(raised, axis=1, keepdims=True)
    derivs = back[:, pl.ds(width, LANES)]
    derivs = jnp.where(chosen, derivs + pltpu.roll(derivs, LANES - LOW_AT, 1), 0.0)
    logit_grad = (
        gates * (derivs - jnp.sum(gates * derivs, axis=1, keepdims=True))
    ).astype(bf16)
    small_out[...] = jnp.zeros(small_out.shape, f32)
    small_out[pl.ds(0, experts), :] = mm(logit_grad, x, TN)[:experts]
    routed_grad = back[:, pl.ds(0, width)] + mm(logit_grad, router[...], NT)
    mid = middle[...]
    r2 = scale_mid[...]
    small_out[pl.ds(experts, 1), :] = jnp.sum(routed_grad * mid * r2, axis=0, keepdims=True)
    gained = moe_gain[...] * routed_grad
    middle_grad[...] = (
        grad_top[...].astype(f32)
        + r2 * gained
        - mid * (r2 * r2 * r2) * jnp.mean(mid * gained, axis=1, keepdims=True)
    )
    branch[mine, :] = (residual_scale * middle_grad[...]).astype(bf16)
    pl.semaphore_wait(barrier, len(masks) + len(others))
    branch_copies = []
    for m, other in enumerate(others):
        c = pltpu.make_async_remote_copy(
            src_ref=branch.at[mine], dst_ref=branch.at[mine], send_sem=branch_send.at[m],
            recv_sem=branch_recv.at[m], device_id={"tensor": other}, device_id_type=MESH,
        )
        c.start()
        branch_copies.append(c)
    mask_bias(bias, seg_col, seg_row)
    for c in branch_copies:
        c.wait()
    for i in range(width // q_width):
        at = pl.ds(i * q_width, q_width)
        acc_o[at, :] = mm(heads[...], branch[:, at], TN).astype(bf16)
    sum_o = AllReduce(orders_o, groups_o, acc_o, got_o, out_o, send_o, recv_o)
    events_o = sum_o.events()
    events_o.pop(0)()
    heads_grad[...] = mm(branch[...], w_out[...], NT).astype(bf16)
    half = length // 2
    spans = ((0, half, half), (half, half, length))
    count = 0
    for pair in range(k_width // 128):
        k_tile = k_ref[:, pair * 128 : pair * 128 + 128]
        v_tile = v_ref[:, pair * 128 : pair * 128 + 128]
        for g in range(2):
            kg = k_tile[:, g * HEAD_DIM : (g + 1) * HEAD_DIM]
            vg = v_tile[:, g * HEAD_DIM : (g + 1) * HEAD_DIM]
            side = pl.ds(g * HEAD_DIM, HEAD_DIM)
            for h in range(per_kv):
                head = (pair * 2 + g) * per_kv + h
                lanes = pl.ds(head * HEAD_DIM, HEAD_DIM)
                for start, size, cols in spans:
                    at = pl.ds(start, size)
                    qh = q_ref[at, lanes]
                    oh = heads_grad[at, lanes]
                    scores = mm(qh, kg[:cols], NT) * attn_scale + bias[at, pl.ds(0, cols)]
                    raised = jnp.exp(scores - jnp.max(scores, axis=1, keepdims=True))
                    probability = raised * (1.0 / jnp.sum(raised, axis=1, keepdims=True))
                    prob_grad = mm(oh, vg[:cols], NT)
                    weighted = jnp.sum(probability * prob_grad, axis=1, keepdims=True)
                    score_low = (probability * (prob_grad - weighted)).astype(bf16)
                    probs_low = probability.astype(bf16)
                    scratch_q[at, lanes] = mm(score_low, kg[:cols], NN) * attn_scale
                    dk = mm(score_low, qh, TN) * attn_scale
                    dv = mm(probs_low, oh, TN)
                    upto = pl.ds(0, cols)
                    if h == 0 and start == 0:
                        scratch_k[upto, side] = dk
                        scratch_v[upto, side] = dv
                        scratch_k[pl.ds(cols, length - cols), side] = jnp.zeros((length - cols, HEAD_DIM), f32)
                        scratch_v[pl.ds(cols, length - cols), side] = jnp.zeros((length - cols, HEAD_DIM), f32)
                    else:
                        scratch_k[upto, side] += dk
                        scratch_v[upto, side] += dv
                count += 1
                if count % 2 == 0 and len(events_o) > 1:
                    events_o.pop(0)()
        at = pl.ds(q_width + pair * 128, 128)
        qkv_low[:, at] = turn(scratch_k[...], cosine[...], -sine[...]).astype(bf16)
        at = pl.ds(q_width + k_width + pair * 128, 128)
        qkv_low[:, at] = scratch_v[...].astype(bf16)
    for i in range(q_width // 128):
        at = pl.ds(i * 128, 128)
        qkv_low[:, at] = turn(scratch_q[:, at], cosine[...], -sine[...]).astype(bf16)
    chunk = width // len(orders_q)
    for i in range(len(orders_q)):
        at = pl.ds(i * chunk, chunk)
        acc_q[at, :] = mm(normed[:, at], qkv_low[...], TN).astype(bf16)
    sum_q = AllReduce(orders_q, groups_q, acc_q, got_q, out_q, send_q, recv_q)
    events_q = sum_q.events()
    events_q.pop(0)()
    while events_o:
        events_o.pop(0)()

    def shares_of(t):
        at = pl.ds(pl.multiple_of(t * rows, 16), rows)
        low = qkv_low[at, :]
        return (
            mm(low[:, :q_width], w_query[...], NT)
            + mm(low[:, q_width : q_width + k_width], w_key[...], NT)
            + mm(low[:, q_width + k_width :], w_value[...], NT)
        )

    share_copies = []
    for m, other in enumerate(others):
        shares[m] = shares_of(other)
        slot = tensor_size - 2 - m
        c = pltpu.make_async_remote_copy(
            src_ref=shares.at[m], dst_ref=got_shares.at[slot], send_sem=share_send.at[m],
            recv_sem=share_recv.at[slot], device_id={"tensor": other}, device_id_type=MESH,
        )
        c.start()
        share_copies.append(c)
    normed_grad = shares_of(core)
    events_q.pop(0)()
    out_input[mine, :] = normed_grad
    for m, c in enumerate(share_copies):
        c.wait_send()
        slot = tensor_size - 2 - m
        pltpu.make_async_remote_copy(
            src_ref=shares.at[m], dst_ref=got_shares.at[slot], send_sem=share_send.at[m],
            recv_sem=share_recv.at[slot], device_id={"tensor": others[m]}, device_id_type=MESH,
        ).wait_recv()
        out_input[mine, :] += got_shares[slot]
    normed_grad = out_input[mine, :]
    inputs = hidden[...].astype(f32)
    r1 = scale_in[...]
    gained = gain[...] * normed_grad
    small_out[pl.ds(small_out.shape[0] - 1, 1), :] = jnp.sum(normed_grad * inputs * r1, axis=0, keepdims=True)
    out_input[mine, :] = (
        middle_grad[...]
        + r1 * gained
        - inputs * (r1 * r1 * r1) * jnp.mean(inputs * gained, axis=1, keepdims=True)
    )
    in_copies = []
    for m, other in enumerate(others):
        c = pltpu.make_async_remote_copy(
            src_ref=out_input.at[mine], dst_ref=out_input.at[mine], send_sem=in_send.at[m],
            recv_sem=in_recv.at[m], device_id={"tensor": other}, device_id_type=MESH,
        )
        c.start()
        in_copies.append(c)
    ways = [("dp", m) for m in masks] + [("tensor", m) for m in tensor_masks]
    small_copies = []

    def small_step(step):
        if step > 0:
            small_copies[-1].wait_send()
            small_copies[-1].wait_recv()
            small_out[...] += small_got[step - 1]
        if step < len(ways):
            axis, m = ways[step]
            device = {"dp": peer_of(m)[0]} if axis == "dp" else {"tensor": mate(m)}
            c = pltpu.make_async_remote_copy(
                src_ref=small_out, dst_ref=small_got.at[step], send_sem=small_send.at[step],
                recv_sem=small_recv.at[step], device_id=device, device_id_type=MESH,
            )
            c.start()
            small_copies.append(c)

    steps = len(ways) + 1
    done = 0
    while events_q:
        if done < steps:
            small_step(done)
            done += 1
        events_q.pop(0)()
    while done < steps:
        small_step(done)
        done += 1
    sum_o.finish()
    sum_q.finish()
    for c in in_copies:
        c.wait()


def attention_back(
    back, middle, scale_mid, routed, grad_top, picked, router, moe_gain,
    heads, q, k, v, w_out, w_query, w_key, w_value, normed, cosine, sine, seg,
    hidden, gain, scale_in, dp_size, tensor_size, collective_id,
):
    length, width = normed.shape
    small = jax.ShapeDtypeStruct(((dp_size + 2 + 7) // 8 * 8, width), f32)
    q_width, k_width = q.shape[1], k.shape[1]
    rows = hidden.shape[0]
    orders_o, groups_o = sum_orders(dp_size, width, 1)
    orders_q, groups_q = sum_orders(dp_size, width, 2)
    steps = len(bit_masks(dp_size))
    small_steps = steps + len(bit_masks(tensor_size))
    qkv_width = q_width + 2 * k_width
    others = tensor_size - 1
    vmem = pl.BlockSpec(memory_space=pltpu.VMEM)
    dma = pltpu.SemaphoreType.DMA
    return pl.pallas_call(
        functools.partial(
            attention_back_kernel, dp_size, tensor_size, orders_o, groups_o, orders_q, groups_q
        ),
        out_shape=[
            jax.ShapeDtypeStruct((width, q_width), bf16),
            jax.ShapeDtypeStruct((width, qkv_width), bf16),
            jax.ShapeDtypeStruct((length, width), f32),
            jax.ShapeDtypeStruct(small.shape, f32),
        ],
        in_specs=[vmem] * 24,
        out_specs=[vmem] * 4,
        scratch_shapes=[
            pltpu.VMEM((length, width), bf16),
            pltpu.VMEM((rows, width), f32),
            pltpu.VMEM((length, length), f32),
            pltpu.VMEM((length, q_width), bf16),
            pltpu.VMEM((length, qkv_width), bf16),
            pltpu.VMEM((length, q_width), f32),
            pltpu.VMEM((length, 128), f32),
            pltpu.VMEM((length, 128), f32),
            pltpu.VMEM((width, q_width), bf16),
            pltpu.VMEM((width, q_width), bf16),
            pltpu.VMEM((width, qkv_width), bf16),
            pltpu.VMEM((width, qkv_width), bf16),
            pltpu.VMEM((others, rows, width), f32),
            pltpu.VMEM((others, rows, width), f32),
            pltpu.VMEM((small_steps,) + small.shape, f32),
            dma((len(orders_o), 2 * steps)),
            dma((len(orders_o), 2 * steps)),
            dma((len(orders_q), 2 * steps)),
            dma((len(orders_q), 2 * steps)),
            dma((small_steps,)),
            dma((small_steps,)),
            dma((others,)),
            dma((others,)),
            dma((others,)),
            dma((others,)),
            dma((others,)),
            dma((others,)),
        ],
        compiler_params=pltpu.CompilerParams(
            collective_id=collective_id, has_side_effects=True, vmem_limit_bytes=60 << 20
        ),
    )(
        back, middle, scale_mid, routed, grad_top, picked, router, moe_gain[None],
        heads, q, k, v, w_out, w_query, w_key, w_value, normed, cosine, sine,
        seg[:, None], seg[None, :], hidden, gain[None], scale_in,
    )


def dot(a, b, spec):
    return jnp.einsum(spec, a, b, preferred_element_type=f32)


def per_device(
    hidden_in,
    attn_gain,
    w_query,
    key_weight,
    value_weight,
    w_output,
    moe_gain,
    w_router,
    w_gate,
    w_up,
    w_down,
    expert_ids,
    segment_ids,
    out_grad,
):
    tokens_here, model_width = hidden_in.shape
    head_size = HEAD_DIM
    dp_size = lax.axis_size("dp")
    tensor_size = lax.axis_size("tensor")
    experts = dp_size
    tensor_index = lax.axis_index("tensor")
    masks = bit_masks(dp_size)
    tensor_masks = bit_masks(tensor_size)
    tensor_down = tensor_masks[::-1]
    rows_here = tokens_here // tensor_size
    groups = [list(range(pair, dp_size, 2)) for pair in range(2)]

    def my_rows(x):
        return lax.dynamic_slice_in_dim(x, tensor_index * rows_here, rows_here, 0)

    block = w_gate.shape[2] // tensor_size

    def my_units(x, dim):
        return lax.dynamic_slice_in_dim(x, tensor_index * block, block, dim)

    def relative_gather(x, dim):
        for mask in tensor_masks:
            x = jnp.concatenate([x, swap(x, "tensor", mask)], dim)
        return x

    far_set = [
        relative_gather(swap(my_units(w_gate[0], 1), "dp", 1), 1),
        relative_gather(swap(my_units(w_up[0], 1), "dp", 1), 1),
        relative_gather(swap(my_units(w_down[0], 0), "dp", 1), 0),
    ]
    grad_mine = my_rows(out_grad)
    lanes = jnp.arange(LANES, dtype=jnp.int32)
    picked_mine = jnp.any(my_rows(expert_ids)[:, :, None] == lanes[None, None, :], axis=1)
    picked_low = picked_mine.astype(bf16)
    grads = lax.all_gather(
        jnp.concatenate([grad_mine, picked_low], 1),
        "dp",
        axis=0,
        tiled=True,
        axis_index_groups=groups,
    )
    router_wide = jnp.pad(w_router, ((0, 0), (0, LANES - experts)))

    inputs = hidden_in.astype(f32)
    scale_in = lax.rsqrt(jnp.mean(inputs * inputs, axis=-1, keepdims=True) + epsilon)
    normed_low = (inputs * scale_in * attn_gain).astype(bf16)
    segment = segment_ids[0]
    tables = rope_tables(segment, head_size)
    heads_flat, query_heads, key_heads, value_heads, log_sums = attend_forward(
        normed_low, segment, tables, w_query, key_weight, value_weight, head_size
    )
    attn_part = jnp.dot(heads_flat, w_output, preferred_element_type=f32)
    attn_total = scatter_sum(attn_part, "tensor", tensor_down, f32)

    inputs_mine = my_rows(hidden_in).astype(f32)
    scale_in_mine = my_rows(scale_in)
    middle = inputs_mine + residual_scale * attn_total
    scale_mid = lax.rsqrt(jnp.mean(middle * middle, axis=-1, keepdims=True) + epsilon)
    routed_low = (middle * scale_mid * moe_gain).astype(bf16)

    near_set = [w_gate[0], w_up[0], w_down[0]]
    moe_part, back, *expert_parts = experts_call(
        routed_low, grads, router_wide, near_set, far_set, dp_size, tensor_size, 0
    )
    moe_total = lax.psum_scatter(
        moe_part, "dp", scatter_dimension=0, tiled=True, axis_index_groups=groups
    )

    near_mine = expert_parts[:3]
    returning = [swap(x, "dp", 1) for x in expert_parts[3:]]
    dims = (1, 1, 0)
    heads_width = heads_flat.shape[1]
    width_q, width_k = query_heads.shape[1] * head_size, key_heads.shape[1] * head_size
    qkv_width = width_q + 2 * width_k
    w_output_sum, qkv_grad, input_grad, small = attention_back(
        back,
        middle,
        scale_mid,
        routed_low,
        grad_mine,
        picked_low,
        router_wide,
        moe_gain,
        heads_flat,
        query_heads.reshape(tokens_here, -1),
        key_heads.reshape(tokens_here, -1),
        value_heads.reshape(tokens_here, -1),
        w_output,
        w_query,
        key_weight,
        value_weight,
        normed_low,
        jnp.tile(tables[0][:, 0, :], (1, 4)),
        jnp.tile(jnp.concatenate([-tables[1][:, 0, :], tables[1][:, 0, :]], 1), (1, 2)),
        segment,
        my_rows(hidden_in),
        attn_gain,
        scale_in_mine,
        dp_size,
        tensor_size,
        2,
    )
    w_output_sum, returning, moe_total = lax.optimization_barrier(
        (w_output_sum, returning, moe_total)
    )
    block_mine = (middle + residual_scale * moe_total.astype(f32)).astype(bf16)
    block_out = gather_blocks(block_mine, "tensor", tensor_down)
    expert_mine = [
        mine.astype(f32) + away.astype(f32) for mine, away in zip(near_mine, returning)
    ]
    if tensor_size == 2:
        expert_grads = place(expert_mine, [swap(x, "tensor", 1) for x in expert_mine], dims)
    else:
        expert_grads = [
            gather_blocks(x, "tensor", tensor_down, dim) for x, dim in zip(expert_mine, dims)
        ]
    w_output_sum, qkv_grad = w_output_sum.astype(f32), qkv_grad.astype(f32)
    w_output_grad = jnp.concatenate(
        [w_output_sum[i : i + heads_width] for i in range(0, model_width, heads_width)], 1
    )
    return (
        block_out,
        input_grad,
        small[-1],
        qkv_grad[:, :width_q],
        qkv_grad[:, width_q : width_q + width_k],
        qkv_grad[:, width_q + width_k : qkv_width],
        w_output_grad,
        small[experts],
        small[:experts].T,
        expert_grads[0][None],
        expert_grads[1][None],
        expert_grads[2][None],
    )


def solution(mesh):
    placed = (
        P("dp", None),
        P(),
        P(None, "tensor"),
        P(None, "tensor"),
        P(None, "tensor"),
        P("tensor", None),
        P(),
        P(),
        P("dp", None, None),
        P("dp", None, None),
        P("dp", None, None),
        P("dp", None),
        P("dp", None),
        P("dp", None),
    )
    return jax.shard_map(
        per_device,
        mesh=mesh,
        in_specs=placed,
        out_specs=(
            P("dp", None),
            P("dp", None),
            P(),
            P(None, "tensor"),
            P(None, "tensor"),
            P(None, "tensor"),
            P("tensor", None),
            P(),
            P(),
            P("dp", None, None),
            P("dp", None, None),
            P("dp", None, None),
        ),
        check_vma=False,
    )
```

```python
import functools

import jax
import jax.numpy as jnp
from jax import lax
from jax.experimental import pallas as pl
from jax.experimental.pallas import tpu as pltpu
from jax.sharding import PartitionSpec as P

HEAD_DIM = 64

bf16 = jnp.bfloat16
f32 = jnp.float32
MESH = pl.DeviceIdType.MESH
epsilon = 1e-06
residual_scale = 0.22
attn_scale = 0.015625
rope_base = 10000.0
masked_score = -1e30


def bit_masks(size):
    masks = []
    while size > 1:
        size //= 2
        masks.append(size)
    return masks[::-1]


def swap(x, axis, mask):
    return lax.ppermute(x, axis, [(i, i ^ mask) for i in range(lax.axis_size(axis))])


def bit_of(axis, mask):
    return (lax.axis_index(axis) // mask) % 2


def halves_by_bit(x, axis, mask, dim=0):
    half = x.shape[dim] // 2
    bit = bit_of(axis, mask)
    mine = lax.dynamic_slice_in_dim(x, bit * half, half, dim)
    other = lax.dynamic_slice_in_dim(x, (1 - bit) * half, half, dim)
    return mine, other


def join_by_bit(mine, other, axis, mask, dim=0):
    return jnp.where(
        bit_of(axis, mask) == 0,
        jnp.concatenate([mine, other], dim),
        jnp.concatenate([other, mine], dim),
    )


def scatter_sum(x, axis, masks, kind, dim=0):
    x = x.astype(f32)
    for mask in masks:
        mine, other = halves_by_bit(x, axis, mask, dim)
        x = mine + swap(other.astype(kind), axis, mask).astype(f32)
    return x


def gather_blocks(x, axis, masks, dim=0):
    for mask in reversed(masks):
        x = join_by_bit(x, swap(x, axis, mask), axis, mask, dim)
    return x


def rotated(masks, j):
    j = j % len(masks)
    return masks[j:] + masks[:j]


def peer_of(mask):
    me = lax.axis_index("dp")
    bit = (me // mask) % 2
    return me + mask * (1 - 2 * bit), bit


def greet(masks):
    barrier = pltpu.get_barrier_semaphore()
    for mask in masks:
        pl.semaphore_signal(
            barrier, inc=1, device_id={"dp": peer_of(mask)[0]}, device_id_type=MESH
        )
    pl.semaphore_wait(barrier, len(masks))


def remote(src, dst, send, recv, mask):
    return remote_to(src, dst, send, recv, peer_of(mask)[0])


def add_rows(dst, dst0, a, a0, b, b0, rows, out_dtype):
    step = 16

    def body(i, _):
        r = pl.multiple_of(i * step, step)
        x = a[pl.ds(a0 + r, step), :].astype(f32) + b[pl.ds(b0 + r, step), :].astype(f32)
        dst[pl.ds(dst0 + r, step), :] = x.astype(out_dtype)
        return 0

    lax.fori_loop(0, rows // step, body, 0)


def group_sizes(dp_size):
    a = 4
    return a, dp_size // (2 * a)


class Spot:
    def __init__(self, a, b):
        me = lax.axis_index("dp")
        self.a, self.b = a, b
        self.n = a * b
        self.me = me
        self.A = me // (2 * b)
        self.B = (me // 2) % b
        self.block = me // 2
        self.pair = me % 2
        self.devices = (me + 2 * b, me - 2 * b, me + 2, me - 2)
        self.exists = (self.A < a - 1, self.A > 0, self.B < b - 1, self.B > 0)
        self.some = me + 2 * (1 - 2 * (self.B % 2))

    def greet(self, further=()):
        barrier = pltpu.get_barrier_semaphore()
        for device in further:
            pl.semaphore_signal(barrier, inc=1, device_id=device, device_id_type=MESH)
        for device, there in zip(self.devices, self.exists):

            @pl.when(there)
            def _(device=device):
                pl.semaphore_signal(
                    barrier, inc=1, device_id={"dp": device}, device_id_type=MESH
                )

        a, b = self.a, self.b
        ups = 2 - (self.A + 1) // a - (self.B + 1) // b
        downs = (self.A + a - 1) // a + (self.B + b - 1) // b
        pl.semaphore_wait(barrier, ups + downs + len(further))


def xor4(x, y):
    return ((x // 2 + y // 2) % 2) * 2 + (x % 2 + y % 2) % 2


def is_at(x, value):
    return 1 // (1 + (x - value) * (x - value))


def by_distance(size, place, k):
    found = 0
    for p in range(size):
        order = sorted(range(size), key=lambda q: (abs(q - p), q))
        for j, q in enumerate(order):
            if q > 0:
                found = found + q * is_at(place, p) * is_at(k, j)
    return found


def visit_order(a, b):
    pairs = [(k, l) for k in range(a) for l in range(b)]
    return sorted(pairs, key=lambda kl: kl[0] + (2 * kl[1] + 0.5 if kl[1] else 0))


def remote_to(src, dst, send, recv, device):
    return pltpu.make_async_remote_copy(
        src_ref=src,
        dst_ref=dst,
        send_sem=send,
        recv_sem=recv,
        device_id={"dp": device},
        device_id_type=MESH,
    )


SUM_PIECES = 4


class LineGather:
    def __init__(self, spot, buf, rows, send, recv):
        self.spot, self.buf, self.rows, self.send, self.recv = spot, buf, rows, send, recv
        few = max(16, rows * 3 // 16 // 16 * 16)
        self.parts = ((0, rows - few, False), (rows - few, few, True))

    def coords(self, i):
        s = self.spot
        visits = visit_order(s.a, s.b)
        k = sum(v[0] * is_at(i, j) for j, v in enumerate(visits) if v[0])
        l = sum(v[1] * is_at(i, j) for j, v in enumerate(visits) if v[1])
        return by_distance(s.a, s.A, k), by_distance(s.b, s.B, l)

    def row0(self, i):
        A, B = self.coords(i)
        return pl.multiple_of((A * self.spot.b + B) * self.rows, 16)

    def copy(self, p, block, way, device):
        start, size, _ = self.parts[p]
        there = self.buf.at[pl.ds(pl.multiple_of(block * self.rows + start, 16), size)]
        return remote_to(there, there, self.send.at[block, way, p], self.recv.at[block, p], device)

    def each_way(self, i, p, act):
        s = self.spot
        A, B = self.coords(i)
        block = A * s.b + B
        if self.parts[p][2]:
            along_a, along_b = True, A == s.A
        else:
            along_a, along_b = B == s.B, True
        conditions = (
            along_a & (A <= s.A) & s.exists[0],
            along_a & (A >= s.A) & s.exists[1],
            along_b & (B <= s.B) & s.exists[2],
            along_b & (B >= s.B) & s.exists[3],
        )
        for way, (condition, device) in enumerate(zip(conditions, s.devices)):

            @pl.when(condition)
            def _(way=way, device=device):
                act(self.copy(p, block, way, device))

    def arrive(self, i):
        A, B = self.coords(i)
        for p in range(len(self.parts)):
            self.copy(p, A * self.spot.b + B, 0, self.spot.some).wait_recv()
            self.each_way(i, p, lambda c: c.start())

    def begin(self):
        for p in range(len(self.parts)):
            self.each_way(0, p, lambda c: c.start())

    def finish(self):
        def one(i, _):
            for p in range(len(self.parts)):
                self.each_way(i, p, lambda c: c.wait_send())
            return 0

        lax.fori_loop(0, self.spot.n, one, 0)


def add_into(dst, d0, src, s0, rows, step=16):
    def body(i, _):
        r = pl.multiple_of(i * step, step)
        total = dst[pl.ds(d0 + r, step), :].astype(f32) + src[pl.ds(s0 + r, step), :].astype(f32)
        dst[pl.ds(d0 + r, step), :] = total.astype(dst.dtype)
        return 0

    lax.fori_loop(0, rows // step, body, 0)


class LineSum:
    def __init__(self, size, place, up, down, part, row_of, rows, got, send, recv, some):
        self.size, self.place, self.up, self.down = size, place, up, down
        self.part, self.row_of, self.rows, self.got = part, row_of, rows, got
        self.send, self.recv, self.some = send, recv, some

    def up_slot(self, place, c):
        return c - place

    def down_slot(self, place, c):
        return c + (self.size - place) * ((place + self.size - 1) // self.size)

    def copies(self, c, slot, send, device):
        size = self.rows // SUM_PIECES
        return [
            remote_to(
                self.part.at[pl.ds(pl.multiple_of(self.row_of(c) + p * size, 16), size)],
                self.got.at[pl.ds(pl.multiple_of(slot * self.rows + p * size, 16), size)],
                send.at[p],
                self.recv.at[slot, p],
                device,
            )
            for p in range(SUM_PIECES)
        ]

    def take(self, c, slot, p, dst=None, d0=None):
        if dst is None:
            dst, d0 = self.part, self.row_of(c)
        size = self.rows // SUM_PIECES
        self.copies(c, slot, self.send.at[0, 0], self.some)[p].wait_recv()
        from_row = pl.multiple_of(slot * self.rows + p * size, 16)
        add_into(dst, d0 + p * size, self.got, from_row, size)

    def up_copies(self, k):
        c = self.size - 1 - k
        return self.copies(c, self.up_slot(self.place + 1, c), self.send.at[k, 0], self.up)

    def down_copies(self, k):
        return self.copies(k, self.down_slot(self.place - 1, k), self.send.at[k, 1], self.down)

    def step_up(self, k):
        c = self.size - 1 - k

        @pl.when(c > self.place)
        def _():
            for p, copy in enumerate(self.up_copies(k)):

                @pl.when(self.place > 0)
                def _(p=p):
                    self.take(c, self.up_slot(self.place, c), p)

                copy.start()

    def step_down(self, k):
        @pl.when(k < self.place)
        def _():
            for p, copy in enumerate(self.down_copies(k)):

                @pl.when(self.place < self.size - 1)
                def _(p=p):
                    self.take(k, self.down_slot(self.place, k), p)

                copy.start()

    def step(self, k):
        self.step_up(k)
        self.step_down(k)

    def end(self, out=None):
        p = self.place
        d0 = None
        if out is not None:
            out[...] = self.part[pl.ds(self.row_of(p), self.rows), :].astype(out.dtype)
            d0 = 0

        @pl.when(p > 0)
        def _():
            for j in range(SUM_PIECES):
                self.take(p, self.up_slot(p, p), j, out, d0)

        @pl.when(p < self.size - 1)
        def _():
            for j in range(SUM_PIECES):
                self.take(p, self.down_slot(p, p), j, out, d0)

        for k in range(self.size - 1):

            @pl.when(self.size - 1 - k > p)
            def _(k=k):
                for c in self.up_copies(k):
                    c.wait_send()

            @pl.when(k < p)
            def _(k=k):
                for c in self.down_copies(k):
                    c.wait_send()


def slots_of(size):
    return 1 if size == 2 else size + 1


class GroupSum:
    def __init__(self, spot, part, rows, got_b, got_a, send_b, recv_b, send_a, recv_a):
        self.spot, self.part, self.rows = spot, part, rows
        a, b = spot.a, spot.b
        slots_b = slots_of(b)

        def b_line(A):
            return LineSum(
                b, spot.B, spot.devices[2], spot.devices[3], part,
                lambda B: pl.multiple_of((A * b + B) * rows, 16), rows,
                got_b.at[pl.ds(pl.multiple_of(A * slots_b * rows, 16), slots_b * rows)],
                send_b.at[A], recv_b.at[A], spot.some,
            )

        self.b_line = b_line
        self.a_line = LineSum(
            a, spot.A, spot.devices[0], spot.devices[1], part,
            lambda A: pl.multiple_of((A * b + spot.B) * rows, 16), rows,
            got_a, send_a, recv_a, spot.some,
        )

    def ready(self, A, B):
        if self.spot.b == 2:
            line = self.b_line(A)

            @pl.when(B != self.spot.B)
            def _():
                line.step(0)

    def along_b(self):
        if self.spot.b > 2:

            def one(A, _):
                for k in range(self.spot.b - 1):
                    self.b_line(A).step(k)
                return 0

            lax.fori_loop(0, self.spot.a, one, 0)

    def flow(self, fills):
        a, line = self.spot.a, self.a_line
        fills = list(fills)

        def fill():
            if fills:
                fills.pop(0)()

        for k in range(a - 1):
            if 2 * k < a:
                self.b_line(a - 1 - k).end()
            line.step_up(k)
            fill()
            if 2 * k < a and a - 1 - k != k:
                self.b_line(k).end()
            line.step_down(k)
            fill()
        while fills:
            fill()

    def order(self, j):
        a = self.spot.a
        places = sorted(range(a), key=lambda c: (min(c, a - 1 - c), -c))
        return sum(c * is_at(j, i) for i, c in enumerate(places) if c)

    def steps_a(self):
        return self.spot.a - 1

    @staticmethod
    def scratch(a, b, rows, width):
        return [
            pltpu.VMEM((a * slots_of(b) * rows, width), bf16),
            pltpu.VMEM((slots_of(a) * rows, width), bf16),
            pltpu.SemaphoreType.DMA((a, b - 1, 2, SUM_PIECES)),
            pltpu.SemaphoreType.DMA((a, slots_of(b), SUM_PIECES)),
            pltpu.SemaphoreType.DMA((a - 1, 2, SUM_PIECES)),
            pltpu.SemaphoreType.DMA((slots_of(a), SUM_PIECES)),
        ]


LANES = 128
LOW_AT = 64


def mm(x, y, dims):
    return lax.dot_general(x, y, (dims, ((), ())), preferred_element_type=f32)


NN, NT, TN = ((1,), (0,)), ((1,), (1,)), ((0,), (0,))


def experts_kernel(
    a, b, rows, width, cores,
    x_ref, grads_ref, router_ref, near_gate, near_up, near_down, far_gate, far_up, far_down,
    moe_ref, out_ref, o_near_gate, o_near_up, o_near_down, o_far_gate, o_far_up, o_far_down,
    xs, gs, weights, downs, lows, part, extras, stage, got_wide, got_down,
    local, load, send, recv, stage_sem, store, core_send, core_recv, *scratch,
):
    spot = Spot(a, b)
    n = spot.n
    gather = LineGather(spot, xs, rows, send, recv)
    total = GroupSum(spot, part, rows, *scratch)
    mine = pltpu.make_async_copy(
        x_ref, xs.at[pl.ds(pl.multiple_of(spot.block * rows, 16), rows)], local.at[0]
    )
    mine.start()
    sources = (near_gate, near_up, far_gate, far_up)
    arriving = [
        pltpu.make_async_copy(src, weights.at[k], local.at[1 + k]) for k, src in enumerate(sources)
    ] + [
        pltpu.make_async_copy(src, downs.at[k], local.at[5 + k])
        for k, src in enumerate((near_down, far_down))
    ]

    def grads_copy(i):
        at = pl.ds(gather.row0(i), rows)
        return pltpu.make_async_copy(grads_ref.at[at], gs.at[at], load.at[i])

    grads_copy(0).start()
    for c in arriving:
        c.start()
    for i in range(1, n):
        grads_copy(i).start()
    core = lax.axis_index("tensor")
    mates = [xor4(core, m) for m in range(1, cores)]
    spot.greet([{"tensor": mate} for mate in mates])
    mine.wait()
    gather.begin()
    for c in arriving:
        c.wait()
    lane = lax.broadcasted_iota(jnp.int32, (rows, LANES), 1)
    near, far = spot.me, spot.me + 1 - 2 * spot.pair

    def block(i, _):
        at = pl.ds(gather.row0(i), rows)
        grads_copy(i).wait()
        x = xs[at, :]
        chosen = gs[at, pl.ds(width, LANES)] > 0
        logits = jnp.where(chosen, mm(x, router_ref[...], NN), masked_score)
        raised = jnp.where(chosen, jnp.exp(logits - jnp.max(logits, axis=1, keepdims=True)), 0.0)
        gates = raised / jnp.sum(raised, axis=1, keepdims=True)
        extra = jnp.zeros((rows, LANES), f32)
        for e, expert in enumerate((near, far)):
            if e == 1:

                @pl.when(i + 1 < n)
                def _():
                    gather.arrive(i + 1)

            column = jnp.sum(jnp.where(lane == expert, gates, 0.0), axis=1, keepdims=True)
            x = xs[at, :]
            gate_act = mm(x, weights[2 * e], NN)
            up_act = mm(x, weights[2 * e + 1], NN)
            down_in = residual_scale * mm(gs[at, pl.ds(0, width)], downs[e], NT)
            sigmoid_gate = jax.nn.sigmoid(gate_act)
            silu_gate = gate_act * sigmoid_gate
            hidden = silu_gate * up_act
            deriv = jnp.sum(hidden * down_in, axis=1, keepdims=True)
            high = deriv.astype(bf16).astype(f32)
            extra += jnp.where(lane == expert, high, 0.0)
            extra += jnp.where(lane == expert + LOW_AT, deriv - high, 0.0)
            down_in = down_in * column
            lows[3 * e, at, :] = (hidden * column).astype(bf16)
            lows[3 * e + 1, at, :] = (
                down_in * up_act * sigmoid_gate * (1.0 + gate_act * (1.0 - sigmoid_gate))
            ).astype(bf16)
            lows[3 * e + 2, at, :] = (down_in * silu_gate).astype(bf16)

        extras[at, :] = extra.astype(bf16)
        return 0

    lax.fori_loop(0, n, block, 0)

    def rows_of(A, B):
        return pl.ds(pl.multiple_of((A * b + B) * rows, 16), rows)

    def back_block(A, B):
        at = rows_of(A, B)
        back = mm(lows[1, at, :], weights[0], NT) + mm(lows[2, at, :], weights[1], NT)
        back += mm(lows[4, at, :], weights[2], NT) + mm(lows[5, at, :], weights[3], NT)
        part[at, pl.ds(0, width)] = back.astype(bf16)
        part[at, pl.ds(width, LANES)] = extras[at, :]
        total.ready(A, B)

    def back_others(i, _):
        A = total.order(i // (b - 1))
        B = by_distance(b, spot.B, 1 + i % (b - 1))
        back_block(A, B)
        return 0

    def back_own(i, _):
        back_block(total.order(i), spot.B)
        return 0

    def stage_copy(i):
        at = pl.ds(pl.multiple_of(i * rows, 16), rows)
        return pltpu.make_async_copy(stage.at[i % 2], moe_ref.at[at], stage_sem.at[i % 2])

    def moe_block(i, _):
        at = pl.ds(pl.multiple_of(i * rows, 16), rows)

        @pl.when(i >= 2)
        def _():
            stage_copy(i - 2).wait()

        stage[i % 2] = (mm(lows[0, at, :], downs[0], NN) + mm(lows[3, at, :], downs[1], NN)).astype(
            bf16
        )
        stage_copy(i).start()
        return 0

    lax.fori_loop(0, a * (b - 1), back_others, 0)
    lax.fori_loop(0, 2, back_own, 0)
    if b > 2:
        lax.fori_loop(2, a, back_own, 0)
    total.along_b()
    tile = 256

    def weight_grads(e):
        def wide(k, _):
            at = pl.ds(pl.multiple_of(k * tile, tile), tile)
            x = xs[:, at]
            weights[2 * e, at, :] = mm(x, lows[3 * e + 1], TN).astype(bf16)
            weights[2 * e + 1, at, :] = mm(x, lows[3 * e + 2], TN).astype(bf16)
            downs[e, :, at] = (residual_scale * mm(lows[3 * e], gs[:, at], TN)).astype(bf16)
            return 0

        lax.fori_loop(0, width // tile, wide, 0)
        give(e)

    units = lows.shape[2] // cores

    def blocks(e, k):
        at = pl.ds(pl.multiple_of(k * units, units), units)
        return (weights.at[2 * e, :, at], weights.at[2 * e + 1, :, at], downs.at[e, at, :])

    def own(e):
        return blocks(e, core if e == 0 else 0)

    def gifts(e):
        copies = []
        for m, mate in enumerate(mates):
            landing = (got_wide.at[e, m, 0], got_wide.at[e, m, 1], got_down.at[e, m])
            for i, (src, dst) in enumerate(zip(blocks(e, mate if e == 0 else m + 1), landing)):
                copies.append(
                    pltpu.make_async_remote_copy(
                        src_ref=src,
                        dst_ref=dst,
                        send_sem=core_send.at[e, m, i],
                        recv_sem=core_recv.at[e, m, i],
                        device_id={"tensor": mate},
                        device_id_type=MESH,
                    )
                )
        return copies

    def give(e):
        for c in gifts(e):
            c.start()

    def collect(e):
        for c in gifts(e):
            c.wait()
        outs = (o_near_gate, o_near_up, o_near_down) if e == 0 else (o_far_gate, o_far_up, o_far_down)
        for i, (view, out) in enumerate(zip(own(e), outs)):

            def chunk(k, _, i=i, view=view):
                size = view.shape[0] // 8
                at = pl.ds(pl.multiple_of(k * size, 16), size)
                total = view[at, :].astype(f32)
                for m in range(len(mates)):
                    got = got_wide[e, m, i, at, :] if i < 2 else got_down[e, m, at, :]
                    total += got.astype(f32)
                view[at, :] = total.astype(bf16)
                return 0

            lax.fori_loop(0, 8, chunk, 0)
            c = pltpu.make_async_copy(view, out, store.at[3 * e + i])
            c.start()
            stored.append(c)

    stored = []

    def moe_all():
        lax.fori_loop(0, n, moe_block, 0)

    total.flow(
        [
            (lambda: lax.fori_loop(2, a, back_own, 0)) if b == 2 else (lambda: None),
            moe_all,
            lambda: weight_grads(1),
            lambda: weight_grads(0),
            lambda: collect(1),
            lambda: collect(0),
        ]
    )
    line = total.a_line
    line.end(out_ref)
    gather.finish()
    stage_copy(n - 2).wait()
    stage_copy(n - 1).wait()
    for c in stored:
        c.wait()


def experts_call(rows_low, grads, router, near, far, dp_size, cores, collective_id):
    a, b = group_sizes(dp_size)
    n = a * b
    rows, width = rows_low.shape
    units = near[0].shape[1]
    hbm, vmem = pl.BlockSpec(memory_space=pl.ANY), pl.BlockSpec(memory_space=pltpu.VMEM)
    outs = [
        jax.ShapeDtypeStruct((n * rows, width), bf16),
        jax.ShapeDtypeStruct((rows, width + LANES), f32),
    ] + [
        jax.ShapeDtypeStruct(shape, bf16)
        for shape in 2 * [(width, units // cores), (width, units // cores), (units // cores, width)]
    ]
    return pl.pallas_call(
        functools.partial(experts_kernel, a, b, rows, width, cores),
        out_shape=outs,
        in_specs=[hbm, hbm, vmem] + [hbm] * 6,
        out_specs=[hbm, vmem] + [hbm] * 6,
        scratch_shapes=[
            pltpu.VMEM((n * rows, width), bf16),
            pltpu.VMEM((n * rows, width + LANES), bf16),
            pltpu.VMEM((4, width, units), bf16),
            pltpu.VMEM((2, units, width), bf16),
            pltpu.VMEM((6, n * rows, units), bf16),
            pltpu.VMEM((n * rows, width + LANES), bf16),
            pltpu.VMEM((n * rows, LANES), bf16),
            pltpu.VMEM((2, rows, width), bf16),
            pltpu.VMEM((2, cores - 1, 2, width, units // cores), bf16),
            pltpu.VMEM((2, cores - 1, units // cores, width), bf16),
            pltpu.SemaphoreType.DMA((7,)),
            pltpu.SemaphoreType.DMA((n,)),
            pltpu.SemaphoreType.DMA((n, 4, 2)),
            pltpu.SemaphoreType.DMA((n, 2)),
            pltpu.SemaphoreType.DMA((2,)),
            pltpu.SemaphoreType.DMA((6,)),
            pltpu.SemaphoreType.DMA((2, cores - 1, 3)),
            pltpu.SemaphoreType.DMA((2, cores - 1, 3)),
        ]
        + GroupSum.scratch(a, b, rows, width + LANES),
        compiler_params=pltpu.CompilerParams(
            collective_id=collective_id, has_side_effects=True, vmem_limit_bytes=62 << 20
        ),
    )(rows_low, grads, router, *near, *far)


def reduce_schedule(steps, groups):
    sums = [("sum", s) for s in range(steps)]
    backs = [("back", s) for s in reversed(range(steps))]
    lines = [[(g,) + e for e in sums + backs] for g in range(groups)]
    if groups == 1:
        return lines[0]
    first, second = lines
    order = first[: steps - 1]
    first = first[steps - 1 :]
    while first or second:
        if second:
            order.append(second.pop(0))
        if first:
            order.append(first.pop(0))
    return order


def place_kernel(dims, *refs):
    n = len(dims)
    mine, other, outs = refs[:n], refs[n : 2 * n], refs[2 * n : 3 * n]
    bufs, sems, out_sems = refs[3 * n : 4 * n], refs[4 * n], refs[4 * n + 1]
    me = lax.axis_index("tensor")

    def copy(i, which, src):
        size = src.shape[dims[i]]
        at = pl.multiple_of((me + which - 2 * which * me) * size, size)
        window = (slice(None),) * dims[i] + (pl.ds(at, size),)
        return pltpu.make_async_copy(src, bufs[i].at[window], sems.at[i, which])

    copies = [[copy(i, w, src) for w, src in enumerate((mine[i], other[i]))] for i in range(n)]
    for pair in copies:
        for c in pair:
            c.start()
    back = []
    for i, pair in enumerate(copies):
        for c in pair:
            c.wait()
        c = pltpu.make_async_copy(bufs[i], outs[i], out_sems.at[i])
        c.start()
        back.append(c)
    for c in back:
        c.wait()


def place(mine, other, dims):
    n = len(dims)
    shapes = [x.shape[:d] + (2 * x.shape[d],) + x.shape[d + 1 :] for x, d in zip(mine, dims)]
    return pl.pallas_call(
        functools.partial(place_kernel, dims),
        out_shape=[jax.ShapeDtypeStruct(s, x.dtype) for x, s in zip(mine, shapes)],
        in_specs=[pl.BlockSpec(memory_space=pl.ANY)] * (2 * n),
        out_specs=[pl.BlockSpec(memory_space=pl.ANY)] * n,
        scratch_shapes=[pltpu.VMEM(s, x.dtype) for x, s in zip(mine, shapes)]
        + [pltpu.SemaphoreType.DMA((n, 2)), pltpu.SemaphoreType.DMA((n,))],
        compiler_params=pltpu.CompilerParams(vmem_limit_bytes=24 << 20),
    )(*mine, *other)


class AllReduce:
    def __init__(self, orders, groups, acc, got, out, send, recv):
        self.orders, self.groups = orders, groups
        self.acc, self.got, self.out, self.send, self.recv = acc, got, out, send, recv
        self.k = len(orders[0])
        self.size = acc.shape[0] // len(orders)
        self.where = [j * self.size for j in range(len(orders))]
        self.sums, self.backs = {}, {}

    def sum_send(self, j, step):
        count = self.size >> (step + 1)
        mask = self.orders[j][step]
        _, bit = peer_of(mask)
        keep = pl.multiple_of(self.where[j] + bit * count, 16)
        give = pl.multiple_of(self.where[j] + (1 - bit) * count, 16)
        acc, got = self.acc, self.got
        p0 = j * self.size + (self.size - (self.size >> max(step - 1, 0)))
        if step > 0:
            self.sums[j, step - 1].wait_recv()
            add_rows(acc, give, acc, give, got, p0 + pl.multiple_of((1 - bit) * count, 16), count, bf16)
        g0 = j * self.size + (self.size - (self.size >> step))
        c = remote(
            acc.at[pl.ds(give, count)],
            got.at[pl.ds(g0, count)],
            self.send.at[j, step],
            self.recv.at[j, step],
            mask,
        )
        c.start()
        self.sums[j, step] = c
        self.where[j] = keep

        def stay():
            if step > 0:
                add_rows(acc, keep, acc, keep, got, p0 + pl.multiple_of(bit * count, 16), count, bf16)

        return stay

    def back_step(self, j, step):
        count = self.size >> (step + 1)
        mask = self.orders[j][step]
        _, bit = peer_of(mask)
        here = self.where[j]
        if step == self.k - 1:
            self.sums[j, step].wait_recv()
            p0 = j * self.size + (self.size - (self.size >> step))
            add_rows(self.out, here, self.acc, here, self.got, p0, count, bf16)
        else:
            self.backs[j, step + 1].wait_recv()
        there = self.out.at[pl.ds(here, count)]
        c = remote(
            there, there, self.send.at[j, self.k + step], self.recv.at[j, self.k + step], mask
        )
        c.start()
        self.backs[j, step] = c
        self.where[j] = pl.multiple_of(here - bit * count, 16)

    def events(self):
        per_group = len(self.orders) // self.groups

        def event(g, kind, step):
            members = range(g * per_group, (g + 1) * per_group)
            if kind == "sum":
                for stay in [self.sum_send(j, step) for j in members]:
                    stay()
            else:
                for j in members:
                    self.back_step(j, step)

        return [
            functools.partial(event, *e) for e in reduce_schedule(self.k, self.groups)
        ]

    def finish(self):
        for j in range(len(self.orders)):
            self.backs[j, 0].wait_recv()
        for c in list(self.sums.values()) + list(self.backs.values()):
            c.wait_send()


def sum_orders(dp_size, rows, most):
    masks = bit_masks(dp_size)
    groups = most if rows % (3 * most * 16 * dp_size) == 0 else 1
    return [rotated(masks[:-1], j) + masks[-1:] for j in range(3 * groups)], groups


def turn(x, cosine, sine):
    lane = lax.broadcasted_iota(jnp.int32, x.shape, 1)
    swapped = jnp.where(lane % HEAD_DIM < HEAD_DIM // 2, pltpu.roll(x, 128 - 32, 1), pltpu.roll(x, 32, 1))
    return x * cosine + swapped * sine


def mask_bias(bias, seg_col, seg_row):
    length = bias.shape[0]
    row = lax.broadcasted_iota(jnp.int32, bias.shape, 0)
    col = lax.broadcasted_iota(jnp.int32, bias.shape, 1)
    allowed = (row >= col) & (seg_col[...] == seg_row[...])
    bias[...] = jnp.where(allowed, 0.0, masked_score)


def attention_back_kernel(
    dp_size, tensor_size, orders_o, groups_o, orders_q, groups_q,
    back, middle, routed, grad_top, picked, router, moe_gain,
    heads, q_ref, k_ref, v_ref, w_out, w_query, w_key, w_value, normed, cosine, sine,
    seg_col, seg_row, hidden, gain,
    out_o, out_q, out_input, small_out,
    branch, middle_grad, bias, heads_grad, qkv_low, scratch_q, scratch_k, scratch_v,
    acc_o, got_o, acc_q, got_q, shares, got_shares, small_got,
    send_o, recv_o, send_q, recv_q, small_send, small_recv, share_send, share_recv, in_send, in_recv, branch_send, branch_recv,
):
    length, width = normed.shape
    q_width, k_width = q_ref.shape[1], k_ref.shape[1]
    rows = hidden.shape[0]
    per_kv = q_width // k_width
    core = lax.axis_index("tensor")
    tensor_masks = bit_masks(tensor_size)

    def mate(m):
        bit = (core // m) % 2
        return core + m * (1 - 2 * bit)

    barrier = pltpu.get_barrier_semaphore()
    masks = bit_masks(dp_size)
    others = [(core + m) % tensor_size for m in range(1, tensor_size)]
    for mask in masks:
        pl.semaphore_signal(
            barrier, inc=1, device_id={"dp": peer_of(mask)[0]}, device_id_type=MESH
        )
    for other in others:
        pl.semaphore_signal(barrier, inc=1, device_id={"tensor": other}, device_id_type=MESH)
    mine = pl.ds(pl.multiple_of(core * rows, 16), rows)
    experts = dp_size
    x = routed[...]
    chosen = picked[...] > 0
    logits = jnp.where(chosen, mm(x, router[...], NN), masked_score)
    raised = jnp.where(chosen, jnp.exp(logits - jnp.max(logits, axis=1, keepdims=True)), 0.0)
    gates = raised / jnp.sum(raised, axis=1, keepdims=True)
    derivs = back[:, pl.ds(width, LANES)]
    derivs = jnp.where(chosen, derivs + pltpu.roll(derivs, LANES - LOW_AT, 1), 0.0)
    logit_grad = (
        gates * (derivs - jnp.sum(gates * derivs, axis=1, keepdims=True))
    ).astype(bf16)
    small_out[...] = jnp.zeros(small_out.shape, f32)
    small_out[pl.ds(0, experts), :] = mm(logit_grad, x, TN)[:experts]
    routed_grad = back[:, pl.ds(0, width)] + mm(logit_grad, router[...], NT)
    mid = middle[...]
    r2 = lax.rsqrt(jnp.mean(mid * mid, axis=1, keepdims=True) + epsilon)
    small_out[pl.ds(experts, 1), :] = jnp.sum(routed_grad * mid * r2, axis=0, keepdims=True)
    gained = moe_gain[...] * routed_grad
    middle_grad[...] = (
        grad_top[...].astype(f32)
        + r2 * gained
        - mid * (r2 * r2 * r2) * jnp.mean(mid * gained, axis=1, keepdims=True)
    )
    branch[mine, :] = (residual_scale * middle_grad[...]).astype(bf16)
    pl.semaphore_wait(barrier, len(masks) + len(others))
    branch_copies = []
    for m, other in enumerate(others):
        c = pltpu.make_async_remote_copy(
            src_ref=branch.at[mine], dst_ref=branch.at[mine], send_sem=branch_send.at[m],
            recv_sem=branch_recv.at[m], device_id={"tensor": other}, device_id_type=MESH,
        )
        c.start()
        branch_copies.append(c)
    mask_bias(bias, seg_col, seg_row)
    for c in branch_copies:
        c.wait()
    for i in range(width // q_width):
        at = pl.ds(i * q_width, q_width)
        acc_o[at, :] = mm(heads[...], branch[:, at], TN).astype(bf16)
    sum_o = AllReduce(orders_o, groups_o, acc_o, got_o, out_o, send_o, recv_o)
    events_o = sum_o.events()
    events_o.pop(0)()
    heads_grad[...] = mm(branch[...], w_out[...], NT).astype(bf16)
    half = length // 2
    spans = ((0, half, half), (half, half, length))
    count = 0
    for pair in range(k_width // 128):
        k_tile = k_ref[:, pair * 128 : pair * 128 + 128]
        v_tile = v_ref[:, pair * 128 : pair * 128 + 128]
        for g in range(2):
            kg = k_tile[:, g * HEAD_DIM : (g + 1) * HEAD_DIM]
            vg = v_tile[:, g * HEAD_DIM : (g + 1) * HEAD_DIM]
            side = pl.ds(g * HEAD_DIM, HEAD_DIM)
            for h in range(per_kv):
                head = (pair * 2 + g) * per_kv + h
                lanes = pl.ds(head * HEAD_DIM, HEAD_DIM)
                for start, size, cols in spans:
                    at = pl.ds(start, size)
                    qh = q_ref[at, lanes]
                    oh = heads_grad[at, lanes]
                    scores = mm(qh, kg[:cols], NT) * attn_scale + bias[at, pl.ds(0, cols)]
                    raised = jnp.exp(scores - jnp.max(scores, axis=1, keepdims=True))
                    probability = raised * (1.0 / jnp.sum(raised, axis=1, keepdims=True))
                    prob_grad = mm(oh, vg[:cols], NT)
                    weighted = jnp.sum(probability * prob_grad, axis=1, keepdims=True)
                    score_low = (probability * (prob_grad - weighted)).astype(bf16)
                    probs_low = probability.astype(bf16)
                    scratch_q[at, lanes] = mm(score_low, kg[:cols], NN) * attn_scale
                    dk = mm(score_low, qh, TN) * attn_scale
                    dv = mm(probs_low, oh, TN)
                    upto = pl.ds(0, cols)
                    if h == 0 and start == 0:
                        scratch_k[upto, side] = dk
                        scratch_v[upto, side] = dv
                        scratch_k[pl.ds(cols, length - cols), side] = jnp.zeros((length - cols, HEAD_DIM), f32)
                        scratch_v[pl.ds(cols, length - cols), side] = jnp.zeros((length - cols, HEAD_DIM), f32)
                    else:
                        scratch_k[upto, side] += dk
                        scratch_v[upto, side] += dv
                count += 1
                if count % 2 == 0 and len(events_o) > 1:
                    events_o.pop(0)()
        at = pl.ds(q_width + pair * 128, 128)
        qkv_low[:, at] = turn(scratch_k[...], cosine[...], -sine[...]).astype(bf16)
        at = pl.ds(q_width + k_width + pair * 128, 128)
        qkv_low[:, at] = scratch_v[...].astype(bf16)
    for i in range(q_width // 128):
        at = pl.ds(i * 128, 128)
        qkv_low[:, at] = turn(scratch_q[:, at], cosine[...], -sine[...]).astype(bf16)
    chunk = width // len(orders_q)
    for i in range(len(orders_q)):
        at = pl.ds(i * chunk, chunk)
        acc_q[at, :] = mm(normed[:, at], qkv_low[...], TN).astype(bf16)
    sum_q = AllReduce(orders_q, groups_q, acc_q, got_q, out_q, send_q, recv_q)
    events_q = sum_q.events()
    events_q.pop(0)()
    while events_o:
        events_o.pop(0)()

    def shares_of(t):
        at = pl.ds(pl.multiple_of(t * rows, 16), rows)
        low = qkv_low[at, :]
        return (
            mm(low[:, :q_width], w_query[...], NT)
            + mm(low[:, q_width : q_width + k_width], w_key[...], NT)
            + mm(low[:, q_width + k_width :], w_value[...], NT)
        )

    share_copies = []
    for m, other in enumerate(others):
        shares[m] = shares_of(other)
        slot = tensor_size - 2 - m
        c = pltpu.make_async_remote_copy(
            src_ref=shares.at[m], dst_ref=got_shares.at[slot], send_sem=share_send.at[m],
            recv_sem=share_recv.at[slot], device_id={"tensor": other}, device_id_type=MESH,
        )
        c.start()
        share_copies.append(c)
    normed_grad = shares_of(core)
    events_q.pop(0)()
    out_input[mine, :] = normed_grad
    for m, c in enumerate(share_copies):
        c.wait_send()
        slot = tensor_size - 2 - m
        pltpu.make_async_remote_copy(
            src_ref=shares.at[m], dst_ref=got_shares.at[slot], send_sem=share_send.at[m],
            recv_sem=share_recv.at[slot], device_id={"tensor": others[m]}, device_id_type=MESH,
        ).wait_recv()
        out_input[mine, :] += got_shares[slot]
    normed_grad = out_input[mine, :]
    inputs = hidden[...].astype(f32)
    r1 = lax.rsqrt(jnp.mean(inputs * inputs, axis=1, keepdims=True) + epsilon)
    gained = gain[...] * normed_grad
    small_out[pl.ds(small_out.shape[0] - 1, 1), :] = jnp.sum(normed_grad * inputs * r1, axis=0, keepdims=True)
    out_input[mine, :] = (
        middle_grad[...]
        + r1 * gained
        - inputs * (r1 * r1 * r1) * jnp.mean(inputs * gained, axis=1, keepdims=True)
    )
    in_copies = []
    for m, other in enumerate(others):
        c = pltpu.make_async_remote_copy(
            src_ref=out_input.at[mine], dst_ref=out_input.at[mine], send_sem=in_send.at[m],
            recv_sem=in_recv.at[m], device_id={"tensor": other}, device_id_type=MESH,
        )
        c.start()
        in_copies.append(c)
    ways = [("dp", m) for m in masks] + [("tensor", m) for m in tensor_masks]
    small_copies = []

    def small_step(step):
        if step > 0:
            small_copies[-1].wait_send()
            small_copies[-1].wait_recv()
            small_out[...] += small_got[step - 1]
        if step < len(ways):
            axis, m = ways[step]
            device = {"dp": peer_of(m)[0]} if axis == "dp" else {"tensor": mate(m)}
            c = pltpu.make_async_remote_copy(
                src_ref=small_out, dst_ref=small_got.at[step], send_sem=small_send.at[step],
                recv_sem=small_recv.at[step], device_id=device, device_id_type=MESH,
            )
            c.start()
            small_copies.append(c)

    steps = len(ways) + 1
    done = 0
    while events_q:
        if done < steps:
            small_step(done)
            done += 1
        events_q.pop(0)()
    while done < steps:
        small_step(done)
        done += 1
    sum_o.finish()
    sum_q.finish()
    for c in in_copies:
        c.wait()


def attention_back(
    back, middle, routed, grad_top, picked, router, moe_gain,
    heads, q, k, v, w_out, w_query, w_key, w_value, normed, cosine, sine, seg,
    hidden, gain, dp_size, tensor_size, collective_id,
):
    length, width = normed.shape
    small = jax.ShapeDtypeStruct(((dp_size + 2 + 7) // 8 * 8, width), f32)
    q_width, k_width = q.shape[1], k.shape[1]
    rows = hidden.shape[0]
    orders_o, groups_o = sum_orders(dp_size, width, 1)
    orders_q, groups_q = sum_orders(dp_size, width, 2)
    steps = len(bit_masks(dp_size))
    small_steps = steps + len(bit_masks(tensor_size))
    qkv_width = q_width + 2 * k_width
    others = tensor_size - 1
    vmem = pl.BlockSpec(memory_space=pltpu.VMEM)
    dma = pltpu.SemaphoreType.DMA
    return pl.pallas_call(
        functools.partial(
            attention_back_kernel, dp_size, tensor_size, orders_o, groups_o, orders_q, groups_q
        ),
        out_shape=[
            jax.ShapeDtypeStruct((width, q_width), bf16),
            jax.ShapeDtypeStruct((width, qkv_width), bf16),
            jax.ShapeDtypeStruct((length, width), f32),
            jax.ShapeDtypeStruct(small.shape, f32),
        ],
        in_specs=[vmem] * 22,
        out_specs=[vmem] * 4,
        scratch_shapes=[
            pltpu.VMEM((length, width), bf16),
            pltpu.VMEM((rows, width), f32),
            pltpu.VMEM((length, length), f32),
            pltpu.VMEM((length, q_width), bf16),
            pltpu.VMEM((length, qkv_width), bf16),
            pltpu.VMEM((length, q_width), f32),
            pltpu.VMEM((length, 128), f32),
            pltpu.VMEM((length, 128), f32),
            pltpu.VMEM((width, q_width), bf16),
            pltpu.VMEM((width, q_width), bf16),
            pltpu.VMEM((width, qkv_width), bf16),
            pltpu.VMEM((width, qkv_width), bf16),
            pltpu.VMEM((others, rows, width), f32),
            pltpu.VMEM((others, rows, width), f32),
            pltpu.VMEM((small_steps,) + small.shape, f32),
            dma((len(orders_o), 2 * steps)),
            dma((len(orders_o), 2 * steps)),
            dma((len(orders_q), 2 * steps)),
            dma((len(orders_q), 2 * steps)),
            dma((small_steps,)),
            dma((small_steps,)),
            dma((others,)),
            dma((others,)),
            dma((others,)),
            dma((others,)),
            dma((others,)),
            dma((others,)),
        ],
        compiler_params=pltpu.CompilerParams(
            collective_id=collective_id, has_side_effects=True, vmem_limit_bytes=60 << 20
        ),
    )(
        back, middle, routed, grad_top, picked, router, moe_gain[None],
        heads, q, k, v, w_out, w_query, w_key, w_value, normed, cosine, sine,
        seg[:, None], seg[None, :], hidden, gain[None],
    )


def attention_kernel(
    a, b, tensor_size,
    w_gate, w_up, w_down,
    payload, hidden, gain, w_query, w_key, w_value, w_out, seg_col, seg_row, frequency, moe_gain,
    grads, cosine, sine, heads, q_ref, k_ref, v_ref, normed, middle, routed, far_gate, far_up, far_down,
    bias, shares, got_shares, own_gate, own_up, own_down, local, send, recv, share_send, share_recv,
    own_load, pair_send, pair_recv, mate_send, mate_recv,
):
    spot = Spot(a, b)
    length, width = hidden.shape
    rows = payload.shape[0]
    q_width, k_width = q_ref.shape[1], k_ref.shape[1]
    per_kv = q_width // k_width
    core = lax.axis_index("tensor")
    others = [(core + m) % tensor_size for m in range(1, tensor_size)]
    own = pl.ds(pl.multiple_of(spot.block * rows, 16), rows)
    mine_copy = pltpu.make_async_copy(payload, grads.at[own], local)
    mine_copy.start()
    units = own_gate.shape[1]
    unit_at = pl.ds(pl.multiple_of(core * units, units), units)
    loads = [
        pltpu.make_async_copy(src, dst, own_load.at[i])
        for i, (src, dst) in enumerate(
            ((w_gate.at[:, unit_at], own_gate), (w_up.at[:, unit_at], own_up), (w_down.at[unit_at, :], own_down))
        )
    ]
    for c in loads:
        c.start()

    def far_blocks(m):
        at = pl.ds(m * units, units)
        return (far_gate.at[:, at], far_up.at[:, at], far_down.at[at, :])

    partner = spot.me + 1 - 2 * spot.pair
    to_pair = [
        remote_to(src, dst, pair_send.at[i], pair_recv.at[i], partner)
        for i, (src, dst) in enumerate(zip((own_gate, own_up, own_down), far_blocks(0)))
    ]
    to_mates = [
        pltpu.make_async_remote_copy(
            src_ref=src, dst_ref=dst, send_sem=mate_send.at[m - 1, i], recv_sem=mate_recv.at[m - 1, i],
            device_id={"tensor": xor4(core, m)}, device_id_type=MESH,
        )
        for m in range(1, tensor_size)
        for i, (src, dst) in enumerate(zip(far_blocks(0), far_blocks(m)))
    ]
    spot.greet([{"tensor": other} for other in others] + [{"dp": partner}])
    mine_copy.wait()
    gather = LineGather(spot, grads, rows, send, recv)
    gather.begin()
    for load, c in zip(loads, to_pair):
        load.wait()
        c.start()
    earlier = jnp.sum(jnp.where(seg_row[...] < seg_col[...], 1.0, 0.0), axis=1, keepdims=True)
    lane = lax.broadcasted_iota(jnp.int32, (length, 128), 1)
    position = lax.broadcasted_iota(jnp.int32, (length, 128), 0).astype(f32) - earlier
    angle = position * frequency[...]
    cosine[...] = jnp.cos(angle)
    sine[...] = jnp.where(lane % HEAD_DIM < HEAD_DIM // 2, -1.0, 1.0) * jnp.sin(angle)
    mask_bias(bias, seg_col, seg_row)
    inputs = hidden[...].astype(f32)
    r1 = lax.rsqrt(jnp.mean(inputs * inputs, axis=1, keepdims=True) + epsilon)
    normed[...] = (inputs * r1 * gain[...]).astype(bf16)
    for out, weight, turned in ((q_ref, w_query, True), (k_ref, w_key, True), (v_ref, w_value, False)):
        tile = min(256, out.shape[1])
        for i in range(out.shape[1] // tile):
            product = mm(normed[...], weight[:, i * tile : (i + 1) * tile], NN)
            for j in range(tile // 128):
                piece = product[:, j * 128 : (j + 1) * 128]
                if turned:
                    piece = turn(piece, cosine[...], sine[...])
                at = i * tile + j * 128
                out[:, at : at + 128] = piece.astype(bf16)
    arrivals = list(range(1, spot.n))

    def arrive(count):
        for _ in range(count):
            gather.arrive(arrivals.pop(0))

    half = length // 2
    spans = ((0, half, half), (half, half, length))
    kv_count = k_width // HEAD_DIM
    for g in range(kv_count):
        kg = k_ref[:, g * HEAD_DIM : (g + 1) * HEAD_DIM]
        vg = v_ref[:, g * HEAD_DIM : (g + 1) * HEAD_DIM]
        for h in range(per_kv):
            lanes = pl.ds((g * per_kv + h) * HEAD_DIM, HEAD_DIM)
            for start, size, cols in spans:
                at = pl.ds(start, size)
                scores = mm(q_ref[at, lanes], kg[:cols], NT) * attn_scale + bias[at, pl.ds(0, cols)]
                raised = jnp.exp(scores - jnp.max(scores, axis=1, keepdims=True))
                probs_low = (raised * (1.0 / jnp.sum(raised, axis=1, keepdims=True))).astype(bf16)
                heads[at, lanes] = mm(probs_low, vg[:cols], NN).astype(bf16)
        if g == kv_count // 2 - 1:
            arrive(2)

    def part_of(t):
        at = pl.ds(pl.multiple_of(t * rows, 16), rows)
        return mm(heads[at, :], w_out[...], NN)

    def share_copy(m):
        slot = tensor_size - 2 - m
        return pltpu.make_async_remote_copy(
            src_ref=shares.at[m], dst_ref=got_shares.at[slot], send_sem=share_send.at[m],
            recv_sem=share_recv.at[slot], device_id={"tensor": others[m]}, device_id_type=MESH,
        )

    for m, other in enumerate(others):
        shares[m] = part_of(other)
        share_copy(m).start()
    arrive(1)
    mine = pl.ds(pl.multiple_of(core * rows, 16), rows)
    total = part_of(core)
    for m in range(len(others)):
        share_copy(m).wait_send()
        share_copy(m).wait_recv()
    for m in range(len(others)):
        total += got_shares[m]
    mid = hidden[mine, :].astype(f32) + residual_scale * total
    middle[...] = mid
    r2 = lax.rsqrt(jnp.mean(mid * mid, axis=1, keepdims=True) + epsilon)
    routed[...] = (mid * r2 * moe_gain[...]).astype(bf16)
    arrive(max(0, len(arrivals) - 2))
    for c in to_pair:
        c.wait_recv()
    for c in to_mates:
        c.start()
    arrive(len(arrivals))
    for c in to_mates:
        c.wait()
    for c in to_pair:
        c.wait_send()
    gather.finish()


def attention_forward(
    w_gate, w_up, w_down, payload, hidden, gain, w_query, w_key, w_value, w_out, seg, moe_gain, dp_size, tensor_size, collective_id
):
    a, b = group_sizes(dp_size)
    n = a * b
    length, width = hidden.shape
    rows = payload.shape[0]
    q_width, k_width = w_query.shape[1], w_key.shape[1]
    others = tensor_size - 1
    units = w_gate.shape[1] // tensor_size
    half = HEAD_DIM // 2
    frequency = rope_base ** (-jnp.arange(half, dtype=f32) * 2.0 / HEAD_DIM)
    vmem = pl.BlockSpec(memory_space=pltpu.VMEM)
    dma = pltpu.SemaphoreType.DMA
    struct = jax.ShapeDtypeStruct
    return pl.pallas_call(
        functools.partial(attention_kernel, a, b, tensor_size),
        out_shape=[
            struct((n * rows, payload.shape[1]), bf16),
            struct((length, 128), f32),
            struct((length, 128), f32),
            struct((length, q_width), bf16),
            struct((length, q_width), bf16),
            struct((length, k_width), bf16),
            struct((length, k_width), bf16),
            struct((length, width), bf16),
            struct((rows, width), f32),
            struct((rows, width), bf16),
            struct(w_gate.shape, bf16),
            struct(w_up.shape, bf16),
            struct(w_down.shape, bf16),
        ],
        in_specs=[pl.BlockSpec(memory_space=pl.ANY)] * 3 + [vmem] * 11,
        out_specs=[vmem] * 13,
        scratch_shapes=[
            pltpu.VMEM((length, length), f32),
            pltpu.VMEM((others, rows, width), f32),
            pltpu.VMEM((others, rows, width), f32),
            pltpu.VMEM((width, units), bf16),
            pltpu.VMEM((width, units), bf16),
            pltpu.VMEM((units, width), bf16),
            dma(()),
            dma((n, 4, 2)),
            dma((n, 2)),
            dma((others,)),
            dma((others,)),
            dma((3,)),
            dma((3,)),
            dma((3,)),
            dma((others, 3)),
            dma((others, 3)),
        ],
        compiler_params=pltpu.CompilerParams(
            collective_id=collective_id, has_side_effects=True, vmem_limit_bytes=52 << 20
        ),
    )(
        w_gate, w_up, w_down, payload, hidden, gain[None], w_query, w_key, w_value, w_out,
        seg[:, None], seg[None, :], jnp.tile(frequency, 4)[None], moe_gain[None],
    )


def dot(a, b, spec):
    return jnp.einsum(spec, a, b, preferred_element_type=f32)


def per_device(
    hidden_in,
    attn_gain,
    w_query,
    key_weight,
    value_weight,
    w_output,
    moe_gain,
    w_router,
    w_gate,
    w_up,
    w_down,
    expert_ids,
    segment_ids,
    out_grad,
):
    tokens_here, model_width = hidden_in.shape
    dp_size = lax.axis_size("dp")
    tensor_size = lax.axis_size("tensor")
    experts = dp_size
    tensor_index = lax.axis_index("tensor")
    masks = bit_masks(dp_size)
    tensor_masks = bit_masks(tensor_size)
    tensor_down = tensor_masks[::-1]
    rows_here = tokens_here // tensor_size
    groups = [list(range(pair, dp_size, 2)) for pair in range(2)]

    def my_rows(x):
        return lax.dynamic_slice_in_dim(x, tensor_index * rows_here, rows_here, 0)

    grad_mine = my_rows(out_grad)
    lanes = jnp.arange(LANES, dtype=jnp.int32)
    picked_mine = jnp.any(my_rows(expert_ids)[:, :, None] == lanes[None, None, :], axis=1)
    picked_low = picked_mine.astype(bf16)
    router_wide = jnp.pad(w_router, ((0, 0), (0, LANES - experts)))

    segment = segment_ids[0]
    grads, cosine, sine, heads_flat, query_heads, key_heads, value_heads, normed_low, middle, routed_low, *far_set = (
        attention_forward(
            w_gate[0],
            w_up[0],
            w_down[0],
            jnp.concatenate([grad_mine, picked_low], 1),
            hidden_in,
            attn_gain,
            w_query,
            key_weight,
            value_weight,
            w_output,
            segment,
            moe_gain,
            dp_size,
            tensor_size,
            3,
        )
    )

    near_set = [w_gate[0], w_up[0], w_down[0]]
    moe_part, back, *expert_parts = experts_call(
        routed_low, grads, router_wide, near_set, far_set, dp_size, tensor_size, 0
    )
    moe_total = lax.psum_scatter(
        moe_part, "dp", scatter_dimension=0, tiled=True, axis_index_groups=groups
    )

    near_mine = expert_parts[:3]
    returning = [swap(x, "dp", 1) for x in expert_parts[3:]]
    dims = (1, 1, 0)
    heads_width = heads_flat.shape[1]
    width_q, width_k = query_heads.shape[1], key_heads.shape[1]
    qkv_width = width_q + 2 * width_k
    w_output_sum, qkv_grad, input_grad, small = attention_back(
        back,
        middle,
        routed_low,
        grad_mine,
        picked_low,
        router_wide,
        moe_gain,
        heads_flat,
        query_heads,
        key_heads,
        value_heads,
        w_output,
        w_query,
        key_weight,
        value_weight,
        normed_low,
        cosine,
        sine,
        segment,
        my_rows(hidden_in),
        attn_gain,
        dp_size,
        tensor_size,
        2,
    )
    w_output_sum, returning, moe_total = lax.optimization_barrier(
        (w_output_sum, returning, moe_total)
    )
    block_mine = (middle + residual_scale * moe_total.astype(f32)).astype(bf16)
    block_out = gather_blocks(block_mine, "tensor", tensor_down)
    expert_mine = [
        mine.astype(f32) + away.astype(f32) for mine, away in zip(near_mine, returning)
    ]
    if tensor_size == 2:
        expert_grads = place(expert_mine, [swap(x, "tensor", 1) for x in expert_mine], dims)
    else:
        expert_grads = [
            gather_blocks(x, "tensor", tensor_down, dim) for x, dim in zip(expert_mine, dims)
        ]
    w_output_sum, qkv_grad = w_output_sum.astype(f32), qkv_grad.astype(f32)
    w_output_grad = jnp.concatenate(
        [w_output_sum[i : i + heads_width] for i in range(0, model_width, heads_width)], 1
    )
    return (
        block_out,
        input_grad,
        small[-1],
        qkv_grad[:, :width_q],
        qkv_grad[:, width_q : width_q + width_k],
        qkv_grad[:, width_q + width_k : qkv_width],
        w_output_grad,
        small[experts],
        small[:experts].T,
        expert_grads[0][None],
        expert_grads[1][None],
        expert_grads[2][None],
    )


def solution(mesh):
    placed = (
        P("dp", None),
        P(),
        P(None, "tensor"),
        P(None, "tensor"),
        P(None, "tensor"),
        P("tensor", None),
        P(),
        P(),
        P("dp", None, None),
        P("dp", None, None),
        P("dp", None, None),
        P("dp", None),
        P("dp", None),
        P("dp", None),
    )
    return jax.shard_map(
        per_device,
        mesh=mesh,
        in_specs=placed,
        out_specs=(
            P("dp", None),
            P("dp", None),
            P(),
            P(None, "tensor"),
            P(None, "tensor"),
            P(None, "tensor"),
            P("tensor", None),
            P(),
            P(),
            P("dp", None, None),
            P("dp", None, None),
            P("dp", None, None),
        ),
        check_vma=False,
    )
```

```python
import functools

import jax
import jax.numpy as jnp
from jax import lax
from jax.experimental import pallas as pl
from jax.experimental.pallas import tpu as pltpu
from jax.sharding import PartitionSpec as P

HEAD_DIM = 64

bf16 = jnp.bfloat16
f32 = jnp.float32
MESH = pl.DeviceIdType.MESH
epsilon = 1e-06
residual_scale = 0.22
attn_scale = 0.015625
rope_base = 10000.0
masked_score = -1e30


def bit_masks(size):
    masks = []
    while size > 1:
        size //= 2
        masks.append(size)
    return masks[::-1]


def swap(x, axis, mask):
    return lax.ppermute(x, axis, [(i, i ^ mask) for i in range(lax.axis_size(axis))])


def bit_of(axis, mask):
    return (lax.axis_index(axis) // mask) % 2


def halves_by_bit(x, axis, mask, dim=0):
    half = x.shape[dim] // 2
    bit = bit_of(axis, mask)
    mine = lax.dynamic_slice_in_dim(x, bit * half, half, dim)
    other = lax.dynamic_slice_in_dim(x, (1 - bit) * half, half, dim)
    return mine, other


def join_by_bit(mine, other, axis, mask, dim=0):
    return jnp.where(
        bit_of(axis, mask) == 0,
        jnp.concatenate([mine, other], dim),
        jnp.concatenate([other, mine], dim),
    )


def scatter_sum(x, axis, masks, kind, dim=0):
    x = x.astype(f32)
    for mask in masks:
        mine, other = halves_by_bit(x, axis, mask, dim)
        x = mine + swap(other.astype(kind), axis, mask).astype(f32)
    return x


def gather_blocks(x, axis, masks, dim=0):
    for mask in reversed(masks):
        x = join_by_bit(x, swap(x, axis, mask), axis, mask, dim)
    return x


def rotated(masks, j):
    j = j % len(masks)
    return masks[j:] + masks[:j]


def peer_of(mask):
    me = lax.axis_index("dp")
    bit = (me // mask) % 2
    return me + mask * (1 - 2 * bit), bit


def greet(masks):
    barrier = pltpu.get_barrier_semaphore()
    for mask in masks:
        pl.semaphore_signal(
            barrier, inc=1, device_id={"dp": peer_of(mask)[0]}, device_id_type=MESH
        )
    pl.semaphore_wait(barrier, len(masks))


def remote(src, dst, send, recv, mask):
    return remote_to(src, dst, send, recv, peer_of(mask)[0])


def add_rows(dst, dst0, a, a0, b, b0, rows, out_dtype):
    step = 16

    def body(i, _):
        r = pl.multiple_of(i * step, step)
        x = a[pl.ds(a0 + r, step), :].astype(f32) + b[pl.ds(b0 + r, step), :].astype(f32)
        dst[pl.ds(dst0 + r, step), :] = x.astype(out_dtype)
        return 0

    lax.fori_loop(0, rows // step, body, 0, unroll=rows // step <= 4)


def group_sizes(dp_size):
    a = 4
    return a, dp_size // (2 * a)


class Spot:
    def __init__(self, a, b):
        me = lax.axis_index("dp")
        self.a, self.b = a, b
        self.n = a * b
        self.me = me
        self.A = me // (2 * b)
        self.B = (me // 2) % b
        self.block = me // 2
        self.pair = me % 2
        self.devices = (me + 2 * b, me - 2 * b, me + 2, me - 2)
        self.exists = (self.A < a - 1, self.A > 0, self.B < b - 1, self.B > 0)
        self.some = me + 2 * (1 - 2 * (self.B % 2))

    def greet(self, further=()):
        barrier = pltpu.get_barrier_semaphore()
        for device in further:
            pl.semaphore_signal(barrier, inc=1, device_id=device, device_id_type=MESH)
        for device, there in zip(self.devices, self.exists):

            @pl.when(there)
            def _(device=device):
                pl.semaphore_signal(
                    barrier, inc=1, device_id={"dp": device}, device_id_type=MESH
                )

        a, b = self.a, self.b
        ups = 2 - (self.A + 1) // a - (self.B + 1) // b
        downs = (self.A + a - 1) // a + (self.B + b - 1) // b
        pl.semaphore_wait(barrier, ups + downs + len(further))


def xor4(x, y):
    return ((x // 2 + y // 2) % 2) * 2 + (x % 2 + y % 2) % 2


def is_at(x, value):
    return 1 // (1 + (x - value) * (x - value))


def by_distance(size, place, k):
    found = 0
    for p in range(size):
        order = sorted(range(size), key=lambda q: (abs(q - p), q))
        for j, q in enumerate(order):
            if q > 0:
                found = found + q * is_at(place, p) * is_at(k, j)
    return found


def visit_order(a, b):
    pairs = [(k, l) for k in range(a) for l in range(b)]
    return sorted(pairs, key=lambda kl: kl[0] + (2 * kl[1] + 0.5 if kl[1] else 0))


def remote_to(src, dst, send, recv, device):
    return pltpu.make_async_remote_copy(
        src_ref=src,
        dst_ref=dst,
        send_sem=send,
        recv_sem=recv,
        device_id={"dp": device},
        device_id_type=MESH,
    )


SUM_PIECES = 4


class LineGather:
    def __init__(self, spot, buf, rows, send, recv):
        self.spot, self.buf, self.rows, self.send, self.recv = spot, buf, rows, send, recv
        few = max(16, rows * 3 // 16 // 16 * 16)
        self.parts = ((0, rows - few, False), (rows - few, few, True))

    def coords(self, i):
        s = self.spot
        visits = visit_order(s.a, s.b)
        k = sum(v[0] * is_at(i, j) for j, v in enumerate(visits) if v[0])
        l = sum(v[1] * is_at(i, j) for j, v in enumerate(visits) if v[1])
        return by_distance(s.a, s.A, k), by_distance(s.b, s.B, l)

    def row0(self, i):
        A, B = self.coords(i)
        return pl.multiple_of((A * self.spot.b + B) * self.rows, 16)

    def copy(self, p, block, way, device):
        start, size, _ = self.parts[p]
        there = self.buf.at[pl.ds(pl.multiple_of(block * self.rows + start, 16), size)]
        return remote_to(there, there, self.send.at[block, way, p], self.recv.at[block, p], device)

    def each_way(self, i, p, act):
        s = self.spot
        A, B = self.coords(i)
        block = A * s.b + B
        if self.parts[p][2]:
            along_a, along_b = True, A == s.A
        else:
            along_a, along_b = B == s.B, True
        conditions = (
            along_a & (A <= s.A) & s.exists[0],
            along_a & (A >= s.A) & s.exists[1],
            along_b & (B <= s.B) & s.exists[2],
            along_b & (B >= s.B) & s.exists[3],
        )
        for way, (condition, device) in enumerate(zip(conditions, s.devices)):

            @pl.when(condition)
            def _(way=way, device=device):
                act(self.copy(p, block, way, device))

    def arrive(self, i):
        A, B = self.coords(i)
        for p in range(len(self.parts)):
            self.copy(p, A * self.spot.b + B, 0, self.spot.some).wait_recv()
            self.each_way(i, p, lambda c: c.start())

    def begin(self):
        for p in range(len(self.parts)):
            self.each_way(0, p, lambda c: c.start())

    def finish(self):
        def one(i, _):
            for p in range(len(self.parts)):
                self.each_way(i, p, lambda c: c.wait_send())
            return 0

        lax.fori_loop(0, self.spot.n, one, 0)


def add_into(dst, d0, src, s0, rows, step=16):
    def body(i, _):
        r = pl.multiple_of(i * step, step)
        total = dst[pl.ds(d0 + r, step), :].astype(f32) + src[pl.ds(s0 + r, step), :].astype(f32)
        dst[pl.ds(d0 + r, step), :] = total.astype(dst.dtype)
        return 0

    lax.fori_loop(0, rows // step, body, 0, unroll=rows // step <= 4)


class LineSum:
    def __init__(self, size, place, up, down, part, row_of, rows, got, send, recv, some):
        self.size, self.place, self.up, self.down = size, place, up, down
        self.part, self.row_of, self.rows, self.got = part, row_of, rows, got
        self.send, self.recv, self.some = send, recv, some

    def up_slot(self, place, c):
        return c - place

    def down_slot(self, place, c):
        return c + (self.size - place) * ((place + self.size - 1) // self.size)

    def copies(self, c, slot, send, device):
        size = self.rows // SUM_PIECES
        return [
            remote_to(
                self.part.at[pl.ds(pl.multiple_of(self.row_of(c) + p * size, 16), size)],
                self.got.at[pl.ds(pl.multiple_of(slot * self.rows + p * size, 16), size)],
                send.at[p],
                self.recv.at[slot, p],
                device,
            )
            for p in range(SUM_PIECES)
        ]

    def take(self, c, slot, p, dst=None, d0=None):
        if dst is None:
            dst, d0 = self.part, self.row_of(c)
        size = self.rows // SUM_PIECES
        self.copies(c, slot, self.send.at[0, 0], self.some)[p].wait_recv()
        from_row = pl.multiple_of(slot * self.rows + p * size, 16)
        add_into(dst, d0 + p * size, self.got, from_row, size)

    def up_copies(self, k):
        c = self.size - 1 - k
        return self.copies(c, self.up_slot(self.place + 1, c), self.send.at[k, 0], self.up)

    def down_copies(self, k):
        return self.copies(k, self.down_slot(self.place - 1, k), self.send.at[k, 1], self.down)

    def step_up(self, k):
        c = self.size - 1 - k

        @pl.when(c > self.place)
        def _():
            for p, copy in enumerate(self.up_copies(k)):

                @pl.when(self.place > 0)
                def _(p=p):
                    self.take(c, self.up_slot(self.place, c), p)

                copy.start()

    def step_down(self, k):
        @pl.when(k < self.place)
        def _():
            for p, copy in enumerate(self.down_copies(k)):

                @pl.when(self.place < self.size - 1)
                def _(p=p):
                    self.take(k, self.down_slot(self.place, k), p)

                copy.start()

    def step(self, k):
        self.step_up(k)
        self.step_down(k)

    def end(self, out=None):
        p = self.place
        d0 = None
        if out is not None:
            out[...] = self.part[pl.ds(self.row_of(p), self.rows), :].astype(out.dtype)
            d0 = 0

        @pl.when(p > 0)
        def _():
            for j in range(SUM_PIECES):
                self.take(p, self.up_slot(p, p), j, out, d0)

        @pl.when(p < self.size - 1)
        def _():
            for j in range(SUM_PIECES):
                self.take(p, self.down_slot(p, p), j, out, d0)

        for k in range(self.size - 1):

            @pl.when(self.size - 1 - k > p)
            def _(k=k):
                for c in self.up_copies(k):
                    c.wait_send()

            @pl.when(k < p)
            def _(k=k):
                for c in self.down_copies(k):
                    c.wait_send()


def slots_of(size):
    return 1 if size == 2 else size + 1


class GroupSum:
    def __init__(self, spot, part, rows, got_b, got_a, send_b, recv_b, send_a, recv_a):
        self.spot, self.part, self.rows = spot, part, rows
        a, b = spot.a, spot.b
        slots_b = slots_of(b)

        def b_line(A):
            return LineSum(
                b, spot.B, spot.devices[2], spot.devices[3], part,
                lambda B: pl.multiple_of((A * b + B) * rows, 16), rows,
                got_b.at[pl.ds(pl.multiple_of(A * slots_b * rows, 16), slots_b * rows)],
                send_b.at[A], recv_b.at[A], spot.some,
            )

        self.b_line = b_line
        self.a_line = LineSum(
            a, spot.A, spot.devices[0], spot.devices[1], part,
            lambda A: pl.multiple_of((A * b + spot.B) * rows, 16), rows,
            got_a, send_a, recv_a, spot.some,
        )

    def ready(self, A, B):
        if self.spot.b == 2:
            line = self.b_line(A)

            @pl.when(B != self.spot.B)
            def _():
                line.step(0)

    def along_b(self):
        if self.spot.b > 2:

            def one(A, _):
                for k in range(self.spot.b - 1):
                    self.b_line(A).step(k)
                return 0

            lax.fori_loop(0, self.spot.a, one, 0)

    def flow(self, fills):
        a, line = self.spot.a, self.a_line
        fills = list(fills)

        def fill():
            if fills:
                fills.pop(0)()

        for k in range(a - 1):
            if 2 * k < a:
                self.b_line(a - 1 - k).end()
            line.step_up(k)
            fill()
            if 2 * k < a and a - 1 - k != k:
                self.b_line(k).end()
            line.step_down(k)
            fill()
        while fills:
            fill()

    def order(self, j):
        a = self.spot.a
        places = sorted(range(a), key=lambda c: (min(c, a - 1 - c), -c))
        return sum(c * is_at(j, i) for i, c in enumerate(places) if c)

    def steps_a(self):
        return self.spot.a - 1

    @staticmethod
    def scratch(a, b, rows, width):
        return [
            pltpu.VMEM((a * slots_of(b) * rows, width), bf16),
            pltpu.VMEM((slots_of(a) * rows, width), bf16),
            pltpu.SemaphoreType.DMA((a, b - 1, 2, SUM_PIECES)),
            pltpu.SemaphoreType.DMA((a, slots_of(b), SUM_PIECES)),
            pltpu.SemaphoreType.DMA((a - 1, 2, SUM_PIECES)),
            pltpu.SemaphoreType.DMA((slots_of(a), SUM_PIECES)),
        ]


LANES = 128
LOW_AT = 64


def mm(x, y, dims):
    return lax.dot_general(x, y, (dims, ((), ())), preferred_element_type=f32)


NN, NT, TN = ((1,), (0,)), ((1,), (1,)), ((0,), (0,))


def experts_kernel(
    a, b, rows, width, cores,
    x_ref, grads_ref, router_ref, near_gate, near_up, near_down, far_gate, far_up, far_down,
    moe_ref, out_ref, o_near_gate, o_near_up, o_near_down, o_far_gate, o_far_up, o_far_down,
    xs, gs, weights, downs, lows, part, extras, stage, got_wide, got_down,
    local, load, send, recv, stage_sem, store, core_send, core_recv, *scratch,
):
    spot = Spot(a, b)
    n = spot.n
    gather = LineGather(spot, xs, rows, send, recv)
    total = GroupSum(spot, part, rows, *scratch)
    mine = pltpu.make_async_copy(
        x_ref, xs.at[pl.ds(pl.multiple_of(spot.block * rows, 16), rows)], local.at[0]
    )
    mine.start()
    sources = (near_gate, near_up, far_gate, far_up)
    arriving = [
        pltpu.make_async_copy(src, weights.at[k], local.at[1 + k]) for k, src in enumerate(sources)
    ] + [
        pltpu.make_async_copy(src, downs.at[k], local.at[5 + k])
        for k, src in enumerate((near_down, far_down))
    ]

    def grads_copy(i):
        at = pl.ds(gather.row0(i), rows)
        return pltpu.make_async_copy(grads_ref.at[at], gs.at[at], load.at[i])

    grads_copy(0).start()
    for c in arriving:
        c.start()
    for i in range(1, n):
        grads_copy(i).start()
    core = lax.axis_index("tensor")
    mates = [xor4(core, m) for m in range(1, cores)]
    spot.greet([{"tensor": mate} for mate in mates])
    mine.wait()
    gather.begin()
    for c in arriving:
        c.wait()
    lane = lax.broadcasted_iota(jnp.int32, (rows, LANES), 1)
    near, far = spot.me, spot.me + 1 - 2 * spot.pair

    def block(i, _):
        at = pl.ds(gather.row0(i), rows)
        grads_copy(i).wait()
        x = xs[at, :]
        chosen = gs[at, pl.ds(width, LANES)] > 0
        logits = jnp.where(chosen, mm(x, router_ref[...], NN), masked_score)
        raised = jnp.where(chosen, jnp.exp(logits - jnp.max(logits, axis=1, keepdims=True)), 0.0)
        gates = raised / jnp.sum(raised, axis=1, keepdims=True)
        extra = jnp.zeros((rows, LANES), f32)
        for e, expert in enumerate((near, far)):
            if e == 1:

                @pl.when(i + 1 < n)
                def _():
                    gather.arrive(i + 1)

            column = jnp.sum(jnp.where(lane == expert, gates, 0.0), axis=1, keepdims=True)
            x = xs[at, :]
            gate_act = mm(x, weights[2 * e], NN)
            up_act = mm(x, weights[2 * e + 1], NN)
            down_in = residual_scale * mm(gs[at, pl.ds(0, width)], downs[e], NT)
            sigmoid_gate = jax.nn.sigmoid(gate_act)
            silu_gate = gate_act * sigmoid_gate
            hidden = silu_gate * up_act
            deriv = jnp.sum(hidden * down_in, axis=1, keepdims=True)
            high = deriv.astype(bf16).astype(f32)
            extra += jnp.where(lane == expert, high, 0.0)
            extra += jnp.where(lane == expert + LOW_AT, deriv - high, 0.0)
            down_in = down_in * column
            lows[3 * e, at, :] = (hidden * column).astype(bf16)
            lows[3 * e + 1, at, :] = (
                down_in * up_act * sigmoid_gate * (1.0 + gate_act * (1.0 - sigmoid_gate))
            ).astype(bf16)
            lows[3 * e + 2, at, :] = (down_in * silu_gate).astype(bf16)

        extras[at, :] = extra.astype(bf16)
        return 0

    lax.fori_loop(0, n, block, 0)

    def rows_of(A, B):
        return pl.ds(pl.multiple_of((A * b + B) * rows, 16), rows)

    def back_block(A, B):
        at = rows_of(A, B)
        back = mm(lows[1, at, :], weights[0], NT) + mm(lows[2, at, :], weights[1], NT)
        back += mm(lows[4, at, :], weights[2], NT) + mm(lows[5, at, :], weights[3], NT)
        part[at, pl.ds(0, width)] = back.astype(bf16)
        part[at, pl.ds(width, LANES)] = extras[at, :]
        total.ready(A, B)

    def back_others(i, _):
        A = total.order(i // (b - 1))
        B = by_distance(b, spot.B, 1 + i % (b - 1))
        back_block(A, B)
        return 0

    def back_own(i, _):
        back_block(total.order(i), spot.B)
        return 0

    def stage_copy(i):
        at = pl.ds(pl.multiple_of(i * rows, 16), rows)
        return pltpu.make_async_copy(stage.at[i % 2], moe_ref.at[at], stage_sem.at[i % 2])

    def moe_block(i, _):
        at = pl.ds(pl.multiple_of(i * rows, 16), rows)

        @pl.when(i >= 2)
        def _():
            stage_copy(i - 2).wait()

        stage[i % 2] = (mm(lows[0, at, :], downs[0], NN) + mm(lows[3, at, :], downs[1], NN)).astype(
            bf16
        )
        stage_copy(i).start()
        return 0

    lax.fori_loop(0, a * (b - 1), back_others, 0)
    lax.fori_loop(0, 2, back_own, 0)
    if b > 2:
        lax.fori_loop(2, a, back_own, 0)
    total.along_b()
    tile = 256

    def weight_grads(e):
        def wide(k, _):
            at = pl.ds(pl.multiple_of(k * tile, tile), tile)
            x = xs[:, at]
            weights[2 * e, at, :] = mm(x, lows[3 * e + 1], TN).astype(bf16)
            weights[2 * e + 1, at, :] = mm(x, lows[3 * e + 2], TN).astype(bf16)
            downs[e, :, at] = (residual_scale * mm(lows[3 * e], gs[:, at], TN)).astype(bf16)
            return 0

        lax.fori_loop(0, width // tile, wide, 0)
        give(e)

    units = lows.shape[2] // cores

    def blocks(e, k):
        at = pl.ds(pl.multiple_of(k * units, units), units)
        return (weights.at[2 * e, :, at], weights.at[2 * e + 1, :, at], downs.at[e, at, :])

    def own(e):
        return blocks(e, core if e == 0 else 0)

    def gifts(e):
        copies = []
        for m, mate in enumerate(mates):
            landing = (got_wide.at[e, m, 0], got_wide.at[e, m, 1], got_down.at[e, m])
            for i, (src, dst) in enumerate(zip(blocks(e, mate if e == 0 else m + 1), landing)):
                copies.append(
                    pltpu.make_async_remote_copy(
                        src_ref=src,
                        dst_ref=dst,
                        send_sem=core_send.at[e, m, i],
                        recv_sem=core_recv.at[e, m, i],
                        device_id={"tensor": mate},
                        device_id_type=MESH,
                    )
                )
        return copies

    def give(e):
        for c in gifts(e):
            c.start()

    def collect(e):
        for c in gifts(e):
            c.wait()
        outs = (o_near_gate, o_near_up, o_near_down) if e == 0 else (o_far_gate, o_far_up, o_far_down)
        for i, (view, out) in enumerate(zip(own(e), outs)):

            def chunk(k, _, i=i, view=view):
                size = view.shape[0] // 8
                at = pl.ds(pl.multiple_of(k * size, 16), size)
                total = view[at, :].astype(f32)
                for m in range(len(mates)):
                    got = got_wide[e, m, i, at, :] if i < 2 else got_down[e, m, at, :]
                    total += got.astype(f32)
                view[at, :] = total.astype(bf16)
                return 0

            lax.fori_loop(0, 8, chunk, 0)
            c = pltpu.make_async_copy(view, out, store.at[3 * e + i])
            c.start()
            stored.append(c)

    stored = []

    def moe_all():
        lax.fori_loop(0, n, moe_block, 0)

    total.flow(
        [
            (lambda: lax.fori_loop(2, a, back_own, 0)) if b == 2 else (lambda: None),
            moe_all,
            lambda: weight_grads(1),
            lambda: weight_grads(0),
            lambda: collect(1),
            lambda: collect(0),
        ]
    )
    line = total.a_line
    line.end(out_ref)
    gather.finish()
    stage_copy(n - 2).wait()
    stage_copy(n - 1).wait()
    for c in stored:
        c.wait()


def experts_call(rows_low, grads, router, near, far, dp_size, cores, collective_id):
    a, b = group_sizes(dp_size)
    n = a * b
    rows, width = rows_low.shape
    units = near[0].shape[1]
    hbm, vmem = pl.BlockSpec(memory_space=pl.ANY), pl.BlockSpec(memory_space=pltpu.VMEM)
    outs = [
        jax.ShapeDtypeStruct((n * rows, width), bf16),
        jax.ShapeDtypeStruct((rows, width + LANES), f32),
    ] + [
        jax.ShapeDtypeStruct(shape, bf16)
        for shape in 2 * [(width, units // cores), (width, units // cores), (units // cores, width)]
    ]
    return pl.pallas_call(
        functools.partial(experts_kernel, a, b, rows, width, cores),
        out_shape=outs,
        in_specs=[hbm, hbm, vmem] + [hbm] * 6,
        out_specs=[hbm, vmem] + [hbm] * 6,
        scratch_shapes=[
            pltpu.VMEM((n * rows, width), bf16),
            pltpu.VMEM((n * rows, width + LANES), bf16),
            pltpu.VMEM((4, width, units), bf16),
            pltpu.VMEM((2, units, width), bf16),
            pltpu.VMEM((6, n * rows, units), bf16),
            pltpu.VMEM((n * rows, width + LANES), bf16),
            pltpu.VMEM((n * rows, LANES), bf16),
            pltpu.VMEM((2, rows, width), bf16),
            pltpu.VMEM((2, cores - 1, 2, width, units // cores), bf16),
            pltpu.VMEM((2, cores - 1, units // cores, width), bf16),
            pltpu.SemaphoreType.DMA((7,)),
            pltpu.SemaphoreType.DMA((n,)),
            pltpu.SemaphoreType.DMA((n, 4, 2)),
            pltpu.SemaphoreType.DMA((n, 2)),
            pltpu.SemaphoreType.DMA((2,)),
            pltpu.SemaphoreType.DMA((6,)),
            pltpu.SemaphoreType.DMA((2, cores - 1, 3)),
            pltpu.SemaphoreType.DMA((2, cores - 1, 3)),
        ]
        + GroupSum.scratch(a, b, rows, width + LANES),
        compiler_params=pltpu.CompilerParams(
            collective_id=collective_id, has_side_effects=True, vmem_limit_bytes=62 << 20
        ),
    )(rows_low, grads, router, *near, *far)


def reduce_schedule(steps, groups):
    sums = [("sum", s) for s in range(steps)]
    backs = [("back", s) for s in reversed(range(steps))]
    lines = [[(g,) + e for e in sums + backs] for g in range(groups)]
    if groups == 1:
        return lines[0]
    first, second = lines
    order = first[: steps - 1]
    first = first[steps - 1 :]
    while first or second:
        if second:
            order.append(second.pop(0))
        if first:
            order.append(first.pop(0))
    return order


def place_kernel(dims, *refs):
    n = len(dims)
    mine, other, outs = refs[:n], refs[n : 2 * n], refs[2 * n : 3 * n]
    bufs, sems, out_sems = refs[3 * n : 4 * n], refs[4 * n], refs[4 * n + 1]
    me = lax.axis_index("tensor")

    def copy(i, which, src):
        size = src.shape[dims[i]]
        at = pl.multiple_of((me + which - 2 * which * me) * size, size)
        window = (slice(None),) * dims[i] + (pl.ds(at, size),)
        return pltpu.make_async_copy(src, bufs[i].at[window], sems.at[i, which])

    copies = [[copy(i, w, src) for w, src in enumerate((mine[i], other[i]))] for i in range(n)]
    for pair in copies:
        for c in pair:
            c.start()
    back = []
    for i, pair in enumerate(copies):
        for c in pair:
            c.wait()
        c = pltpu.make_async_copy(bufs[i], outs[i], out_sems.at[i])
        c.start()
        back.append(c)
    for c in back:
        c.wait()


def place(mine, other, dims):
    n = len(dims)
    shapes = [x.shape[:d] + (2 * x.shape[d],) + x.shape[d + 1 :] for x, d in zip(mine, dims)]
    return pl.pallas_call(
        functools.partial(place_kernel, dims),
        out_shape=[jax.ShapeDtypeStruct(s, x.dtype) for x, s in zip(mine, shapes)],
        in_specs=[pl.BlockSpec(memory_space=pl.ANY)] * (2 * n),
        out_specs=[pl.BlockSpec(memory_space=pl.ANY)] * n,
        scratch_shapes=[pltpu.VMEM(s, x.dtype) for x, s in zip(mine, shapes)]
        + [pltpu.SemaphoreType.DMA((n, 2)), pltpu.SemaphoreType.DMA((n,))],
        compiler_params=pltpu.CompilerParams(vmem_limit_bytes=24 << 20),
    )(*mine, *other)


class AllReduce:
    def __init__(self, orders, groups, acc, got, out, send, recv):
        self.orders, self.groups = orders, groups
        self.acc, self.got, self.out, self.send, self.recv = acc, got, out, send, recv
        self.k = len(orders[0])
        self.size = acc.shape[0] // len(orders)
        self.where = [j * self.size for j in range(len(orders))]
        self.sums, self.backs = {}, {}

    def sum_send(self, j, step):
        count = self.size >> (step + 1)
        mask = self.orders[j][step]
        _, bit = peer_of(mask)
        keep = pl.multiple_of(self.where[j] + bit * count, 16)
        give = pl.multiple_of(self.where[j] + (1 - bit) * count, 16)
        acc, got = self.acc, self.got
        p0 = j * self.size + (self.size - (self.size >> max(step - 1, 0)))
        if step > 0:
            self.sums[j, step - 1].wait_recv()
            add_rows(acc, give, acc, give, got, p0 + pl.multiple_of((1 - bit) * count, 16), count, bf16)
        g0 = j * self.size + (self.size - (self.size >> step))
        c = remote(
            acc.at[pl.ds(give, count)],
            got.at[pl.ds(g0, count)],
            self.send.at[j, step],
            self.recv.at[j, step],
            mask,
        )
        c.start()
        self.sums[j, step] = c
        self.where[j] = keep

        def stay():
            if step > 0:
                add_rows(acc, keep, acc, keep, got, p0 + pl.multiple_of(bit * count, 16), count, bf16)

        return stay

    def back_step(self, j, step):
        count = self.size >> (step + 1)
        mask = self.orders[j][step]
        _, bit = peer_of(mask)
        here = self.where[j]
        if step == self.k - 1:
            self.sums[j, step].wait_recv()
            p0 = j * self.size + (self.size - (self.size >> step))
            add_rows(self.out, here, self.acc, here, self.got, p0, count, bf16)
        else:
            self.backs[j, step + 1].wait_recv()
        there = self.out.at[pl.ds(here, count)]
        c = remote(
            there, there, self.send.at[j, self.k + step], self.recv.at[j, self.k + step], mask
        )
        c.start()
        self.backs[j, step] = c
        self.where[j] = pl.multiple_of(here - bit * count, 16)

    def events(self):
        per_group = len(self.orders) // self.groups

        def event(g, kind, step):
            members = range(g * per_group, (g + 1) * per_group)
            if kind == "sum":
                for stay in [self.sum_send(j, step) for j in members]:
                    stay()
            else:
                for j in members:
                    self.back_step(j, step)

        return [
            functools.partial(event, *e) for e in reduce_schedule(self.k, self.groups)
        ]

    def finish(self):
        for j in range(len(self.orders)):
            self.backs[j, 0].wait_recv()
        for c in list(self.sums.values()) + list(self.backs.values()):
            c.wait_send()


def sum_orders(dp_size, rows, most):
    masks = bit_masks(dp_size)
    groups = most if rows % (3 * most * 16 * dp_size) == 0 else 1
    return [rotated(masks[:-1], j) + masks[-1:] for j in range(3 * groups)], groups


class OutputSum:
    def __init__(self, spot, src, own, rows, got_b, got_a, load, send_b, recv_b, send_a, recv_a):
        self.spot, self.src, self.own, self.rows, self.got_b = spot, src, own, rows, got_b
        self.load, self.send_b, self.recv_b = load, send_b, recv_b
        self.line = LineSum(
            spot.a, spot.A, spot.devices[0], spot.devices[1], own, lambda A: A * rows, rows,
            got_a, send_a, recv_a, spot.some,
        )

    def block(self, A, B):
        return pl.multiple_of((A * 2 + B) * self.rows, 16)

    def own_copy(self, A):
        src = self.src.at[pl.ds(self.block(A, self.spot.B), self.rows)]
        return pltpu.make_async_copy(src, self.own.at[pl.ds(A * self.rows, self.rows)], self.load.at[A])

    def start(self):
        for A in range(self.spot.a):
            self.own_copy(A).start()

    def b_copies(self, A):
        size = self.rows // SUM_PIECES
        return [
            remote_to(
                self.src.at[pl.ds(pl.multiple_of(self.block(A, 1 - self.spot.B) + p * size, 16), size)],
                self.got_b.at[pl.ds(A * self.rows + p * size, size)],
                self.send_b.at[A, p],
                self.recv_b.at[A, p],
                self.spot.some,
            )
            for p in range(SUM_PIECES)
        ]

    def b_send(self, A):
        for c in self.b_copies(A):
            c.start()

    def b_end(self, A):
        self.own_copy(A).wait()
        size = self.rows // SUM_PIECES
        for p, c in enumerate(self.b_copies(A)):
            c.wait_recv()
            at = A * self.rows + p * size
            add_into(self.own, at, self.got_b, at, size)

    def events(self):
        a, line = self.spot.a, self.line
        sends = [functools.partial(self.b_send, A) for k in range(a // 2) for A in (a - 1 - k, k)]

        def up(k):
            if 2 * k < a:
                self.b_end(a - 1 - k)
            line.step_up(k)

        def down(k):
            if 2 * k < a:
                self.b_end(k)
            line.step_down(k)

        flow = [functools.partial(f, k) for k in range(a - 1) for f in (up, down)]
        return sends, flow

    def finish(self):
        for A in range(self.spot.a):
            for c in self.b_copies(A):
                c.wait_send()


def turn(x, cosine, sine):
    lane = lax.broadcasted_iota(jnp.int32, x.shape, 1)
    swapped = jnp.where(lane % HEAD_DIM < HEAD_DIM // 2, pltpu.roll(x, 128 - 32, 1), pltpu.roll(x, 32, 1))
    return x * cosine + swapped * sine


def mask_bias(bias, seg_col, seg_row):
    length = bias.shape[0]
    row = lax.broadcasted_iota(jnp.int32, bias.shape, 0)
    col = lax.broadcasted_iota(jnp.int32, bias.shape, 1)
    allowed = (row >= col) & (seg_col[...] == seg_row[...])
    bias[...] = jnp.where(allowed, 0.0, masked_score).astype(bias.dtype)


def attention_back_kernel(
    dp_size, tensor_size, orders_o, groups_o, orders_q, groups_q, moe_inside,
    moe_ref, back, middle, routed, grad_top, picked, router, moe_gain,
    heads, q_ref, k_ref, v_ref, w_out, w_query, w_key, w_value, normed, cosine, sine,
    seg_col, seg_row, hidden, gain,
    out_o, out_q, out_input, small_out, out_block,
    middle_grad, bias, heads_grad, qkv_low, scratch_q, scratch_k, scratch_v,
    acc_o, got_o, acc_q, got_q, shares, got_shares, small_got,
    send_o, recv_o, send_q, recv_q, small_send, small_recv, share_send, share_recv, in_send, in_recv, branch_send, branch_recv, block_send, block_recv,
    *moe_scratch,
):
    length, width = normed.shape
    q_width, k_width = q_ref.shape[1], k_ref.shape[1]
    rows = hidden.shape[0]
    per_kv = q_width // k_width
    core = lax.axis_index("tensor")
    branch = out_block
    tensor_masks = bit_masks(tensor_size)

    def mate(m):
        bit = (core // m) % 2
        return core + m * (1 - 2 * bit)

    barrier = pltpu.get_barrier_semaphore()
    masks = bit_masks(dp_size)
    others = [(core + m) % tensor_size for m in range(1, tensor_size)]
    for mask in masks:
        pl.semaphore_signal(
            barrier, inc=1, device_id={"dp": peer_of(mask)[0]}, device_id_type=MESH
        )
    for other in others:
        pl.semaphore_signal(barrier, inc=1, device_id={"tensor": other}, device_id_type=MESH)
    sends_m, flow_m = [], []
    if moe_inside:
        spot = Spot(*group_sizes(dp_size))
        for device, there in zip(spot.devices[:2], spot.exists[:2]):

            @pl.when(there)
            def _(device=device):
                pl.semaphore_signal(
                    barrier, inc=1, device_id={"dp": device}, device_id_type=MESH
                )

        lines = 1 - (spot.A + 1) // spot.a + (spot.A + spot.a - 1) // spot.a
        moe = OutputSum(spot, moe_ref, moe_scratch[0], rows, *moe_scratch[1:])
        moe.start()
        sends_m, flow_m = moe.events()
    else:
        lines = 0
    pl.semaphore_wait(barrier, len(masks) + len(others) + lines)
    for event in sends_m:
        event()
    mine = pl.ds(pl.multiple_of(core * rows, 16), rows)
    experts = dp_size
    x = routed[...]
    chosen = picked[...] > 0
    logits = jnp.where(chosen, mm(x, router[...], NN), masked_score)
    raised = jnp.where(chosen, jnp.exp(logits - jnp.max(logits, axis=1, keepdims=True)), 0.0)
    gates = raised / jnp.sum(raised, axis=1, keepdims=True)
    derivs = back[:, pl.ds(width, LANES)]
    derivs = jnp.where(chosen, derivs + pltpu.roll(derivs, LANES - LOW_AT, 1), 0.0)
    logit_grad = (
        gates * (derivs - jnp.sum(gates * derivs, axis=1, keepdims=True))
    ).astype(bf16)
    small_out[...] = jnp.zeros(small_out.shape, f32)
    small_out[pl.ds(0, experts), :] = mm(logit_grad, x, TN)[:experts]
    routed_grad = back[:, pl.ds(0, width)] + mm(logit_grad, router[...], NT)
    mid = middle[...]
    r2 = lax.rsqrt(jnp.mean(mid * mid, axis=1, keepdims=True) + epsilon)
    small_out[pl.ds(experts, 1), :] = jnp.sum(routed_grad * mid * r2, axis=0, keepdims=True)
    gained = moe_gain[...] * routed_grad
    middle_grad[...] = (
        grad_top[...].astype(f32)
        + r2 * gained
        - mid * (r2 * r2 * r2) * jnp.mean(mid * gained, axis=1, keepdims=True)
    )
    branch[mine, :] = (residual_scale * middle_grad[...]).astype(bf16)
    branch_copies = []
    for m, other in enumerate(others):
        c = pltpu.make_async_remote_copy(
            src_ref=branch.at[mine], dst_ref=branch.at[mine], send_sem=branch_send.at[m],
            recv_sem=branch_recv.at[m], device_id={"tensor": other}, device_id_type=MESH,
        )
        c.start()
        branch_copies.append(c)
    mask_bias(bias, seg_col, seg_row)
    for c in branch_copies:
        c.wait()
    for i in range(width // q_width):
        at = pl.ds(i * q_width, q_width)
        acc_o[at, :] = mm(heads[...], branch[:, at], TN).astype(bf16)
    sum_o = AllReduce(orders_o, groups_o, acc_o, got_o, out_o, send_o, recv_o)
    events_o = sum_o.events()
    events_o.pop(0)()
    heads_grad[...] = mm(branch[...], w_out[...], NT).astype(bf16)
    half = length // 2
    spans = ((0, half, half), (half, half, length))
    count = 0
    for pair in range(k_width // 128):
        k_tile = k_ref[:, pair * 128 : pair * 128 + 128]
        v_tile = v_ref[:, pair * 128 : pair * 128 + 128]
        for g in range(2):
            kg = k_tile[:, g * HEAD_DIM : (g + 1) * HEAD_DIM]
            vg = v_tile[:, g * HEAD_DIM : (g + 1) * HEAD_DIM]
            side = pl.ds(g * HEAD_DIM, HEAD_DIM)
            for h in range(per_kv):
                head = (pair * 2 + g) * per_kv + h
                lanes = pl.ds(head * HEAD_DIM, HEAD_DIM)
                for start, size, cols in spans:
                    at = pl.ds(start, size)
                    qh = q_ref[at, lanes]
                    oh = heads_grad[at, lanes]
                    scores = mm(qh, kg[:cols], NT) * attn_scale + bias[at, pl.ds(0, cols)].astype(f32)
                    raised = jnp.exp(scores - jnp.max(scores, axis=1, keepdims=True))
                    probability = raised * (1.0 / jnp.sum(raised, axis=1, keepdims=True))
                    prob_grad = mm(oh, vg[:cols], NT)
                    weighted = jnp.sum(probability * prob_grad, axis=1, keepdims=True)
                    score_low = (probability * (prob_grad - weighted)).astype(bf16)
                    probs_low = probability.astype(bf16)
                    scratch_q[at, lanes] = mm(score_low, kg[:cols], NN) * attn_scale
                    dk = mm(score_low, qh, TN) * attn_scale
                    dv = mm(probs_low, oh, TN)
                    upto = pl.ds(0, cols)
                    if h == 0 and start == 0:
                        scratch_k[upto, side] = dk
                        scratch_v[upto, side] = dv
                        scratch_k[pl.ds(cols, length - cols), side] = jnp.zeros((length - cols, HEAD_DIM), f32)
                        scratch_v[pl.ds(cols, length - cols), side] = jnp.zeros((length - cols, HEAD_DIM), f32)
                    else:
                        scratch_k[upto, side] += dk
                        scratch_v[upto, side] += dv
                count += 1
                if count in BESIDE_M and flow_m:
                    flow_m.pop(0)()
        at = pl.ds(q_width + pair * 128, 128)
        qkv_low[:, at] = turn(scratch_k[...], cosine[...], -sine[...]).astype(bf16)
        at = pl.ds(q_width + k_width + pair * 128, 128)
        qkv_low[:, at] = scratch_v[...].astype(bf16)
    for i in range(q_width // 128):
        at = pl.ds(i * 128, 128)
        qkv_low[:, at] = turn(scratch_q[:, at], cosine[...], -sine[...]).astype(bf16)
    chunk = width // len(orders_q)
    for i in range(len(orders_q)):
        at = pl.ds(i * chunk, chunk)
        acc_q[at, :] = mm(normed[:, at], qkv_low[...], TN).astype(bf16)
    sum_q = AllReduce(orders_q, groups_q, acc_q, got_q, out_q, send_q, recv_q)
    events_q = sum_q.events()
    events_q.pop(0)()

    def shares_of(t):
        at = pl.ds(pl.multiple_of(t * rows, 16), rows)
        low = qkv_low[at, :]
        return (
            mm(low[:, :q_width], w_query[...], NT)
            + mm(low[:, q_width : q_width + k_width], w_key[...], NT)
            + mm(low[:, q_width + k_width :], w_value[...], NT)
        )

    share_copies = []
    for m, other in enumerate(others):
        shares[m] = shares_of(other)
        slot = tensor_size - 2 - m
        c = pltpu.make_async_remote_copy(
            src_ref=shares.at[m], dst_ref=got_shares.at[slot], send_sem=share_send.at[m],
            recv_sem=share_recv.at[slot], device_id={"tensor": other}, device_id_type=MESH,
        )
        c.start()
        share_copies.append(c)
    normed_grad = shares_of(core)
    events_q.pop(0)()
    events_o.pop(0)()
    out_input[mine, :] = normed_grad
    for m, c in enumerate(share_copies):
        c.wait_send()
        slot = tensor_size - 2 - m
        pltpu.make_async_remote_copy(
            src_ref=shares.at[m], dst_ref=got_shares.at[slot], send_sem=share_send.at[m],
            recv_sem=share_recv.at[slot], device_id={"tensor": others[m]}, device_id_type=MESH,
        ).wait_recv()
        out_input[mine, :] += got_shares[slot]
    normed_grad = out_input[mine, :]
    inputs = hidden[...].astype(f32)
    r1 = lax.rsqrt(jnp.mean(inputs * inputs, axis=1, keepdims=True) + epsilon)
    gained = gain[...] * normed_grad
    small_out[pl.ds(small_out.shape[0] - 1, 1), :] = jnp.sum(normed_grad * inputs * r1, axis=0, keepdims=True)
    out_input[mine, :] = (
        middle_grad[...]
        + r1 * gained
        - inputs * (r1 * r1 * r1) * jnp.mean(inputs * gained, axis=1, keepdims=True)
    )
    in_copies = []
    for m, other in enumerate(others):
        c = pltpu.make_async_remote_copy(
            src_ref=out_input.at[mine], dst_ref=out_input.at[mine], send_sem=in_send.at[m],
            recv_sem=in_recv.at[m], device_id={"tensor": other}, device_id_type=MESH,
        )
        c.start()
        in_copies.append(c)
    ways = [("dp", m) for m in masks] + [("tensor", m) for m in tensor_masks]
    small_copies = []

    def small_step(step):
        if step > 0:
            small_copies[-1].wait_send()
            small_copies[-1].wait_recv()
            small_out[...] += small_got[step - 1]
        if step < len(ways):
            axis, m = ways[step]
            device = {"dp": peer_of(m)[0]} if axis == "dp" else {"tensor": mate(m)}
            c = pltpu.make_async_remote_copy(
                src_ref=small_out, dst_ref=small_got.at[step], send_sem=small_send.at[step],
                recv_sem=small_recv.at[step], device_id=device, device_id_type=MESH,
            )
            c.start()
            small_copies.append(c)

    steps = len(ways) + 1
    done = 0
    block_copies = []

    def block_end():
        total = shares.at[0]
        moe.line.end(total)
        out_block[mine, :] = (middle[...] + residual_scale * total[...]).astype(bf16)
        for m, other in enumerate(others):
            c = pltpu.make_async_remote_copy(
                src_ref=out_block.at[mine], dst_ref=out_block.at[mine], send_sem=block_send.at[m],
                recv_sem=block_recv.at[m], device_id={"tensor": other}, device_id_type=MESH,
            )
            c.start()
            block_copies.append(c)

    if moe_inside:
        flow_m.append(block_end)
    else:
        out_block[...] = jnp.zeros(out_block.shape, bf16)
    while events_q or events_o or flow_m:
        if done < steps:
            small_step(done)
            done += 1
        for events in (events_q, events_o, flow_m):
            if events:
                events.pop(0)()
    while done < steps:
        small_step(done)
        done += 1
    sum_o.finish()
    sum_q.finish()
    for c in in_copies + block_copies:
        c.wait()
    if moe_inside:
        moe.finish()


BESIDE_M = (6, 12)


def attention_back(
    moe_part, back, middle, routed, grad_top, picked, router, moe_gain,
    heads, q, k, v, w_out, w_query, w_key, w_value, normed, cosine, sine, seg,
    hidden, gain, dp_size, tensor_size, collective_id,
):
    length, width = normed.shape
    small = jax.ShapeDtypeStruct(((dp_size + 2 + 7) // 8 * 8, width), f32)
    q_width, k_width = q.shape[1], k.shape[1]
    rows = hidden.shape[0]
    orders_o, groups_o = sum_orders(dp_size, width, 1)
    orders_q, groups_q = sum_orders(dp_size, width, 2)
    steps = len(bit_masks(dp_size))
    small_steps = steps + len(bit_masks(tensor_size))
    qkv_width = q_width + 2 * k_width
    others = tensor_size - 1
    vmem, hbm = pl.BlockSpec(memory_space=pltpu.VMEM), pl.BlockSpec(memory_space=pl.ANY)
    dma = pltpu.SemaphoreType.DMA
    a, b = group_sizes(dp_size)
    moe_inside = b == 2
    moe_scratch = [
        pltpu.VMEM((a * rows, width), bf16),
        pltpu.VMEM((a * rows, width), bf16),
        pltpu.VMEM((slots_of(a) * rows, width), bf16),
        dma((a,)),
        dma((a, SUM_PIECES)),
        dma((a, SUM_PIECES)),
        dma((a - 1, 2, SUM_PIECES)),
        dma((slots_of(a), SUM_PIECES)),
    ]
    return pl.pallas_call(
        functools.partial(
            attention_back_kernel,
            dp_size, tensor_size, orders_o, groups_o, orders_q, groups_q, moe_inside,
        ),
        out_shape=[
            jax.ShapeDtypeStruct((width, q_width), bf16),
            jax.ShapeDtypeStruct((width, qkv_width), bf16),
            jax.ShapeDtypeStruct((length, width), f32),
            jax.ShapeDtypeStruct(small.shape, f32),
            jax.ShapeDtypeStruct((length, width), bf16),
        ],
        in_specs=[hbm] + [vmem] * 22,
        out_specs=[vmem] * 5,
        scratch_shapes=[
            pltpu.VMEM((rows, width), f32),
            pltpu.VMEM((length, length), bf16),
            pltpu.VMEM((length, q_width), bf16),
            pltpu.VMEM((length, qkv_width), bf16),
            pltpu.VMEM((length, q_width), f32),
            pltpu.VMEM((length, 128), f32),
            pltpu.VMEM((length, 128), f32),
            pltpu.VMEM((width, q_width), bf16),
            pltpu.VMEM((width, q_width), bf16),
            pltpu.VMEM((width, qkv_width), bf16),
            pltpu.VMEM((width, qkv_width), bf16),
            pltpu.VMEM((others, rows, width), f32),
            pltpu.VMEM((others, rows, width), f32),
            pltpu.VMEM((small_steps,) + small.shape, f32),
            dma((len(orders_o), 2 * steps)),
            dma((len(orders_o), 2 * steps)),
            dma((len(orders_q), 2 * steps)),
            dma((len(orders_q), 2 * steps)),
            dma((small_steps,)),
            dma((small_steps,)),
            dma((others,)),
            dma((others,)),
            dma((others,)),
            dma((others,)),
            dma((others,)),
            dma((others,)),
            dma((others,)),
            dma((others,)),
        ]
        + (moe_scratch if moe_inside else []),
        compiler_params=pltpu.CompilerParams(
            collective_id=collective_id, has_side_effects=True, vmem_limit_bytes=63 << 20
        ),
    )(
        moe_part, back, middle, routed, grad_top, picked, router, moe_gain[None],
        heads, q, k, v, w_out, w_query, w_key, w_value, normed, cosine, sine,
        seg[:, None], seg[None, :], hidden, gain[None],
    )


def attention_kernel(
    a, b, tensor_size,
    w_gate, w_up, w_down,
    payload, hidden, gain, w_query, w_key, w_value, w_out, seg_col, seg_row, frequency, moe_gain,
    grads, cosine, sine, heads, q_ref, k_ref, v_ref, normed, middle, routed, far_gate, far_up, far_down,
    bias, shares, got_shares, own_gate, own_up, own_down, local, send, recv, share_send, share_recv,
    own_load, pair_send, pair_recv, mate_send, mate_recv,
):
    spot = Spot(a, b)
    length, width = hidden.shape
    rows = payload.shape[0]
    q_width, k_width = q_ref.shape[1], k_ref.shape[1]
    per_kv = q_width // k_width
    core = lax.axis_index("tensor")
    others = [(core + m) % tensor_size for m in range(1, tensor_size)]
    own = pl.ds(pl.multiple_of(spot.block * rows, 16), rows)
    mine_copy = pltpu.make_async_copy(payload, grads.at[own], local)
    mine_copy.start()
    units = own_gate.shape[1]
    unit_at = pl.ds(pl.multiple_of(core * units, units), units)
    loads = [
        pltpu.make_async_copy(src, dst, own_load.at[i])
        for i, (src, dst) in enumerate(
            ((w_gate.at[:, unit_at], own_gate), (w_up.at[:, unit_at], own_up), (w_down.at[unit_at, :], own_down))
        )
    ]
    for c in loads:
        c.start()

    def far_blocks(m):
        at = pl.ds(m * units, units)
        return (far_gate.at[:, at], far_up.at[:, at], far_down.at[at, :])

    partner = spot.me + 1 - 2 * spot.pair
    to_pair = [
        remote_to(src, dst, pair_send.at[i], pair_recv.at[i], partner)
        for i, (src, dst) in enumerate(zip((own_gate, own_up, own_down), far_blocks(0)))
    ]
    to_mates = [
        pltpu.make_async_remote_copy(
            src_ref=src, dst_ref=dst, send_sem=mate_send.at[m - 1, i], recv_sem=mate_recv.at[m - 1, i],
            device_id={"tensor": xor4(core, m)}, device_id_type=MESH,
        )
        for m in range(1, tensor_size)
        for i, (src, dst) in enumerate(zip(far_blocks(0), far_blocks(m)))
    ]
    spot.greet([{"tensor": other} for other in others] + [{"dp": partner}])
    mine_copy.wait()
    gather = LineGather(spot, grads, rows, send, recv)
    gather.begin()
    for load, c in zip(loads, to_pair):
        load.wait()
        c.start()
    earlier = jnp.sum(jnp.where(seg_row[...] < seg_col[...], 1.0, 0.0), axis=1, keepdims=True)
    lane = lax.broadcasted_iota(jnp.int32, (length, 128), 1)
    position = lax.broadcasted_iota(jnp.int32, (length, 128), 0).astype(f32) - earlier
    angle = position * frequency[...]
    cosine[...] = jnp.cos(angle)
    sine[...] = jnp.where(lane % HEAD_DIM < HEAD_DIM // 2, -1.0, 1.0) * jnp.sin(angle)
    mask_bias(bias, seg_col, seg_row)
    inputs = hidden[...].astype(f32)
    r1 = lax.rsqrt(jnp.mean(inputs * inputs, axis=1, keepdims=True) + epsilon)
    normed[...] = (inputs * r1 * gain[...]).astype(bf16)
    for out, weight, turned in ((q_ref, w_query, True), (k_ref, w_key, True), (v_ref, w_value, False)):
        tile = min(256, out.shape[1])
        for i in range(out.shape[1] // tile):
            product = mm(normed[...], weight[:, i * tile : (i + 1) * tile], NN)
            for j in range(tile // 128):
                piece = product[:, j * 128 : (j + 1) * 128]
                if turned:
                    piece = turn(piece, cosine[...], sine[...])
                at = i * tile + j * 128
                out[:, at : at + 128] = piece.astype(bf16)
    arrivals = list(range(1, spot.n))

    def arrive(count):
        for _ in range(count):
            gather.arrive(arrivals.pop(0))

    half = length // 2
    spans = ((0, half, half), (half, half, length))
    kv_count = k_width // HEAD_DIM
    for g in range(kv_count):
        kg = k_ref[:, g * HEAD_DIM : (g + 1) * HEAD_DIM]
        vg = v_ref[:, g * HEAD_DIM : (g + 1) * HEAD_DIM]
        for h in range(per_kv):
            lanes = pl.ds((g * per_kv + h) * HEAD_DIM, HEAD_DIM)
            for start, size, cols in spans:
                at = pl.ds(start, size)
                scores = mm(q_ref[at, lanes], kg[:cols], NT) * attn_scale + bias[at, pl.ds(0, cols)]
                raised = jnp.exp(scores - jnp.max(scores, axis=1, keepdims=True))
                probs_low = (raised * (1.0 / jnp.sum(raised, axis=1, keepdims=True))).astype(bf16)
                heads[at, lanes] = mm(probs_low, vg[:cols], NN).astype(bf16)
        if g == kv_count // 2 - 1:
            arrive(2)

    def part_of(t):
        at = pl.ds(pl.multiple_of(t * rows, 16), rows)
        return mm(heads[at, :], w_out[...], NN)

    def share_copy(m):
        slot = tensor_size - 2 - m
        return pltpu.make_async_remote_copy(
            src_ref=shares.at[m], dst_ref=got_shares.at[slot], send_sem=share_send.at[m],
            recv_sem=share_recv.at[slot], device_id={"tensor": others[m]}, device_id_type=MESH,
        )

    for m, other in enumerate(others):
        shares[m] = part_of(other)
        share_copy(m).start()
    arrive(1)
    mine = pl.ds(pl.multiple_of(core * rows, 16), rows)
    total = part_of(core)
    for m in range(len(others)):
        share_copy(m).wait_send()
        share_copy(m).wait_recv()
    for m in range(len(others)):
        total += got_shares[m]
    mid = hidden[mine, :].astype(f32) + residual_scale * total
    middle[...] = mid
    r2 = lax.rsqrt(jnp.mean(mid * mid, axis=1, keepdims=True) + epsilon)
    routed[...] = (mid * r2 * moe_gain[...]).astype(bf16)
    arrive(max(0, len(arrivals) - 2))
    for c in to_pair:
        c.wait_recv()
    for c in to_mates:
        c.start()
    arrive(len(arrivals))
    for c in to_mates:
        c.wait()
    for c in to_pair:
        c.wait_send()
    gather.finish()


def attention_forward(
    w_gate, w_up, w_down, payload, hidden, gain, w_query, w_key, w_value, w_out, seg, moe_gain, dp_size, tensor_size, collective_id
):
    a, b = group_sizes(dp_size)
    n = a * b
    length, width = hidden.shape
    rows = payload.shape[0]
    q_width, k_width = w_query.shape[1], w_key.shape[1]
    others = tensor_size - 1
    units = w_gate.shape[1] // tensor_size
    half = HEAD_DIM // 2
    frequency = rope_base ** (-jnp.arange(half, dtype=f32) * 2.0 / HEAD_DIM)
    vmem = pl.BlockSpec(memory_space=pltpu.VMEM)
    dma = pltpu.SemaphoreType.DMA
    struct = jax.ShapeDtypeStruct
    return pl.pallas_call(
        functools.partial(attention_kernel, a, b, tensor_size),
        out_shape=[
            struct((n * rows, payload.shape[1]), bf16),
            struct((length, 128), f32),
            struct((length, 128), f32),
            struct((length, q_width), bf16),
            struct((length, q_width), bf16),
            struct((length, k_width), bf16),
            struct((length, k_width), bf16),
            struct((length, width), bf16),
            struct((rows, width), f32),
            struct((rows, width), bf16),
            struct(w_gate.shape, bf16),
            struct(w_up.shape, bf16),
            struct(w_down.shape, bf16),
        ],
        in_specs=[pl.BlockSpec(memory_space=pl.ANY)] * 3 + [vmem] * 11,
        out_specs=[vmem] * 13,
        scratch_shapes=[
            pltpu.VMEM((length, length), f32),
            pltpu.VMEM((others, rows, width), f32),
            pltpu.VMEM((others, rows, width), f32),
            pltpu.VMEM((width, units), bf16),
            pltpu.VMEM((width, units), bf16),
            pltpu.VMEM((units, width), bf16),
            dma(()),
            dma((n, 4, 2)),
            dma((n, 2)),
            dma((others,)),
            dma((others,)),
            dma((3,)),
            dma((3,)),
            dma((3,)),
            dma((others, 3)),
            dma((others, 3)),
        ],
        compiler_params=pltpu.CompilerParams(
            collective_id=collective_id, has_side_effects=True, vmem_limit_bytes=52 << 20
        ),
    )(
        w_gate, w_up, w_down, payload, hidden, gain[None], w_query, w_key, w_value, w_out,
        seg[:, None], seg[None, :], jnp.tile(frequency, 4)[None], moe_gain[None],
    )


def dot(a, b, spec):
    return jnp.einsum(spec, a, b, preferred_element_type=f32)


def per_device(
    hidden_in,
    attn_gain,
    w_query,
    key_weight,
    value_weight,
    w_output,
    moe_gain,
    w_router,
    w_gate,
    w_up,
    w_down,
    expert_ids,
    segment_ids,
    out_grad,
):
    tokens_here, model_width = hidden_in.shape
    dp_size = lax.axis_size("dp")
    tensor_size = lax.axis_size("tensor")
    experts = dp_size
    tensor_index = lax.axis_index("tensor")
    masks = bit_masks(dp_size)
    tensor_masks = bit_masks(tensor_size)
    tensor_down = tensor_masks[::-1]
    rows_here = tokens_here // tensor_size
    groups = [list(range(pair, dp_size, 2)) for pair in range(2)]

    def my_rows(x):
        return lax.dynamic_slice_in_dim(x, tensor_index * rows_here, rows_here, 0)

    grad_mine = my_rows(out_grad)
    lanes = jnp.arange(LANES, dtype=jnp.int32)
    picked_mine = jnp.any(my_rows(expert_ids)[:, :, None] == lanes[None, None, :], axis=1)
    picked_low = picked_mine.astype(bf16)
    router_wide = jnp.pad(w_router, ((0, 0), (0, LANES - experts)))

    segment = segment_ids[0]
    grads, cosine, sine, heads_flat, query_heads, key_heads, value_heads, normed_low, middle, routed_low, *far_set = (
        attention_forward(
            w_gate[0],
            w_up[0],
            w_down[0],
            jnp.concatenate([grad_mine, picked_low], 1),
            hidden_in,
            attn_gain,
            w_query,
            key_weight,
            value_weight,
            w_output,
            segment,
            moe_gain,
            dp_size,
            tensor_size,
            3,
        )
    )

    near_set = [w_gate[0], w_up[0], w_down[0]]
    moe_part, back, *expert_parts = experts_call(
        routed_low, grads, router_wide, near_set, far_set, dp_size, tensor_size, 0
    )
    near_mine = expert_parts[:3]
    returning = [swap(x, "dp", 1) for x in expert_parts[3:]]
    dims = (1, 1, 0)
    heads_width = heads_flat.shape[1]
    width_q, width_k = query_heads.shape[1], key_heads.shape[1]
    qkv_width = width_q + 2 * width_k
    w_output_sum, qkv_grad, input_grad, small, block_out = attention_back(
        moe_part,
        back,
        middle,
        routed_low,
        grad_mine,
        picked_low,
        router_wide,
        moe_gain,
        heads_flat,
        query_heads,
        key_heads,
        value_heads,
        w_output,
        w_query,
        key_weight,
        value_weight,
        normed_low,
        cosine,
        sine,
        segment,
        my_rows(hidden_in),
        attn_gain,
        dp_size,
        tensor_size,
        2,
    )
    w_output_sum, returning = lax.optimization_barrier((w_output_sum, returning))
    if group_sizes(dp_size)[1] > 2:
        moe_total = lax.psum_scatter(
            moe_part, "dp", scatter_dimension=0, tiled=True, axis_index_groups=groups
        )
        block_mine = (middle + residual_scale * moe_total.astype(f32)).astype(bf16)
        block_out = gather_blocks(block_mine, "tensor", tensor_down)
    expert_mine = [
        mine.astype(f32) + away.astype(f32) for mine, away in zip(near_mine, returning)
    ]
    if tensor_size == 2:
        expert_grads = place(expert_mine, [swap(x, "tensor", 1) for x in expert_mine], dims)
    else:
        expert_grads = [
            gather_blocks(x, "tensor", tensor_down, dim) for x, dim in zip(expert_mine, dims)
        ]
    w_output_sum, qkv_grad = w_output_sum.astype(f32), qkv_grad.astype(f32)
    w_output_grad = jnp.concatenate(
        [w_output_sum[i : i + heads_width] for i in range(0, model_width, heads_width)], 1
    )
    return (
        block_out,
        input_grad,
        small[-1],
        qkv_grad[:, :width_q],
        qkv_grad[:, width_q : width_q + width_k],
        qkv_grad[:, width_q + width_k : qkv_width],
        w_output_grad,
        small[experts],
        small[:experts].T,
        expert_grads[0][None],
        expert_grads[1][None],
        expert_grads[2][None],
    )


def solution(mesh):
    placed = (
        P("dp", None),
        P(),
        P(None, "tensor"),
        P(None, "tensor"),
        P(None, "tensor"),
        P("tensor", None),
        P(),
        P(),
        P("dp", None, None),
        P("dp", None, None),
        P("dp", None, None),
        P("dp", None),
        P("dp", None),
        P("dp", None),
    )
    return jax.shard_map(
        per_device,
        mesh=mesh,
        in_specs=placed,
        out_specs=(
            P("dp", None),
            P("dp", None),
            P(),
            P(None, "tensor"),
            P(None, "tensor"),
            P(None, "tensor"),
            P("tensor", None),
            P(),
            P(),
            P("dp", None, None),
            P("dp", None, None),
            P("dp", None, None),
        ),
        check_vma=False,
    )
```
